32 devices in a mesh: wide: 4 (over y, core), narrow: 8 (over z, x).
Axes of the slice: x: 2, y: 2, z: 4, core: 2. Of those that a mesh axis runs over, the one named last changes fastest.
Arguments:
- tokens: bfloat16 [32768, 384], P(('wide', 'narrow')), may hold values from -6 to 6
- cotangent: bfloat16 [32768, 384], P(('wide', 'narrow')), may hold values from -6 to 6
- routes: int32 [32768, 1], P(('wide', 'narrow')), may hold values from 0 to 31
- images: int32 [32], P(('wide', 'narrow')), may hold values from 0 to 1, as said below
- dense_weight: float32 [384, 1568], P(('wide', 'narrow'))
- dense_moment: float32 [384, 1568], P(('wide', 'narrow'))
- dense_square: float32 [384, 1568], P(('wide', 'narrow'))
- small_params: float32 [10380], replicated
- small_moment: float32 [10380], replicated
- small_square: float32 [10380], replicated
- inner_weight: float32 [32, 384, 1536], P(('wide', 'narrow')), may hold values from -0.3125 to 0.3125
- inner_moment: float32 [32, 384, 1536], P(('wide', 'narrow'))
- inner_square: float32 [32, 384, 1536], P(('wide', 'narrow'))
- outer_weight: float32 [32, 1536, 384], P(('wide', 'narrow')), may hold values from -0.15625 to 0.15625
- outer_moment: float32 [32, 1536, 384], P(('wide', 'narrow'))
- outer_square: float32 [32, 1536, 384], P(('wide', 'narrow'))
- expert_bias: float32 [32, 1920], P(('wide', 'narrow'))
- bias_moment: float32 [32, 1920], P(('wide', 'narrow'))
- bias_square: float32 [32, 1920], P(('wide', 'narrow'))
Outputs:
- layer_out: bfloat16 [32768, 384], P(('wide', 'narrow'))
- input_grad: bfloat16 [32768, 384], P(('wide', 'narrow'))
- dense_next: float32 [384, 1568], P(('wide', 'narrow'))
- dense_first: float32 [384, 1568], P(('wide', 'narrow'))
- dense_second: float32 [384, 1568], P(('wide', 'narrow'))
- small_next: float32 [10380], replicated
- small_first: float32 [10380], replicated
- small_second: float32 [10380], replicated
- inner_next: float32 [32, 384, 1536], P(('wide', 'narrow'))
- inner_first: float32 [32, 384, 1536], P(('wide', 'narrow'))
- inner_second: float32 [32, 384, 1536], P(('wide', 'narrow'))
- inner_copy: bfloat16 [32, 384, 1536], P(('wide', 'narrow'))
- outer_next: float32 [32, 1536, 384], P(('wide', 'narrow'))
- outer_first: float32 [32, 1536, 384], P(('wide', 'narrow'))
- outer_second: float32 [32, 1536, 384], P(('wide', 'narrow'))
- outer_copy: bfloat16 [32, 1536, 384], P(('wide', 'narrow'))
- bias_next: float32 [32, 1920], P(('wide', 'narrow'))
- bias_first: float32 [32, 1920], P(('wide', 'narrow'))
- bias_second: float32 [32, 1920], P(('wide', 'narrow'))
The draws below stay inside these ranges and needn't reach their ends.
Inputs may be any that keep to these rules, and one draw needn't show every extreme that they name: Device d's first images[d] image slots hold live images; in every draw some device holds 1 and some holds none.
All inputs are finite; a program needn't handle non-finite values.
Results may differ from the reference program's by a relative error of at most 0.013.
The reference program's roundings to bfloat16 on the way count: a program that leaves them out, or rounds other values in their place, can miss the bound.
Values may be sent and summed in bfloat16 or wider, within the bound.
No kernel may reach another device: no remote copies, remote signals or barrier semaphores. Data moves between devices by JAX's collectives and lax.ppermute only.
A program may use at most 192 MiB of HBM per device.

```python
import jax
import jax.numpy as jnp
from jax import lax

MODEL_WIDTH = 384
ATTENTION_HEADS = 12
HEAD_DIM = 32
FF = 1536
BIAS_NET_HIDDEN = 512
EXPERTS = 32
SIDE = 8
IMG_TOK = 1024
IMG_SLOTS = 1
STEP = 10
WIN = 64
SPLIT = 1
SLICES = 32
FF_DEV = 1536
TOK_DEV = 1024
TOKENS = 32768
CAP = 40


def column_scales(layout_pattern):
    return jnp.concatenate([jnp.full((amount,), factor, jnp.float32) for amount, factor in layout_pattern])


def first_state(key, scale_list):
    return 0.111 * scale_list * jax.random.normal(key, scale_list.shape, jnp.float32)


def second_state(key, scale_list):
    return 0.001 * scale_list * scale_list * jax.random.uniform(key, scale_list.shape, jnp.float32, 1.0, 4.0)


def dense_scales():
    layout_pattern = ((MODEL_WIDTH, 0.3), (MODEL_WIDTH, 0.3), (MODEL_WIDTH, 1.0), (MODEL_WIDTH, 1.0), (EXPERTS, 7.0))
    return jnp.zeros((MODEL_WIDTH, 1), jnp.float32) + column_scales(layout_pattern)[None, :] * (0.5 * TOKENS) ** 0.5


def small_scales():
    layout_pattern = ((MODEL_WIDTH, 1.1), (MODEL_WIDTH, 1.1), (MODEL_WIDTH, 0.5), (MODEL_WIDTH, 0.5), (MODEL_WIDTH, 0.3), (MODEL_WIDTH, 1.0), (MODEL_WIDTH, 2.7), (ATTENTION_HEADS, 0.3), (BIAS_NET_HIDDEN, 0.1), (2 * BIAS_NET_HIDDEN, 0.1), (BIAS_NET_HIDDEN * ATTENTION_HEADS, 0.5))
    return column_scales(layout_pattern) * (0.5 * TOKENS) ** 0.5


def expert_base():
    return (0.5 * TOK_DEV * SPLIT) ** 0.5


def bias_scales():
    return jnp.zeros((SLICES, 1), jnp.float32) + column_scales(((FF_DEV, 0.17), (MODEL_WIDTH // SPLIT, 0.55)))[None, :] * expert_base()


def draw_images(key, part):
    key = jax.random.fold_in(key, 5)
    random_subkeys = jax.random.split(key, 4)
    number = SLICES
    first_draw = jax.random.randint(random_subkeys[0], (number,), 0, IMG_SLOTS + 1)
    second_draw = jax.random.randint(random_subkeys[1], (number,), 0, IMG_SLOTS + 1)
    counts = jnp.maximum(first_draw, second_draw)
    empty_at = jax.random.randint(random_subkeys[2], (), 0, number)
    full_at = (empty_at + 1 + jax.random.randint(random_subkeys[3], (), 0, number - 1)) % number
    counts = counts.at[empty_at].set(0).at[full_at].set(IMG_SLOTS)
    return counts.astype(jnp.int32)


def draw_dense_weight(key, part):
    key = jax.random.fold_in(key, 11)
    scale_list = column_scales(((4 * MODEL_WIDTH, 1.0), (EXPERTS, 0.5))) * MODEL_WIDTH ** (-0.5)
    values = jax.random.normal(key, (MODEL_WIDTH, 4 * MODEL_WIDTH + EXPERTS), jnp.float32)
    return values * scale_list[None, :]


def draw_dense_moment(key, part):
    key = jax.random.fold_in(key, 12)
    return first_state(key, dense_scales())


def draw_dense_square(key, part):
    key = jax.random.fold_in(key, 13)
    return second_state(key, dense_scales())


def draw_small_params(key, part):
    key = jax.random.fold_in(key, 21)
    random_subkeys = jax.random.split(key, 7)
    row_gains = jax.random.uniform(random_subkeys[0], (2, MODEL_WIDTH), jnp.float32, 0.7, 1.3)
    shift_list = 0.1 * jax.random.normal(random_subkeys[1], (2, MODEL_WIDTH), jnp.float32)
    bias_list = 0.1 * jax.random.normal(random_subkeys[2], (3 * MODEL_WIDTH,), jnp.float32)
    scale_list = jax.random.uniform(random_subkeys[3], (ATTENTION_HEADS,), jnp.float32, 1.6, 2.2)
    bias_net_shift = 0.5 * jax.random.normal(random_subkeys[4], (BIAS_NET_HIDDEN,), jnp.float32)
    bias_net_first = 0.7 * jax.random.normal(random_subkeys[5], (2 * BIAS_NET_HIDDEN,), jnp.float32)
    bias_net_second = 0.5 * BIAS_NET_HIDDEN ** (-0.5) * jax.random.normal(random_subkeys[6], (BIAS_NET_HIDDEN * ATTENTION_HEADS,), jnp.float32)
    return jnp.concatenate([row_gains[0], shift_list[0], row_gains[1], shift_list[1], bias_list, scale_list, bias_net_shift, bias_net_first, bias_net_second])


def draw_small_moment(key, part):
    key = jax.random.fold_in(key, 22)
    return first_state(key, small_scales())


def draw_small_square(key, part):
    key = jax.random.fold_in(key, 23)
    return second_state(key, small_scales())


def draw_inner_moment(key, part):
    key = jax.random.fold_in(key, 31)
    return first_state(key, jnp.full((SLICES, MODEL_WIDTH, FF_DEV), 0.25 * expert_base(), jnp.float32))


def draw_inner_square(key, part):
    key = jax.random.fold_in(key, 32)
    return second_state(key, jnp.full((SLICES, MODEL_WIDTH, FF_DEV), 0.25 * expert_base(), jnp.float32))


def draw_outer_moment(key, part):
    key = jax.random.fold_in(key, 41)
    return first_state(key, jnp.full((SLICES, FF_DEV, MODEL_WIDTH), 0.5 * expert_base(), jnp.float32))


def draw_outer_square(key, part):
    key = jax.random.fold_in(key, 42)
    return second_state(key, jnp.full((SLICES, FF_DEV, MODEL_WIDTH), 0.5 * expert_base(), jnp.float32))


def draw_expert_bias(key, part):
    key = jax.random.fold_in(key, 51)
    scale_list = column_scales(((FF_DEV, 0.14), (MODEL_WIDTH // SPLIT, 0.1)))
    return jax.random.normal(key, (SLICES, FF_DEV + MODEL_WIDTH // SPLIT), jnp.float32) * scale_list[None, :]


def draw_bias_moment(key, part):
    key = jax.random.fold_in(key, 52)
    return first_state(key, bias_scales())


def draw_bias_square(key, part):
    key = jax.random.fold_in(key, 53)
    return second_state(key, bias_scales())


def steps_of(own_key, dims, cuts, low, top_value):
    level, own = 1.0, jax.random.fold_in(own_key, 6)
    for axis_at, blocks in cuts:
        draws = jnp.exp(jax.random.uniform(jax.random.fold_in(own, axis_at), (blocks,), jnp.float32, low / len(cuts), top_value / len(cuts)))
        level = level * jnp.repeat(draws, dims[axis_at] // blocks).reshape([-1 if axis == axis_at else 1 for axis in range(len(dims))])
    return level


def different_ones(stream_key, rows, count, top, lift):
    order = jax.random.permutation(jax.random.fold_in(stream_key, 1), count)
    favour = order
    for power in range(3):
        favour = favour * favour // count
    favour = favour * lift // count
    chance = jax.random.randint(jax.random.fold_in(stream_key, 2), (rows, count), 0, 4096) + favour
    holders = jax.random.permutation(jax.random.fold_in(stream_key, 3), rows)[jnp.arange(count) % rows]
    chance = jnp.where(jnp.arange(rows)[:, None] == holders[None, :], 1 << 14, chance)
    score = chance * count + jnp.arange(count)
    return lax.top_k(score.astype(jnp.int32), top)[1].astype(jnp.int32)


def bell_draw(own_key, dims, width, limit, cuts=(), held_as=jnp.bfloat16):
    drawn = width * jax.random.normal(own_key, dims, jnp.float32)
    if cuts:
        drawn = drawn * steps_of(own_key, dims, cuts, -0.22, 0.18)
    return jnp.clip(drawn, -limit, limit).astype(held_as)


def setup_inputs(seed: int = 0) -> dict:
    keys = jax.random.split(jax.random.key(seed), 20)
    tokens = bell_draw(keys[0], (TOKENS, MODEL_WIDTH), 1.0, 6.0, ((0, 32),))
    cotangent = bell_draw(keys[1], (TOKENS, MODEL_WIDTH), 1.0, 6.0, ((0, 32),))
    routes = different_ones(keys[2], TOKENS, EXPERTS, 1, 256)
    images = draw_images(jax.random.fold_in(keys[19], 71), 0)
    dense_weight = draw_dense_weight(jax.random.fold_in(keys[19], 71), 0)
    dense_moment = draw_dense_moment(jax.random.fold_in(keys[19], 71), 0)
    dense_square = draw_dense_square(jax.random.fold_in(keys[19], 71), 0)
    small_params = draw_small_params(jax.random.fold_in(keys[19], 71), 0)
    small_moment = draw_small_moment(jax.random.fold_in(keys[19], 71), 0)
    small_square = draw_small_square(jax.random.fold_in(keys[19], 71), 0)
    inner_weight = bell_draw(keys[10], (SLICES, MODEL_WIDTH, FF_DEV), MODEL_WIDTH ** -0.5, 0.3125, ((0, 32),), jnp.float32)
    inner_moment = draw_inner_moment(jax.random.fold_in(keys[19], 71), 0)
    inner_square = draw_inner_square(jax.random.fold_in(keys[19], 71), 0)
    outer_weight = bell_draw(keys[13], (SLICES, FF_DEV, MODEL_WIDTH), FF ** -0.5, 0.15625, ((0, 32),), jnp.float32)
    outer_moment = draw_outer_moment(jax.random.fold_in(keys[19], 71), 0)
    outer_square = draw_outer_square(jax.random.fold_in(keys[19], 71), 0)
    expert_bias = draw_expert_bias(jax.random.fold_in(keys[19], 71), 0)
    bias_moment = draw_bias_moment(jax.random.fold_in(keys[19], 71), 0)
    bias_square = draw_bias_square(jax.random.fold_in(keys[19], 71), 0)
    return dict(tokens=tokens, cotangent=cotangent, routes=routes, images=images, dense_weight=dense_weight, dense_moment=dense_moment, dense_square=dense_square, small_params=small_params, small_moment=small_moment, small_square=small_square, inner_weight=inner_weight, inner_moment=inner_moment, inner_square=inner_square, outer_weight=outer_weight, outer_moment=outer_moment, outer_square=outer_square, expert_bias=expert_bias, bias_moment=bias_moment, bias_square=bias_square)


@jax.custom_vjp
def low(v):
    return lax.optimization_barrier(v.astype(jnp.bfloat16)).astype(jnp.float32)

@jax.custom_vjp
def low_back(v):
    return v

def low_keep(v):
    return (low(v), None)

def low_pass(kept, grad):
    return (grad,)

def back_keep(v):
    return (v, None)

def back_low(kept, grad):
    return (low(grad),)
low.defvjp(low_keep, low_pass)
low_back.defvjp(back_keep, back_low)
highest = lax.Precision.HIGHEST
beta_one = 0.9
beta_two = 0.999
epsilon = 1e-08
dense_rate = 0.05
expert_rate = 0.05
small_rate = 0.3
weight_decay = 0.05

def pieces(small_params):
    length_list = (MODEL_WIDTH, MODEL_WIDTH, MODEL_WIDTH, MODEL_WIDTH, MODEL_WIDTH, MODEL_WIDTH, MODEL_WIDTH, ATTENTION_HEADS, BIAS_NET_HIDDEN, 2 * BIAS_NET_HIDDEN, BIAS_NET_HIDDEN * ATTENTION_HEADS)
    piece_collection = []
    offset = 0
    for length in length_list:
        piece_collection.append(small_params[offset:offset + length])
        offset = offset + length
    piece_collection[9] = piece_collection[9].reshape(2, BIAS_NET_HIDDEN)
    piece_collection[10] = piece_collection[10].reshape(BIAS_NET_HIDDEN, ATTENTION_HEADS)
    return piece_collection

def norm_rows(values, gain, shift):
    average = lax.optimization_barrier(jnp.mean(values, axis=-1, keepdims=True))
    centred = values - average
    variance = lax.optimization_barrier(jnp.mean(centred * centred, axis=-1, keepdims=True))
    return centred * lax.rsqrt(variance + 1e-05) * gain + shift

def position_bias(small_params):
    piece_collection = pieces(small_params)
    span = 2 * SIDE - 1
    offsets = jnp.arange(span, dtype=jnp.float32) - (SIDE - 1)
    coords = jnp.stack([jnp.repeat(offsets, span), jnp.tile(offsets, span)], axis=1) * (8.0 / (SIDE - 1))
    coords = jnp.sign(coords) * jnp.log2(jnp.abs(coords) + 1.0) / 3.0
    hidden = jax.nn.gelu(jnp.dot(coords, piece_collection[9], precision=highest) + piece_collection[8])
    table = 16.0 * jax.nn.sigmoid(jnp.dot(hidden, piece_collection[10], precision=highest))
    places = jnp.arange(WIN, dtype=jnp.int32)
    row_pos = places // SIDE
    col_pos = places % SIDE
    index = (row_pos[:, None] - row_pos[None, :] + SIDE - 1) * span + (col_pos[:, None] - col_pos[None, :] + SIDE - 1)
    lookup = (index.reshape(-1, 1) == jnp.arange(span * span, dtype=jnp.int32)[None, :]).astype(table.dtype)
    spread = jnp.dot(lookup, table, precision=highest)
    return spread.T.reshape(ATTENTION_HEADS, WIN, WIN)

def attend_route(inputs, weights, small_params, bias, route_ids):
    piece_collection = pieces(small_params)
    rows_here = inputs.shape[0]
    window_count = rows_here // WIN
    joined_bias = jnp.concatenate([piece_collection[4], jnp.zeros_like(piece_collection[4]), piece_collection[5]])
    projected = low_back(jnp.dot(inputs, weights[:, :3 * MODEL_WIDTH], precision=highest) + joined_bias)
    shaped = projected.reshape(window_count, WIN, 3, ATTENTION_HEADS, HEAD_DIM)
    queries = shaped[:, :, 0]
    key_vecs = shaped[:, :, 1]
    values = low(shaped[:, :, 2])
    queries = low(queries * lax.rsqrt(lax.optimization_barrier(jnp.sum(queries * queries, axis=-1, keepdims=True)) + 1e-06))
    key_vecs = low(key_vecs * lax.rsqrt(lax.optimization_barrier(jnp.sum(key_vecs * key_vecs, axis=-1, keepdims=True)) + 1e-06))
    cosine = low_back(jnp.einsum('wihd,wjhd->whij', queries, key_vecs, precision=highest))
    scores = cosine * jnp.exp(piece_collection[7])[:, None, None] + bias
    softmax_out = jax.nn.softmax(scores, axis=-1)
    mixed = jnp.einsum('whij,wjhd->wihd', low(softmax_out), values, precision=highest).reshape(rows_here, MODEL_WIDTH)
    mixed = low(low_back(mixed))
    attended = low_back(jnp.dot(mixed, weights[:, 3 * MODEL_WIDTH:4 * MODEL_WIDTH], precision=highest) + piece_collection[6])
    section_one = inputs + norm_rows(attended, piece_collection[0], piece_collection[1])
    rounded = low(section_one)
    logits = low_back(jnp.dot(rounded, weights[:, 4 * MODEL_WIDTH:], precision=highest))
    chosen_mask = (route_ids[:, None] == jnp.arange(logits.shape[1], dtype=jnp.int32)[None, :]).astype(logits.dtype)
    gating = jax.nn.sigmoid(lax.optimization_barrier(jnp.sum(logits * chosen_mask, axis=1)))
    return (section_one, gating, rounded)

def finish_block(section_one, gating, combined, kept_rows, live_rows, small_params):
    piece_collection = pieces(small_params)
    branch = norm_rows(combined, piece_collection[2], piece_collection[3]) * (gating * kept_rows)[:, None]
    return (section_one + branch) * live_rows[:, None]

def expert_apply(expert_rows, first_stack, second_stack, bias_stack):
    ff_dev = first_stack.shape[2]
    piece = MODEL_WIDTH // SPLIT
    total = jnp.zeros((expert_rows.shape[0], MODEL_WIDTH), jnp.float32)
    for member in range(SPLIT):
        rows_member = low_back(expert_rows)
        pre_act = low_back(jnp.dot(rows_member, low(first_stack[member]), precision=highest) + bias_stack[member, :ff_dev])
        hidden = low(jax.nn.gelu(pre_act))
        placed = jnp.concatenate([jnp.zeros((member * piece,), jnp.float32), bias_stack[member, ff_dev:], jnp.zeros(((SPLIT - 1 - member) * piece,), jnp.float32)])
        total = total + low(low_back(jnp.dot(hidden, low(second_stack[member]), precision=highest) + placed))
    return total

def assign(route_ids, count, experts, capacity):
    places = jnp.arange(route_ids.shape[0], dtype=jnp.int32)
    live_rows = places // IMG_TOK < count
    chosen = ((route_ids[:, None] == jnp.arange(experts, dtype=jnp.int32)[None, :]) & live_rows[:, None]).astype(jnp.int32)
    before = jnp.cumsum(chosen, axis=0).astype(jnp.int32) - chosen
    slot = lax.optimization_barrier(jnp.sum(before * chosen, axis=1)).astype(jnp.int32)
    kept_rows = live_rows & (slot < capacity)
    dest_slot = jnp.where(kept_rows, route_ids * capacity + slot, experts * capacity).astype(jnp.int32)
    return (live_rows, kept_rows, dest_slot)

def adamw_step(weight, gradient, first, second, rate, decay):
    first_new = beta_one * first + (1.0 - beta_one) * gradient
    second_new = beta_two * second + (1.0 - beta_two) * gradient * gradient
    first_hat = first_new / (1.0 - beta_one ** STEP)
    second_hat = second_new / (1.0 - beta_two ** STEP)
    weight_new = weight - rate * (first_hat / (jnp.sqrt(second_hat) + epsilon) + decay * weight)
    return (weight_new, first_new, second_new)

def reference(tokens, cotangent, routes, images, dense_weight, dense_moment, dense_square, small_params, small_moment, small_square, inner_weight, inner_moment, inner_square, outer_weight, outer_moment, outer_square, expert_bias, bias_moment, bias_square):
    devices = SLICES
    route_dev = routes[:, 0].reshape(devices, TOK_DEV).astype(jnp.int32)

    def assign_one(bundle):
        return assign(bundle[0], bundle[1], EXPERTS, CAP)
    live_rows, kept_rows, dest_slot = lax.map(assign_one, (route_dev, images.astype(jnp.int32)))
    source = jnp.arange(devices, dtype=jnp.int32)[:, None]
    slot_total = EXPERTS * devices * CAP
    position = jnp.where(kept_rows, route_dev * (devices * CAP) + source * CAP + (dest_slot - route_dev * CAP), slot_total).astype(jnp.int32)
    token_ids = jnp.arange(TOKENS, dtype=jnp.int32)
    owner_ids = jnp.full((slot_total + 1,), TOKENS, jnp.int32).at[position.reshape(-1)].set(token_ids)
    owner_ids = owner_ids[:slot_total].reshape(EXPERTS, devices * CAP)
    live_f = live_rows.reshape(TOKENS).astype(jnp.float32)
    keep_f = kept_rows.reshape(TOKENS).astype(jnp.float32)
    flat_position = position.reshape(TOKENS)

    def forward(inputs, dense, params, inner, outer, ebias):
        weights = low(dense)
        bias = position_bias(params)

        def block(bundle):
            return attend_route(bundle[0], weights, params, bias, bundle[1])
        section_one, gating, expert_feed = lax.map(jax.checkpoint(block), (inputs.reshape(devices, TOK_DEV, MODEL_WIDTH), route_dev))
        padded = jnp.concatenate([expert_feed.reshape(TOKENS, MODEL_WIDTH), jnp.zeros((1, MODEL_WIDTH), expert_feed.dtype)], axis=0)
        gathered_rows = jnp.take(padded, owner_ids, axis=0)

        def expert(bundle):
            return expert_apply(bundle[3], bundle[0], bundle[1], bundle[2])
        results = lax.map(jax.checkpoint(expert), (inner.reshape(EXPERTS, SPLIT, MODEL_WIDTH, FF_DEV), outer.reshape(EXPERTS, SPLIT, FF_DEV, MODEL_WIDTH), ebias.reshape(EXPERTS, SPLIT, FF_DEV + MODEL_WIDTH // SPLIT), gathered_rows))
        stacked = jnp.concatenate([results.reshape(-1, MODEL_WIDTH), jnp.zeros((1, MODEL_WIDTH), results.dtype)], axis=0)
        combined = jnp.take(stacked, flat_position, axis=0)
        return finish_block(section_one.reshape(TOKENS, MODEL_WIDTH), gating.reshape(TOKENS), combined, keep_f, live_f, params)
    layer_value, pullback = jax.vjp(forward, tokens.astype(jnp.float32), dense_weight, small_params, inner_weight, outer_weight, expert_bias)
    grads = pullback(cotangent.astype(jnp.float32))
    dense_out = adamw_step(dense_weight, grads[1], dense_moment, dense_square, dense_rate, weight_decay)
    small_out = adamw_step(small_params, grads[2], small_moment, small_square, small_rate, 0.0)
    inner_out = adamw_step(inner_weight, grads[3], inner_moment, inner_square, expert_rate, weight_decay)
    outer_out = adamw_step(outer_weight, grads[4], outer_moment, outer_square, expert_rate, weight_decay)
    bias_out = adamw_step(expert_bias, grads[5], bias_moment, bias_square, expert_rate, 0.0)
    return (layer_value.astype(jnp.bfloat16), grads[0].astype(jnp.bfloat16), dense_out[0], dense_out[1], dense_out[2], small_out[0], small_out[1], small_out[2], inner_out[0], inner_out[1], inner_out[2], inner_out[0].astype(jnp.bfloat16), outer_out[0], outer_out[1], outer_out[2], outer_out[0].astype(jnp.bfloat16), bias_out[0], bias_out[1], bias_out[2])
```

```python
import jax
import jax.numpy as jnp
from jax import lax
from jax.sharding import PartitionSpec as P

MODEL_WIDTH = 384
ATTENTION_HEADS = 12
HEAD_DIM = 32
BIAS_NET_HIDDEN = 512
EXPERTS = 32
SIDE = 8
IMG_TOK = 1024
STEP = 10
WIN = 64


highest = lax.Precision.HIGHEST
beta_one = 0.9
beta_two = 0.999
epsilon = 1e-08
dense_rate = 0.05
expert_rate = 0.05
small_rate = 0.3
weight_decay = 0.05
contract_rows = (((0,), (0,)), ((), ()))
contract_cols = (((1,), (1,)), ((), ()))


def pieces(small_params):
    length_list = (
        MODEL_WIDTH,
        MODEL_WIDTH,
        MODEL_WIDTH,
        MODEL_WIDTH,
        MODEL_WIDTH,
        MODEL_WIDTH,
        MODEL_WIDTH,
        ATTENTION_HEADS,
        BIAS_NET_HIDDEN,
        2 * BIAS_NET_HIDDEN,
        BIAS_NET_HIDDEN * ATTENTION_HEADS,
    )
    piece_collection = []
    offset = 0
    for length in length_list:
        piece_collection.append(small_params[offset : offset + length])
        offset = offset + length
    piece_collection[9] = piece_collection[9].reshape(2, BIAS_NET_HIDDEN)
    piece_collection[10] = piece_collection[10].reshape(BIAS_NET_HIDDEN, ATTENTION_HEADS)
    return piece_collection


def norm_rows(values, gain, shift):
    average = jnp.mean(values, axis=-1, keepdims=True)
    centred = values - average
    variance = jnp.mean(centred * centred, axis=-1, keepdims=True)
    return centred * lax.rsqrt(variance + 1e-05) * gain + shift


def position_bias(small_params):
    piece_collection = pieces(small_params)
    span = 2 * SIDE - 1
    offsets = jnp.arange(span, dtype=jnp.float32) - (SIDE - 1)
    coords = jnp.stack([jnp.repeat(offsets, span), jnp.tile(offsets, span)], axis=1) * (
        8.0 / (SIDE - 1)
    )
    coords = jnp.sign(coords) * jnp.log2(jnp.abs(coords) + 1.0) / 3.0
    hidden = jax.nn.gelu(
        jnp.dot(coords, piece_collection[9], precision=highest) + piece_collection[8]
    )
    table = 16.0 * jax.nn.sigmoid(jnp.dot(hidden, piece_collection[10], precision=highest))
    places = jnp.arange(WIN, dtype=jnp.int32)
    row_pos = places // SIDE
    col_pos = places % SIDE
    index = (row_pos[:, None] - row_pos[None, :] + SIDE - 1) * span + (
        col_pos[:, None] - col_pos[None, :] + SIDE - 1
    )
    lookup = (index.reshape(-1, 1) == jnp.arange(span * span, dtype=jnp.int32)[None, :]).astype(
        table.dtype
    )
    spread = jnp.dot(lookup, table, precision=highest)
    return spread.T.reshape(ATTENTION_HEADS, WIN, WIN)


def matmul_back(left_low, right_low, grad_low):
    grad_left = lax.dot_general(
        grad_low, right_low, contract_cols, preferred_element_type=jnp.float32
    )
    grad_right = lax.dot_general(
        left_low, grad_low, contract_rows, preferred_element_type=jnp.float32
    )
    return (grad_left, grad_right)


def add_joined_bias(raw, params):
    piece_collection = pieces(params)
    return raw + jnp.concatenate(
        [piece_collection[4], jnp.zeros_like(piece_collection[4]), piece_collection[5]]
    )


def add_out_bias(raw, params):
    return raw + pieces(params)[6]


def normalize_heads(projected):
    window_count = projected.shape[0] // WIN
    shaped = projected.reshape(window_count, WIN, 3, ATTENTION_HEADS, HEAD_DIM)
    queries = shaped[:, :, 0]
    key_vecs = shaped[:, :, 1]
    queries = queries * lax.rsqrt(jnp.sum(queries * queries, axis=-1, keepdims=True) + 1e-06)
    key_vecs = key_vecs * lax.rsqrt(jnp.sum(key_vecs * key_vecs, axis=-1, keepdims=True) + 1e-06)
    return (queries, key_vecs, shaped[:, :, 2])


def softmax_part(cosine, params):
    scale = jnp.exp(pieces(params)[7])[:, None, None]
    return jax.nn.softmax(cosine * scale + position_bias(params), axis=-1)


def front_forward(tokens_low, weights_low, params):
    rows_here = tokens_low.shape[0]
    qkv_low = weights_low[:, : 3 * MODEL_WIDTH]
    out_low = weights_low[:, 3 * MODEL_WIDTH : 4 * MODEL_WIDTH]
    raw_qkv = jnp.dot(tokens_low, qkv_low, preferred_element_type=jnp.float32)
    projected = add_joined_bias(raw_qkv, params)
    q_f, k_f, v_f = normalize_heads(projected)
    q_low = q_f.astype(jnp.bfloat16)
    k_low = k_f.astype(jnp.bfloat16)
    v_low = v_f.astype(jnp.bfloat16)
    cosine = jnp.einsum("wihd,wjhd->whij", q_low, k_low, preferred_element_type=jnp.float32)
    probs = softmax_part(cosine, params)
    probs_low = probs.astype(jnp.bfloat16)
    mixed_low = (
        jnp.einsum("whij,wjhd->wihd", probs_low, v_low, preferred_element_type=jnp.float32)
        .astype(jnp.bfloat16)
        .reshape(rows_here, MODEL_WIDTH)
    )
    attended = add_out_bias(jnp.dot(mixed_low, out_low, preferred_element_type=jnp.float32), params)
    piece_collection = pieces(params)
    section_one = tokens_low.astype(jnp.float32) + norm_rows(
        attended, piece_collection[0], piece_collection[1]
    )
    section_low = section_one.astype(jnp.bfloat16)
    kept = (
        projected,
        q_low,
        k_low,
        v_low,
        cosine,
        probs_low,
        mixed_low,
        attended,
    )
    return (section_one, section_low, kept)


def front_backward(tokens_low, weights_low, params, kept, grad_total):
    (
        projected,
        q_low,
        k_low,
        v_low,
        cosine,
        probs_low,
        mixed_low,
        attended,
    ) = kept
    rows_here = tokens_low.shape[0]
    window_count = rows_here // WIN
    qkv_low = weights_low[:, : 3 * MODEL_WIDTH]
    out_low = weights_low[:, 3 * MODEL_WIDTH : 4 * MODEL_WIDTH]

    def section_part(attended_value, params_value):
        piece_collection = pieces(params_value)
        return norm_rows(attended_value, piece_collection[0], piece_collection[1])

    section_back = jax.vjp(section_part, attended, params)[1]
    grad_attended, grad_params_a = section_back(grad_total)
    grad_att_low = grad_attended.astype(jnp.bfloat16)
    grad_params_b = jax.vjp(add_out_bias, jnp.zeros_like(attended), params)[1](
        grad_att_low.astype(jnp.float32)
    )[1]
    grad_mixed, grad_out = matmul_back(mixed_low, out_low, grad_att_low)
    grad_mixed_low = grad_mixed.astype(jnp.bfloat16).reshape(
        window_count, WIN, ATTENTION_HEADS, HEAD_DIM
    )
    grad_probs = jnp.einsum(
        "wihd,wjhd->whij", grad_mixed_low, v_low, preferred_element_type=jnp.float32
    )
    grad_v = jnp.einsum(
        "whij,wihd->wjhd", probs_low, grad_mixed_low, preferred_element_type=jnp.float32
    )
    soft_back = jax.vjp(softmax_part, cosine, params)[1]
    grad_cosine, grad_params_c = soft_back(grad_probs)
    grad_cos_low = grad_cosine.astype(jnp.bfloat16)
    grad_q = jnp.einsum("whij,wjhd->wihd", grad_cos_low, k_low, preferred_element_type=jnp.float32)
    grad_k = jnp.einsum("whij,wihd->wjhd", grad_cos_low, q_low, preferred_element_type=jnp.float32)
    norm_back = jax.vjp(normalize_heads, projected)[1]
    grad_projected = norm_back((grad_q, grad_k, grad_v))[0]
    grad_proj_low = grad_projected.astype(jnp.bfloat16)
    grad_params_d = jax.vjp(add_joined_bias, jnp.zeros_like(projected), params)[1](
        grad_proj_low.astype(jnp.float32)
    )[1]
    grad_tokens, grad_qkv = matmul_back(tokens_low, qkv_low, grad_proj_low)
    grad_inputs = grad_total + grad_tokens
    grad_weights = jnp.concatenate([grad_qkv, grad_out], axis=1)
    grad_params = grad_params_a + grad_params_b + grad_params_c + grad_params_d
    return (grad_inputs, grad_weights, grad_params)


def front_forward_split(tokens_low, weights_low, params, route_ids):
    rows_here = tokens_low.shape[0]
    qkv_low = weights_low[:, : 3 * MODEL_WIDTH]
    out_low = weights_low[:, 3 * MODEL_WIDTH : 4 * MODEL_WIDTH]
    route_low = weights_low[:, 4 * MODEL_WIDTH :]
    raw_qkv = jnp.dot(tokens_low, qkv_low, preferred_element_type=jnp.float32)
    projected = add_joined_bias(raw_qkv, params)
    q_f, k_f, v_f = normalize_heads(projected)
    q_low = q_f.astype(jnp.bfloat16)
    k_low = k_f.astype(jnp.bfloat16)
    v_low = v_f.astype(jnp.bfloat16)
    cosine = jnp.einsum("wihd,wjhd->whij", q_low, k_low, preferred_element_type=jnp.float32)
    probs = softmax_part(cosine, params)
    probs_low = probs.astype(jnp.bfloat16)
    mixed_low = (
        jnp.einsum("whij,wjhd->wihd", probs_low, v_low, preferred_element_type=jnp.float32)
        .astype(jnp.bfloat16)
        .reshape(rows_here, MODEL_WIDTH)
    )
    attended = add_out_bias(jnp.dot(mixed_low, out_low, preferred_element_type=jnp.float32), params)
    piece_collection = pieces(params)
    section_one = tokens_low.astype(jnp.float32) + norm_rows(
        attended, piece_collection[0], piece_collection[1]
    )
    section_low = section_one.astype(jnp.bfloat16)
    logits = jnp.dot(section_low, route_low, preferred_element_type=jnp.float32)
    chosen_mask = (
        route_ids[:, None] == jnp.arange(logits.shape[1], dtype=jnp.int32)[None, :]
    ).astype(jnp.float32)
    gating = jax.nn.sigmoid(jnp.sum(logits * chosen_mask, axis=1))
    kept = (
        projected,
        q_low,
        k_low,
        v_low,
        cosine,
        probs_low,
        mixed_low,
        attended,
        section_low,
        logits,
        chosen_mask,
    )
    return (section_one, gating, section_low, kept)


def front_backward_split(tokens_low, weights_low, params, kept, grad_section, grad_gate, grad_feed):
    (
        projected,
        q_low,
        k_low,
        v_low,
        cosine,
        probs_low,
        mixed_low,
        attended,
        section_low,
        logits,
        chosen_mask,
    ) = kept
    rows_here = tokens_low.shape[0]
    window_count = rows_here // WIN
    qkv_low = weights_low[:, : 3 * MODEL_WIDTH]
    out_low = weights_low[:, 3 * MODEL_WIDTH : 4 * MODEL_WIDTH]
    route_low = weights_low[:, 4 * MODEL_WIDTH :]

    def gate_part(logit_values):
        return jax.nn.sigmoid(jnp.sum(logit_values * chosen_mask, axis=1))

    gate_back = jax.vjp(gate_part, logits)[1]
    grad_logits = gate_back(grad_gate)[0].astype(jnp.bfloat16)
    grad_from_route, grad_route = matmul_back(section_low, route_low, grad_logits)
    grad_total = grad_section + grad_feed + grad_from_route

    def section_part(attended_value, params_value):
        piece_collection = pieces(params_value)
        return norm_rows(attended_value, piece_collection[0], piece_collection[1])

    section_back = jax.vjp(section_part, attended, params)[1]
    grad_attended, grad_params_a = section_back(grad_total)
    grad_att_low = grad_attended.astype(jnp.bfloat16)
    grad_params_b = jax.vjp(add_out_bias, jnp.zeros_like(attended), params)[1](
        grad_att_low.astype(jnp.float32)
    )[1]
    grad_mixed, grad_out = matmul_back(mixed_low, out_low, grad_att_low)
    grad_mixed_low = grad_mixed.astype(jnp.bfloat16).reshape(
        window_count, WIN, ATTENTION_HEADS, HEAD_DIM
    )
    grad_probs = jnp.einsum(
        "wihd,wjhd->whij", grad_mixed_low, v_low, preferred_element_type=jnp.float32
    )
    grad_v = jnp.einsum(
        "whij,wihd->wjhd", probs_low, grad_mixed_low, preferred_element_type=jnp.float32
    )
    soft_back = jax.vjp(softmax_part, cosine, params)[1]
    grad_cosine, grad_params_c = soft_back(grad_probs)
    grad_cos_low = grad_cosine.astype(jnp.bfloat16)
    grad_q = jnp.einsum("whij,wjhd->wihd", grad_cos_low, k_low, preferred_element_type=jnp.float32)
    grad_k = jnp.einsum("whij,wihd->wjhd", grad_cos_low, q_low, preferred_element_type=jnp.float32)
    norm_back = jax.vjp(normalize_heads, projected)[1]
    grad_projected = norm_back((grad_q, grad_k, grad_v))[0]
    grad_proj_low = grad_projected.astype(jnp.bfloat16)
    grad_params_d = jax.vjp(add_joined_bias, jnp.zeros_like(projected), params)[1](
        grad_proj_low.astype(jnp.float32)
    )[1]
    grad_tokens, grad_qkv = matmul_back(tokens_low, qkv_low, grad_proj_low)
    grad_inputs = grad_total + grad_tokens
    grad_weights = jnp.concatenate([grad_qkv, grad_out, grad_route], axis=1)
    grad_params = grad_params_a + grad_params_b + grad_params_c + grad_params_d
    return (grad_inputs, grad_weights, grad_params)


def finish_block(section_one, gating, combined, kept_rows, live_rows, small_params):
    piece_collection = pieces(small_params)
    branch = (
        norm_rows(combined, piece_collection[2], piece_collection[3])
        * (gating * kept_rows)[:, None]
    )
    return (section_one + branch) * live_rows[:, None]


def assign(route_ids, count, experts, capacity):
    places = jnp.arange(route_ids.shape[0], dtype=jnp.int32)
    live_rows = places // IMG_TOK < count
    chosen = (
        (route_ids[:, None] == jnp.arange(experts, dtype=jnp.int32)[None, :]) & live_rows[:, None]
    ).astype(jnp.int32)
    before = jnp.cumsum(chosen, axis=0) - chosen
    slot = jnp.sum(before * chosen, axis=1)
    kept_rows = live_rows & (slot < capacity)
    dest_slot = jnp.where(kept_rows, route_ids * capacity + slot, experts * capacity)
    return (live_rows, kept_rows, dest_slot)


def adamw_step(weight, gradient, first, second, rate, decay):
    first_new = beta_one * first + (1.0 - beta_one) * gradient
    second_new = beta_two * second + (1.0 - beta_two) * gradient * gradient
    first_hat = first_new / (1.0 - beta_one**STEP)
    second_hat = second_new / (1.0 - beta_two**STEP)
    weight_new = weight - rate * (first_hat / (jnp.sqrt(second_hat) + epsilon) + decay * weight)
    return (weight_new, first_new, second_new)


def trade_rows(payload):
    arrived_rows = lax.all_to_all(
        payload, ("wide", "narrow"), split_axis=0, concat_axis=0, tiled=True
    )
    return arrived_rows


def axis_bits(axis):
    size = lax.axis_size(axis)
    return [(axis, 1 << k) for k in range(size.bit_length() - 1)]


def swap(value, step):
    axis, offset = step
    return lax.ppermute(value, axis, [(i, i ^ offset) for i in range(lax.axis_size(axis))])


def upper(step):
    axis, offset = step
    return (lax.axis_index(axis) & offset) > 0


def gather_rows(share):
    steps = axis_bits("narrow") + axis_bits("wide")
    first, rest = steps[0], steps[1:]
    other = swap(share, first)
    block = jnp.where(
        upper(first), jnp.concatenate([other, share]), jnp.concatenate([share, other])
    )
    held = block
    done = []
    core = ("wide", 1)
    for step in [s for s in rest if s != core] + [core]:
        place = sum(1 for d in done if rest.index(d) > rest.index(step))
        other = swap(held, step)
        held = jnp.where(
            upper(step), jnp.stack([other, held], place), jnp.stack([held, other], place)
        )
        done.append(step)
    return held.reshape(-1, share.shape[1])


def sum_grads(partial, small):
    steps = axis_bits("narrow") + axis_bits("wide")
    first, rest = steps[0], steps[1:]
    core = ("wide", 1)
    order = [core] + [s for s in rest[::-1] if s != core]
    count = lax.axis_size(("wide", "narrow"))
    share = partial.shape[0] // count
    held = partial.reshape((2,) * len(rest) + (2 * share, partial.shape[1]))
    left = rest[::-1]
    for step in order:
        place = left.index(step)
        side = upper(step).astype(jnp.int32)
        send = lax.dynamic_index_in_dim(held, 1 - side, place, keepdims=False)
        keep = lax.dynamic_index_in_dim(held, side, place, keepdims=False)
        other = swap(send.astype(jnp.bfloat16), step)
        small = small + swap(small, step)
        held = keep + other.astype(jnp.float32)
        left = [s for s in left if s != step]
    side = upper(first)
    send = jnp.where(side, held[:share], held[share:])
    keep = jnp.where(side, held[share:], held[:share])
    other = swap(send.astype(jnp.bfloat16), first)
    small = small + swap(small, first)
    return keep + other.astype(jnp.float32), small


def per_device_split(
    tokens,
    cotangent,
    routes,
    images,
    dense_weight,
    dense_moment,
    dense_square,
    small_params,
    small_moment,
    small_square,
    inner_weight,
    inner_moment,
    inner_square,
    outer_weight,
    outer_moment,
    outer_square,
    expert_bias,
    bias_moment,
    bias_square,
):
    slices = lax.axis_size(("wide", "narrow"))
    split = slices // EXPERTS
    member = lax.axis_index(("wide", "narrow")) % split
    piece = MODEL_WIDTH // split
    ff_dev = inner_weight.shape[2]
    tok_rows = tokens.shape[0]
    capacity = (5 * tok_rows + 4 * EXPERTS - 1) // (4 * EXPERTS)
    slot_total = EXPERTS * capacity
    route_ids = routes[:, 0]
    live_rows, kept_rows, dest_slot = assign(route_ids, images[0], EXPERTS, capacity)
    live_f = live_rows.astype(jnp.float32)
    keep_f = kept_rows.astype(jnp.float32)
    clipped = jnp.minimum(dest_slot, slot_total - 1)
    gathered = gather_rows(dense_weight.astype(jnp.bfloat16))
    section_one, gating, expert_feed, kept = front_forward_split(
        tokens, gathered, small_params, route_ids
    )

    def fan_out(rows_value):
        placed_rows = (
            jnp.zeros((slot_total, MODEL_WIDTH), jnp.bfloat16)
            .at[dest_slot]
            .set(rows_value.astype(jnp.bfloat16), mode="drop")
        )
        copies = jnp.broadcast_to(
            placed_rows.reshape(EXPERTS, 1, capacity, MODEL_WIDTH),
            (EXPERTS, split, capacity, MODEL_WIDTH),
        )
        return trade_rows(copies.reshape(slices, capacity, MODEL_WIDTH)).reshape(
            slices * capacity, MODEL_WIDTH
        )

    def fan_in(partials):
        arrived = trade_rows(partials.reshape(slices, capacity, MODEL_WIDTH))
        summed = jnp.sum(
            arrived.reshape(EXPERTS, split, capacity, MODEL_WIDTH).astype(jnp.float32), axis=1
        ).reshape(slot_total, MODEL_WIDTH)
        return jnp.take(summed, clipped, axis=0) * keep_f[:, None]

    expert_rows = fan_out(expert_feed)
    first_matrix = inner_weight[0].astype(jnp.bfloat16)
    second_matrix = outer_weight[0].astype(jnp.bfloat16)
    pre_act = (
        jnp.dot(expert_rows, first_matrix, preferred_element_type=jnp.float32)
        + expert_bias[0, :ff_dev]
    )
    hidden = jax.nn.gelu(pre_act).astype(jnp.bfloat16)
    out_bias = lax.dynamic_update_slice(
        jnp.zeros((MODEL_WIDTH,), jnp.float32), expert_bias[0, ff_dev:], (member * piece,)
    )
    result = (jnp.dot(hidden, second_matrix, preferred_element_type=jnp.float32) + out_bias).astype(
        jnp.bfloat16
    )
    combined = fan_in(result)

    def tail_local(section_value, gate_value, combined_value, params):
        return finish_block(section_value, gate_value, combined_value, keep_f, live_f, params)

    layer_value, tail_back = jax.vjp(tail_local, section_one, gating, combined, small_params)
    grad_section, grad_gate, grad_combined, grad_small_tail = tail_back(
        cotangent.astype(jnp.float32)
    )
    grad_result = fan_out(grad_combined)
    grad_outer = lax.dot_general(
        hidden, grad_result, contract_rows, preferred_element_type=jnp.float32
    )
    grad_hidden = lax.dot_general(
        grad_result, second_matrix, contract_cols, preferred_element_type=jnp.float32
    )
    gelu_back = jax.vjp(jax.nn.gelu, pre_act)[1]
    grad_pre = gelu_back(grad_hidden)[0].astype(jnp.bfloat16)
    grad_inner = lax.dot_general(
        expert_rows, grad_pre, contract_rows, preferred_element_type=jnp.float32
    )
    column_total = jnp.sum(grad_result.astype(jnp.float32), axis=0)
    grad_bias = jnp.concatenate(
        [
            jnp.sum(grad_pre.astype(jnp.float32), axis=0),
            lax.dynamic_slice_in_dim(column_total, member * piece, piece, 0),
        ]
    )
    grad_rows = lax.dot_general(
        grad_pre, first_matrix, contract_cols, preferred_element_type=jnp.float32
    ).astype(jnp.bfloat16)
    grad_feed = fan_in(grad_rows)
    grad_inputs, grad_weights, grad_small_front = front_backward_split(
        tokens, gathered, small_params, kept, grad_section, grad_gate, grad_feed
    )
    grad_small = grad_small_front + grad_small_tail
    grad_dense, grad_small = sum_grads(grad_weights, grad_small)
    dense_out = adamw_step(
        dense_weight, grad_dense, dense_moment, dense_square, dense_rate, weight_decay
    )
    small_out = adamw_step(small_params, grad_small, small_moment, small_square, small_rate, 0.0)
    inner_out = adamw_step(
        inner_weight, grad_inner[None], inner_moment, inner_square, expert_rate, weight_decay
    )
    outer_out = adamw_step(
        outer_weight, grad_outer[None], outer_moment, outer_square, expert_rate, weight_decay
    )
    bias_out = adamw_step(expert_bias, grad_bias[None], bias_moment, bias_square, expert_rate, 0.0)
    return (
        layer_value.astype(jnp.bfloat16),
        grad_inputs.astype(jnp.bfloat16),
        dense_out[0],
        dense_out[1],
        dense_out[2],
        small_out[0],
        small_out[1],
        small_out[2],
        inner_out[0],
        inner_out[1],
        inner_out[2],
        inner_out[0].astype(jnp.bfloat16),
        outer_out[0],
        outer_out[1],
        outer_out[2],
        outer_out[0].astype(jnp.bfloat16),
        bias_out[0],
        bias_out[1],
        bias_out[2],
    )


def per_device(
    tokens,
    cotangent,
    routes,
    images,
    dense_weight,
    dense_moment,
    dense_square,
    small_params,
    small_moment,
    small_square,
    inner_weight,
    inner_moment,
    inner_square,
    outer_weight,
    outer_moment,
    outer_square,
    expert_bias,
    bias_moment,
    bias_square,
):
    slices = lax.axis_size(("wide", "narrow"))
    if slices != EXPERTS:
        return per_device_split(
            tokens,
            cotangent,
            routes,
            images,
            dense_weight,
            dense_moment,
            dense_square,
            small_params,
            small_moment,
            small_square,
            inner_weight,
            inner_moment,
            inner_square,
            outer_weight,
            outer_moment,
            outer_square,
            expert_bias,
            bias_moment,
            bias_square,
        )
    expert = lax.axis_index(("wide", "narrow"))
    ff_dev = inner_weight.shape[2]
    tok_rows = tokens.shape[0]
    capacity = (5 * tok_rows + 4 * EXPERTS - 1) // (4 * EXPERTS)
    slot_total = EXPERTS * capacity
    route_ids = routes[:, 0]
    live_rows, kept_rows, dest_slot = assign(route_ids, images[0], EXPERTS, capacity)
    live_f = live_rows.astype(jnp.float32)[:, None]
    keep_f = kept_rows.astype(jnp.float32)[:, None]
    clipped = jnp.minimum(dest_slot, slot_total - 1)

    def place(rows_value):
        placed_rows = (
            jnp.zeros((slot_total, MODEL_WIDTH), jnp.bfloat16)
            .at[dest_slot]
            .set(rows_value, mode="drop")
        )
        return trade_rows(placed_rows.reshape(slices, capacity, MODEL_WIDTH)).reshape(
            slot_total, MODEL_WIDTH
        )

    def fetch(partials):
        arrived = trade_rows(partials.reshape(slices, capacity, MODEL_WIDTH))
        rows = arrived.reshape(slot_total, MODEL_WIDTH)
        return jnp.take(rows, clipped, axis=0).astype(jnp.float32) * keep_f

    grad_out_rows = place(cotangent).astype(jnp.float32)
    gathered = gather_rows(dense_weight.astype(jnp.bfloat16))
    section_one, section_low, kept = front_forward(tokens, gathered, small_params)
    expert_rows = place(section_low)

    piece_collection = pieces(small_params)
    gain_two, shift_two = piece_collection[2], piece_collection[3]
    first_matrix = inner_weight[0].astype(jnp.bfloat16)
    second_matrix = outer_weight[0].astype(jnp.bfloat16)
    pre_act = (
        jnp.dot(expert_rows, first_matrix, preferred_element_type=jnp.float32)
        + expert_bias[0, :ff_dev]
    )
    hidden = jax.nn.gelu(pre_act).astype(jnp.bfloat16)
    result = (
        jnp.dot(hidden, second_matrix, preferred_element_type=jnp.float32)
        + expert_bias[0, ff_dev:]
    ).astype(jnp.bfloat16)
    result_f = result.astype(jnp.float32)
    route_row = lax.dynamic_slice_in_dim(gathered, 4 * MODEL_WIDTH + expert, 1, 1)[:, 0].astype(
        jnp.float32
    )
    logit = jnp.sum(expert_rows.astype(jnp.float32) * route_row, axis=1, keepdims=True)
    gating = jax.nn.sigmoid(logit)
    average = jnp.mean(result_f, axis=-1, keepdims=True)
    centred = result_f - average
    spread = lax.rsqrt(jnp.mean(centred * centred, axis=-1, keepdims=True) + 1e-05)
    unit = centred * spread
    normed = unit * gain_two + shift_two
    branch = (normed * gating).astype(jnp.bfloat16)
    grad_gate = jnp.sum(grad_out_rows * normed, axis=-1, keepdims=True)
    gated = grad_out_rows * gating
    grad_gain_two = jnp.sum(gated * unit, axis=0)
    grad_shift_two = jnp.sum(gated, axis=0)
    grad_unit = gated * gain_two
    grad_result = (
        spread
        * (
            grad_unit
            - jnp.mean(grad_unit, axis=-1, keepdims=True)
            - unit * jnp.mean(grad_unit * unit, axis=-1, keepdims=True)
        )
    ).astype(jnp.bfloat16)
    grad_logit = (grad_gate * gating * (1.0 - gating)).astype(jnp.bfloat16)
    grad_hidden = lax.dot_general(
        grad_result, second_matrix, contract_cols, preferred_element_type=jnp.float32
    )
    gelu_back = jax.vjp(jax.nn.gelu, pre_act)[1]
    grad_pre = gelu_back(grad_hidden)[0].astype(jnp.bfloat16)
    grad_rows = (
        lax.dot_general(grad_pre, first_matrix, contract_cols, preferred_element_type=jnp.float32)
        + grad_logit.astype(jnp.float32) * route_row
    ).astype(jnp.bfloat16)
    grad_feed = fetch(grad_rows)
    grad_outer = lax.dot_general(
        hidden, grad_result, contract_rows, preferred_element_type=jnp.float32
    )
    grad_inner = lax.dot_general(
        expert_rows, grad_pre, contract_rows, preferred_element_type=jnp.float32
    )
    grad_route = lax.dot_general(
        expert_rows, grad_logit, contract_rows, preferred_element_type=jnp.float32
    )
    grad_route = jnp.where(jnp.arange(EXPERTS)[None, :] == expert, grad_route, 0.0)
    grad_bias = jnp.concatenate(
        [
            jnp.sum(grad_pre.astype(jnp.float32), axis=0),
            jnp.sum(grad_result.astype(jnp.float32), axis=0),
        ]
    )
    grad_section = cotangent.astype(jnp.float32) * live_f + grad_feed
    layer_out = ((section_one + fetch(branch)) * live_f).astype(jnp.bfloat16)
    grad_inputs, grad_weights, grad_small = front_backward(
        tokens, gathered, small_params, kept, grad_section
    )
    grad_weights = jnp.concatenate([grad_weights, grad_route], axis=1)
    grad_small = grad_small.at[2 * MODEL_WIDTH : 4 * MODEL_WIDTH].add(
        jnp.concatenate([grad_gain_two, grad_shift_two])
    )
    grad_dense, grad_small = sum_grads(grad_weights, grad_small)
    dense_out = adamw_step(
        dense_weight, grad_dense, dense_moment, dense_square, dense_rate, weight_decay
    )
    small_out = adamw_step(small_params, grad_small, small_moment, small_square, small_rate, 0.0)
    inner_out = adamw_step(
        inner_weight, grad_inner[None], inner_moment, inner_square, expert_rate, weight_decay
    )
    outer_out = adamw_step(
        outer_weight, grad_outer[None], outer_moment, outer_square, expert_rate, weight_decay
    )
    bias_out = adamw_step(expert_bias, grad_bias[None], bias_moment, bias_square, expert_rate, 0.0)
    return (
        layer_out,
        grad_inputs.astype(jnp.bfloat16),
        dense_out[0],
        dense_out[1],
        dense_out[2],
        small_out[0],
        small_out[1],
        small_out[2],
        inner_out[0],
        inner_out[1],
        inner_out[2],
        inner_out[0].astype(jnp.bfloat16),
        outer_out[0],
        outer_out[1],
        outer_out[2],
        outer_out[0].astype(jnp.bfloat16),
        bias_out[0],
        bias_out[1],
        bias_out[2],
    )


def solution(mesh):
    return jax.shard_map(
        per_device,
        mesh=mesh,
        in_specs=(
            P(("wide", "narrow"), None),
            P(("wide", "narrow"), None),
            P(("wide", "narrow"), None),
            P(("wide", "narrow")),
            P(("wide", "narrow"), None),
            P(("wide", "narrow"), None),
            P(("wide", "narrow"), None),
            P(),
            P(),
            P(),
            P(("wide", "narrow"), None, None),
            P(("wide", "narrow"), None, None),
            P(("wide", "narrow"), None, None),
            P(("wide", "narrow"), None, None),
            P(("wide", "narrow"), None, None),
            P(("wide", "narrow"), None, None),
            P(("wide", "narrow"), None),
            P(("wide", "narrow"), None),
            P(("wide", "narrow"), None),
        ),
        out_specs=(
            P(("wide", "narrow"), None),
            P(("wide", "narrow"), None),
            P(("wide", "narrow"), None),
            P(("wide", "narrow"), None),
            P(("wide", "narrow"), None),
            P(),
            P(),
            P(),
            P(("wide", "narrow"), None, None),
            P(("wide", "narrow"), None, None),
            P(("wide", "narrow"), None, None),
            P(("wide", "narrow"), None, None),
            P(("wide", "narrow"), None, None),
            P(("wide", "narrow"), None, None),
            P(("wide", "narrow"), None, None),
            P(("wide", "narrow"), None, None),
            P(("wide", "narrow"), None),
            P(("wide", "narrow"), None),
            P(("wide", "narrow"), None),
        ),
        check_vma=False,
    )
```

```python
import functools
import math

import jax
import jax.numpy as jnp
import numpy as np
from jax import lax
from jax.experimental import pallas as pl
from jax.experimental.pallas import tpu as pltpu
from jax.sharding import PartitionSpec as P

MODEL_WIDTH = 384
ATTENTION_HEADS = 12
HEAD_DIM = 32
BIAS_NET_HIDDEN = 512
EXPERTS = 32
SIDE = 8
IMG_TOK = 1024
STEP = 10
WIN = 64
GROUP = 4
GROUP_LANES = 128
VMEM_BYTES = 48 * 2**20
TABLE = 256
TABLE_MID = 119
STRIDE = 16
SUM_LANES = BIAS_NET_HIDDEN
SECOND_ROWS = 8
SHIFT_ROW = 20
FIRST_ROWS = 21
SCALE_ROWS = 24
ROUTE_ROWS = 32


highest = lax.Precision.HIGHEST
beta_one = 0.9
beta_two = 0.999
epsilon = 1e-08
dense_rate = 0.05
expert_rate = 0.05
small_rate = 0.3
weight_decay = 0.05
contract_rows = (((0,), (0,)), ((), ()))
contract_cols = (((1,), (1,)), ((), ()))


def pieces(small_params):
    length_list = (
        MODEL_WIDTH,
        MODEL_WIDTH,
        MODEL_WIDTH,
        MODEL_WIDTH,
        MODEL_WIDTH,
        MODEL_WIDTH,
        MODEL_WIDTH,
        ATTENTION_HEADS,
        BIAS_NET_HIDDEN,
        2 * BIAS_NET_HIDDEN,
        BIAS_NET_HIDDEN * ATTENTION_HEADS,
    )
    piece_collection = []
    offset = 0
    for length in length_list:
        piece_collection.append(small_params[offset : offset + length])
        offset = offset + length
    piece_collection[9] = piece_collection[9].reshape(2, BIAS_NET_HIDDEN)
    piece_collection[10] = piece_collection[10].reshape(BIAS_NET_HIDDEN, ATTENTION_HEADS)
    return piece_collection


def norm_rows(values, gain, shift):
    average = jnp.mean(values, axis=-1, keepdims=True)
    centred = values - average
    variance = jnp.mean(centred * centred, axis=-1, keepdims=True)
    return centred * lax.rsqrt(variance + 1e-05) * gain + shift


def position_bias(small_params):
    piece_collection = pieces(small_params)
    span = 2 * SIDE - 1
    offsets = jnp.arange(span, dtype=jnp.float32) - (SIDE - 1)
    coords = jnp.stack([jnp.repeat(offsets, span), jnp.tile(offsets, span)], axis=1) * (
        8.0 / (SIDE - 1)
    )
    coords = jnp.sign(coords) * jnp.log2(jnp.abs(coords) + 1.0) / 3.0
    hidden = jax.nn.gelu(
        jnp.dot(coords, piece_collection[9], precision=highest) + piece_collection[8]
    )
    table = 16.0 * jax.nn.sigmoid(jnp.dot(hidden, piece_collection[10], precision=highest))
    places = jnp.arange(WIN, dtype=jnp.int32)
    row_pos = places // SIDE
    col_pos = places % SIDE
    index = (row_pos[:, None] - row_pos[None, :] + SIDE - 1) * span + (
        col_pos[:, None] - col_pos[None, :] + SIDE - 1
    )
    lookup = (index.reshape(-1, 1) == jnp.arange(span * span, dtype=jnp.int32)[None, :]).astype(
        table.dtype
    )
    spread = jnp.dot(lookup, table, precision=highest)
    return spread.T.reshape(ATTENTION_HEADS, WIN, WIN)


def matmul_back(left_low, right_low, grad_low):
    grad_left = lax.dot_general(
        grad_low, right_low, contract_cols, preferred_element_type=jnp.float32
    )
    grad_right = lax.dot_general(
        left_low, grad_low, contract_rows, preferred_element_type=jnp.float32
    )
    return (grad_left, grad_right)


def add_joined_bias(raw, params):
    piece_collection = pieces(params)
    return raw + jnp.concatenate(
        [piece_collection[4], jnp.zeros_like(piece_collection[4]), piece_collection[5]]
    )


def add_out_bias(raw, params):
    return raw + pieces(params)[6]


def normalize_heads(projected):
    window_count = projected.shape[0] // WIN
    shaped = projected.reshape(window_count, WIN, 3, ATTENTION_HEADS, HEAD_DIM)
    queries = shaped[:, :, 0]
    key_vecs = shaped[:, :, 1]
    queries = queries * lax.rsqrt(jnp.sum(queries * queries, axis=-1, keepdims=True) + 1e-06)
    key_vecs = key_vecs * lax.rsqrt(jnp.sum(key_vecs * key_vecs, axis=-1, keepdims=True) + 1e-06)
    return (queries, key_vecs, shaped[:, :, 2])


def softmax_part(cosine, params):
    scale = jnp.exp(pieces(params)[7])[:, None, None]
    return jax.nn.softmax(cosine * scale + position_bias(params), axis=-1)


def front_forward_split(tokens_low, weights_low, params, route_ids):
    rows_here = tokens_low.shape[0]
    qkv_low = weights_low[:, : 3 * MODEL_WIDTH]
    out_low = weights_low[:, 3 * MODEL_WIDTH : 4 * MODEL_WIDTH]
    route_low = weights_low[:, 4 * MODEL_WIDTH :]
    raw_qkv = jnp.dot(tokens_low, qkv_low, preferred_element_type=jnp.float32)
    projected = add_joined_bias(raw_qkv, params)
    q_f, k_f, v_f = normalize_heads(projected)
    q_low = q_f.astype(jnp.bfloat16)
    k_low = k_f.astype(jnp.bfloat16)
    v_low = v_f.astype(jnp.bfloat16)
    cosine = jnp.einsum("wihd,wjhd->whij", q_low, k_low, preferred_element_type=jnp.float32)
    probs = softmax_part(cosine, params)
    probs_low = probs.astype(jnp.bfloat16)
    mixed_low = (
        jnp.einsum("whij,wjhd->wihd", probs_low, v_low, preferred_element_type=jnp.float32)
        .astype(jnp.bfloat16)
        .reshape(rows_here, MODEL_WIDTH)
    )
    attended = add_out_bias(jnp.dot(mixed_low, out_low, preferred_element_type=jnp.float32), params)
    piece_collection = pieces(params)
    section_one = tokens_low.astype(jnp.float32) + norm_rows(
        attended, piece_collection[0], piece_collection[1]
    )
    section_low = section_one.astype(jnp.bfloat16)
    logits = jnp.dot(section_low, route_low, preferred_element_type=jnp.float32)
    chosen_mask = (
        route_ids[:, None] == jnp.arange(logits.shape[1], dtype=jnp.int32)[None, :]
    ).astype(jnp.float32)
    gating = jax.nn.sigmoid(jnp.sum(logits * chosen_mask, axis=1))
    kept = (
        projected,
        q_low,
        k_low,
        v_low,
        cosine,
        probs_low,
        mixed_low,
        attended,
        section_low,
        logits,
        chosen_mask,
    )
    return (section_one, gating, section_low, kept)


def front_backward_split(tokens_low, weights_low, params, kept, grad_section, grad_gate, grad_feed):
    (
        projected,
        q_low,
        k_low,
        v_low,
        cosine,
        probs_low,
        mixed_low,
        attended,
        section_low,
        logits,
        chosen_mask,
    ) = kept
    rows_here = tokens_low.shape[0]
    window_count = rows_here // WIN
    qkv_low = weights_low[:, : 3 * MODEL_WIDTH]
    out_low = weights_low[:, 3 * MODEL_WIDTH : 4 * MODEL_WIDTH]
    route_low = weights_low[:, 4 * MODEL_WIDTH :]

    def gate_part(logit_values):
        return jax.nn.sigmoid(jnp.sum(logit_values * chosen_mask, axis=1))

    gate_back = jax.vjp(gate_part, logits)[1]
    grad_logits = gate_back(grad_gate)[0].astype(jnp.bfloat16)
    grad_from_route, grad_route = matmul_back(section_low, route_low, grad_logits)
    grad_total = grad_section + grad_feed + grad_from_route

    def section_part(attended_value, params_value):
        piece_collection = pieces(params_value)
        return norm_rows(attended_value, piece_collection[0], piece_collection[1])

    section_back = jax.vjp(section_part, attended, params)[1]
    grad_attended, grad_params_a = section_back(grad_total)
    grad_att_low = grad_attended.astype(jnp.bfloat16)
    grad_params_b = jax.vjp(add_out_bias, jnp.zeros_like(attended), params)[1](
        grad_att_low.astype(jnp.float32)
    )[1]
    grad_mixed, grad_out = matmul_back(mixed_low, out_low, grad_att_low)
    grad_mixed_low = grad_mixed.astype(jnp.bfloat16).reshape(
        window_count, WIN, ATTENTION_HEADS, HEAD_DIM
    )
    grad_probs = jnp.einsum(
        "wihd,wjhd->whij", grad_mixed_low, v_low, preferred_element_type=jnp.float32
    )
    grad_v = jnp.einsum(
        "whij,wihd->wjhd", probs_low, grad_mixed_low, preferred_element_type=jnp.float32
    )
    soft_back = jax.vjp(softmax_part, cosine, params)[1]
    grad_cosine, grad_params_c = soft_back(grad_probs)
    grad_cos_low = grad_cosine.astype(jnp.bfloat16)
    grad_q = jnp.einsum("whij,wjhd->wihd", grad_cos_low, k_low, preferred_element_type=jnp.float32)
    grad_k = jnp.einsum("whij,wihd->wjhd", grad_cos_low, q_low, preferred_element_type=jnp.float32)
    norm_back = jax.vjp(normalize_heads, projected)[1]
    grad_projected = norm_back((grad_q, grad_k, grad_v))[0]
    grad_proj_low = grad_projected.astype(jnp.bfloat16)
    grad_params_d = jax.vjp(add_joined_bias, jnp.zeros_like(projected), params)[1](
        grad_proj_low.astype(jnp.float32)
    )[1]
    grad_tokens, grad_qkv = matmul_back(tokens_low, qkv_low, grad_proj_low)
    grad_inputs = grad_total + grad_tokens
    grad_weights = jnp.concatenate([grad_qkv, grad_out, grad_route], axis=1)
    grad_params = grad_params_a + grad_params_b + grad_params_c + grad_params_d
    return (grad_inputs, grad_weights, grad_params)


def finish_block(section_one, gating, combined, kept_rows, live_rows, small_params):
    piece_collection = pieces(small_params)
    branch = (
        norm_rows(combined, piece_collection[2], piece_collection[3])
        * (gating * kept_rows)[:, None]
    )
    return (section_one + branch) * live_rows[:, None]


def assign(route_ids, count, experts, capacity):
    places = jnp.arange(route_ids.shape[0], dtype=jnp.int32)
    live_rows = places // IMG_TOK < count
    chosen = (
        (route_ids[:, None] == jnp.arange(experts, dtype=jnp.int32)[None, :]) & live_rows[:, None]
    ).astype(jnp.int32)
    before = jnp.cumsum(chosen, axis=0) - chosen
    slot = jnp.sum(before * chosen, axis=1)
    kept_rows = live_rows & (slot < capacity)
    dest_slot = jnp.where(kept_rows, route_ids * capacity + slot, experts * capacity)
    return (live_rows, kept_rows, dest_slot)


def adamw_step(weight, gradient, first, second, rate, decay):
    first_new = beta_one * first + (1.0 - beta_one) * gradient
    second_new = beta_two * second + (1.0 - beta_two) * gradient * gradient
    first_hat = first_new / (1.0 - beta_one**STEP)
    second_hat = second_new / (1.0 - beta_two**STEP)
    weight_new = weight - rate * (first_hat / (jnp.sqrt(second_hat) + epsilon) + decay * weight)
    return (weight_new, first_new, second_new)


def trade_rows(payload):
    arrived_rows = lax.all_to_all(
        payload, ("wide", "narrow"), split_axis=0, concat_axis=0, tiled=True
    )
    return arrived_rows


def axis_bits(axis):
    size = lax.axis_size(axis)
    return [(axis, 1 << k) for k in range(size.bit_length() - 1)]


def swap(value, step):
    axis, offset = step
    return lax.ppermute(value, axis, [(i, i ^ offset) for i in range(lax.axis_size(axis))])


def upper(step):
    axis, offset = step
    return (lax.axis_index(axis) & offset) > 0


def gather_rows(share):
    steps = axis_bits("narrow") + axis_bits("wide")
    first, rest = steps[0], steps[1:]
    other = swap(share, first)
    block = jnp.where(
        upper(first), jnp.concatenate([other, share]), jnp.concatenate([share, other])
    )
    held = block
    done = []
    core = ("wide", 1)
    for step in [s for s in rest if s != core] + [core]:
        place = sum(1 for d in done if rest.index(d) > rest.index(step))
        other = swap(held, step)
        held = jnp.where(
            upper(step), jnp.stack([other, held], place), jnp.stack([held, other], place)
        )
        done.append(step)
    return held.reshape(-1, share.shape[1])


def sum_grads(partial, small):
    steps = axis_bits("narrow") + axis_bits("wide")
    first, rest = steps[0], steps[1:]
    core = ("wide", 1)
    order = [core] + [s for s in rest[::-1] if s != core]
    count = lax.axis_size(("wide", "narrow"))
    share = partial.shape[0] // count
    held = partial.reshape((2,) * len(rest) + (2 * share, partial.shape[1]))
    left = rest[::-1]
    for step in order:
        place = left.index(step)
        side = upper(step).astype(jnp.int32)
        send = lax.dynamic_index_in_dim(held, 1 - side, place, keepdims=False)
        keep = lax.dynamic_index_in_dim(held, side, place, keepdims=False)
        other = swap(send.astype(jnp.bfloat16), step)
        small = small + swap(small, step)
        held = keep + other.astype(jnp.float32)
        left = [s for s in left if s != step]
    side = upper(first)
    send = jnp.where(side, held[:share], held[share:])
    keep = jnp.where(side, held[share:], held[:share])
    other = swap(send.astype(jnp.bfloat16), first)
    small = small + swap(small, first)
    return keep + other.astype(jnp.float32), small


def join(held, step, axis=None):
    other = swap(held, step)
    if axis is None or axis >= 0:
        both = functools.partial(jnp.stack, axis=axis or 0)
    else:
        both = functools.partial(jnp.concatenate, axis=axis)
    return jnp.where(upper(step), both([other, held]), both([held, other]))


def sum_quads(small, steps):
    axis, low = steps[0]
    high = steps[1][1]
    near = small + swap(small, (axis, low))
    return near + (swap(small, (axis, high)) + swap(small, (axis, high + low)))


def sum_chip(send, keep):
    return (keep + swap(send, ("wide", 1)).astype(jnp.float32)).astype(jnp.bfloat16)


def sum_shares(held):
    wide, narrow = lax.axis_size("wide"), lax.axis_size("narrow")
    groups = [
        [w * narrow + n for w in range(core, wide, 2) for n in range(narrow)] for core in range(2)
    ]
    arrived = lax.all_to_all(held, ("wide", "narrow"), 0, 0, axis_index_groups=groups, tiled=True)
    return jnp.sum(arrived.astype(jnp.float32), axis=0)


def lane_masks(dtype):
    lane = lax.broadcasted_iota(jnp.int32, (1, GROUP_LANES), 1) // HEAD_DIM
    return [(lane == h).astype(jnp.float32).astype(dtype) for h in range(GROUP)]


def dot(left, right):
    return jnp.dot(left, right, preferred_element_type=jnp.float32)


def dot_cols(left, right):
    return lax.dot_general(left, right, contract_cols, preferred_element_type=jnp.float32)


def dot_rows(left, right):
    return lax.dot_general(left, right, contract_rows, preferred_element_type=jnp.float32)


def stack_heads(rows, masks):
    return jnp.concatenate([rows * m for m in masks], axis=0)


def pick_heads(blocks, masks):
    n = blocks.shape[0] // GROUP
    return sum(blocks[n * h : n * h + n] * masks[h] for h in range(GROUP))


def head_sums(values):
    row = lax.broadcasted_iota(jnp.int32, (2 * GROUP_LANES, GROUP_LANES), 0) % GROUP_LANES
    col = lax.broadcasted_iota(jnp.int32, (2 * GROUP_LANES, GROUP_LANES), 1)
    ones = (row // HEAD_DIM == col // HEAD_DIM).astype(jnp.float32).astype(jnp.bfloat16)
    high = values.astype(jnp.bfloat16)
    rest = (values - high.astype(jnp.float32)).astype(jnp.bfloat16)
    sums = []
    for start in range(0, values.shape[1], GROUP_LANES):
        cut = slice(start, start + GROUP_LANES)
        sums.append(dot(jnp.concatenate([high[:, cut], rest[:, cut]], axis=1), ones))
    return jnp.concatenate(sums, axis=1)


def send_rows(dest_row, rows, out_ref):
    total = out_ref.shape[0]
    block = math.gcd(total, 256)
    for start in range(0, total, block):
        slot = lax.broadcasted_iota(jnp.int32, (block, rows.shape[0]), 0) + start
        chosen = jnp.where(slot == dest_row, 1.0, 0.0).astype(jnp.bfloat16)
        out_ref[pl.ds(start, block), :] = dot(chosen, rows).astype(jnp.bfloat16)


def gelu_pair(pre):
    inner = math.sqrt(2.0 / math.pi)
    square = pre * pre
    bend = jnp.tanh(pre * (inner + (inner * 0.044715) * square))
    half = 0.5 + 0.5 * bend
    slope = half + pre * (half * (1.0 - bend)) * (inner + (3.0 * inner * 0.044715) * square)
    return pre * half, slope


def take_rows(dest_row, rows):
    count, total = dest_row.shape[1], rows.shape[0]
    places = jnp.broadcast_to(dest_row.astype(jnp.float32), (GROUP_LANES, count)).T
    lane = lax.broadcasted_iota(jnp.int32, (count, GROUP_LANES), 1).astype(jnp.float32)
    chosen = jnp.concatenate(
        [
            jnp.where(places == lane + float(start), 1.0, 0.0).astype(jnp.bfloat16)
            for start in range(0, total, GROUP_LANES)
        ],
        axis=1,
    )
    return dot(chosen, rows)


def assign_kernel(capacity, count_ref, route_ref, cot_ref, dest_ref, out_ref):
    tokens = route_ref.shape[1]
    total = out_ref.shape[0]
    span = GROUP_LANES
    live_end = count_ref[0] * IMG_TOK
    first = lax.broadcasted_iota(jnp.int32, (span, span), 0)
    second = lax.broadcasted_iota(jnp.int32, (span, span), 1)
    earlier = jnp.where(first < second, 1.0, 0.0).astype(jnp.bfloat16)
    whole = jnp.ones((span, span), jnp.bfloat16)
    carry = jnp.zeros((EXPERTS, span), jnp.float32)
    for start in range(0, tokens, span):
        route = route_ref[:, start : start + span]
        place = lax.broadcasted_iota(jnp.int32, (1, span), 1) + start
        expert = lax.broadcasted_iota(jnp.int32, (EXPERTS, span), 0)
        chosen = jnp.where((expert == route) & (place < live_end), 1.0, 0.0)
        low = chosen.astype(jnp.bfloat16)
        before = dot(low, earlier) + carry
        carry = carry + dot(low, whole)
        slot = jnp.sum(before * chosen, axis=0, keepdims=True).astype(jnp.int32)
        keep = (place < live_end) & (slot < capacity)
        dest_ref[:, start : start + span] = jnp.where(keep, route * capacity + slot, total)
    send_rows(dest_ref[...], cot_ref[...], out_ref)


def call_assign(images, routes, cotangent, capacity):
    tokens = routes.shape[0]
    total = EXPERTS * capacity
    return pl.pallas_call(
        functools.partial(assign_kernel, capacity),
        out_shape=(
            jax.ShapeDtypeStruct((1, tokens), jnp.int32),
            jax.ShapeDtypeStruct((total, MODEL_WIDTH), jnp.bfloat16),
        ),
        in_specs=[
            pl.BlockSpec(memory_space=pltpu.SMEM),
            pl.BlockSpec(memory_space=pltpu.VMEM),
            pl.BlockSpec(memory_space=pltpu.VMEM),
        ],
        out_specs=(
            pl.BlockSpec(memory_space=pltpu.VMEM),
            pl.BlockSpec(memory_space=pltpu.VMEM),
        ),
        cost_estimate=pl.CostEstimate(
            flops=2 * total * tokens * MODEL_WIDTH, bytes_accessed=4 * 10**6, transcendentals=0
        ),
        compiler_params=pltpu.CompilerParams(vmem_limit_bytes=VMEM_BYTES),
        name="assign",
    )(images, routes.reshape(1, tokens), cotangent)


def front_kernel(
    dest_ref,
    tokens_ref,
    weight_ref,
    rows_ref,
    scale_ref,
    bias_ref,
    placed_ref,
    section_ref,
    attended_ref,
    mixed_ref,
    raw_ref,
    heads_ref,
    probs_ref,
    low_ref,
):
    step = pl.program_id(0)
    block = tokens_ref.shape[0]
    width = MODEL_WIDTH
    tokens = tokens_ref[...]
    masks_low = lane_masks(jnp.bfloat16)
    masks = lane_masks(jnp.float32)
    projected = dot(tokens, weight_ref[:, : 3 * width])
    queries = projected[:, :width] + rows_ref[4:5, :]
    keys = projected[:, width : 2 * width]
    values = projected[:, 2 * width :] + rows_ref[5:6, :]
    raw_ref[:, :width] = queries
    raw_ref[:, width:] = keys
    heads_ref[:, :width] = (queries * lax.rsqrt(head_sums(queries * queries) + 1e-06)).astype(
        jnp.bfloat16
    )
    heads_ref[:, width : 2 * width] = (
        keys * lax.rsqrt(head_sums(keys * keys) + 1e-06)
    ).astype(jnp.bfloat16)
    heads_ref[:, 2 * width :] = values.astype(jnp.bfloat16)
    for window in range(block // WIN):
        at = pl.ds(window * WIN, WIN)
        for group in range(width // GROUP_LANES):
            start = group * GROUP_LANES
            query = heads_ref[at, start : start + GROUP_LANES]
            key = heads_ref[at, width + start : width + start + GROUP_LANES]
            value = heads_ref[at, 2 * width + start : 2 * width + start + GROUP_LANES]
            cosine = dot_cols(key, stack_heads(query, masks_low))
            scores = cosine * scale_ref[group] + bias_ref[group]
            powers = jnp.exp(scores - jnp.max(scores, axis=0, keepdims=True))
            probs = powers * (1.0 / jnp.sum(powers, axis=0, keepdims=True))
            probs_ref[window, group] = probs
            mixed = pick_heads(dot_rows(probs.astype(jnp.bfloat16), value), masks)
            mixed_ref[at, start : start + GROUP_LANES] = mixed.astype(jnp.bfloat16)
    attended = dot(mixed_ref[...], weight_ref[:, 3 * width : 4 * width]) + rows_ref[6:7, :]
    attended_ref[...] = attended
    section = tokens.astype(jnp.float32) + norm_rows(attended, rows_ref[0:1, :], rows_ref[1:2, :])
    section_ref[...] = section
    low_ref[pl.ds(pl.multiple_of(step * block, block), block), :] = section.astype(jnp.bfloat16)

    @pl.when(step == pl.num_programs(0) - 1)
    def _():
        send_rows(dest_ref[...], low_ref[...], placed_ref)


def token_block(tok_rows):
    return math.gcd(tok_rows, 256)


def whole(shape):
    return pl.BlockSpec(shape, lambda i: (0,) * len(shape))


def by_rows(block, width):
    return pl.BlockSpec((block, width), lambda i: (i, 0))


def call_front(dest, tokens, gathered, rows, scale, bias, capacity):
    count, width = tokens.shape
    total = EXPERTS * capacity
    block = token_block(count)
    groups = width // GROUP_LANES
    probs_shape = (count // WIN, groups, WIN, GROUP * WIN)
    return pl.pallas_call(
        front_kernel,
        grid=(count // block,),
        out_shape=(
            jax.ShapeDtypeStruct((total, width), jnp.bfloat16),
            jax.ShapeDtypeStruct((count, width), jnp.float32),
            jax.ShapeDtypeStruct((count, width), jnp.float32),
            jax.ShapeDtypeStruct((count, width), jnp.bfloat16),
            jax.ShapeDtypeStruct((count, 2 * width), jnp.float32),
            jax.ShapeDtypeStruct((count, 3 * width), jnp.bfloat16),
            jax.ShapeDtypeStruct(probs_shape, jnp.float32),
        ),
        in_specs=[
            whole(dest.shape),
            by_rows(block, width),
            whole(gathered.shape),
            whole(rows.shape),
            whole(scale.shape),
            whole(bias.shape),
        ],
        out_specs=(
            whole((total, width)),
            by_rows(block, width),
            by_rows(block, width),
            by_rows(block, width),
            by_rows(block, 2 * width),
            by_rows(block, 3 * width),
            pl.BlockSpec((block // WIN,) + probs_shape[1:], lambda i: (i, 0, 0, 0)),
        ),
        scratch_shapes=[pltpu.VMEM((count, width), jnp.bfloat16)],
        cost_estimate=pl.CostEstimate(
            flops=2 * count * width * width * 8, bytes_accessed=20 * 10**6, transcendentals=0
        ),
        compiler_params=pltpu.CompilerParams(vmem_limit_bytes=VMEM_BYTES),
        name="front",
    )(dest, tokens, gathered, rows, scale, bias)


def back_kernel(
    narrow,
    count_ref,
    place_ref,
    dest_ref,
    arrived_ref,
    cot_ref,
    tokens_ref,
    weight_ref,
    rows_ref,
    scale_ref,
    attended_ref,
    mixed_ref,
    raw_ref,
    heads_ref,
    probs_ref,
    expert_ref,
    table_ref,
    coords_ref,
    net_ref,
    inputs_ref,
    send_ref,
    keep_ref,
    sums_ref,
    grad_bias_ref,
    grad_scale_ref,
    grad_heads,
    low_attended,
    low_projected,
):
    step = pl.program_id(0)
    block = cot_ref.shape[0]
    width = MODEL_WIDTH
    start_row = pl.multiple_of(step * block, block)
    here = pl.ds(start_row, block)
    masks_low = lane_masks(jnp.bfloat16)
    masks = lane_masks(jnp.float32)

    @pl.when(step == 0)
    def _():
        sums_ref[...] = jnp.zeros_like(sums_ref)
        grad_bias_ref[...] = jnp.zeros_like(grad_bias_ref)
        grad_scale_ref[...] = jnp.zeros_like(grad_scale_ref)

    place = lax.broadcasted_iota(jnp.int32, (block, 1), 0) + start_row
    live = jnp.where(place < count_ref[0] * IMG_TOK, 1.0, 0.0)
    feed = take_rows(dest_ref[...], arrived_ref[...])
    total = cot_ref[...].astype(jnp.float32) * live + feed
    attended = attended_ref[...]
    centred = attended - jnp.mean(attended, axis=-1, keepdims=True)
    spread = lax.rsqrt(jnp.mean(centred * centred, axis=-1, keepdims=True) + 1e-05)
    unit = centred * spread
    grad_unit = total * rows_ref[0:1, :]
    grad_attended = spread * (
        grad_unit
        - jnp.mean(grad_unit, axis=-1, keepdims=True)
        - unit * jnp.mean(grad_unit * unit, axis=-1, keepdims=True)
    )
    grad_low = grad_attended.astype(jnp.bfloat16)
    low_attended[here, :] = grad_low
    sums_ref[0:1, :width] += jnp.sum(total * unit, axis=0, keepdims=True)
    sums_ref[1:2, :width] += jnp.sum(total, axis=0, keepdims=True)
    sums_ref[6:7, :width] += jnp.sum(grad_low.astype(jnp.float32), axis=0, keepdims=True)
    grad_mixed = dot_cols(grad_low, weight_ref[:, 3 * width : 4 * width]).astype(jnp.bfloat16)
    for window in range(block // WIN):
        at = pl.ds(window * WIN, WIN)
        for group in range(width // GROUP_LANES):
            start = group * GROUP_LANES
            cut_q = slice(start, start + GROUP_LANES)
            cut_k = slice(width + start, width + start + GROUP_LANES)
            cut_v = slice(2 * width + start, 2 * width + start + GROUP_LANES)
            query = stack_heads(heads_ref[at, cut_q], masks_low)
            key = heads_ref[at, cut_k]
            value = heads_ref[at, cut_v]
            grad_out = stack_heads(grad_mixed[window * WIN : window * WIN + WIN, cut_q], masks_low)
            grad_probs = dot_cols(value, grad_out)
            cosine = dot_cols(key, query)
            probs = probs_ref[window, group]
            grad_heads[at, cut_v] = dot(probs.astype(jnp.bfloat16), grad_out)
            weighed = probs * grad_probs
            grad_scores = weighed - probs * jnp.sum(weighed, axis=0, keepdims=True)
            grad_bias_ref[group] += grad_scores
            grad_scale_ref[group] += jnp.sum(grad_scores * cosine, axis=0, keepdims=True)
            grad_cosine = (grad_scores * scale_ref[group]).astype(jnp.bfloat16)
            grad_heads[at, cut_k] = dot(grad_cosine, query)
            grad_heads[at, cut_q] = pick_heads(dot_rows(grad_cosine, key), masks)
    for side in range(2):
        cut = slice(side * width, side * width + width)
        raw = raw_ref[:, cut]
        inverse = lax.rsqrt(head_sums(raw * raw) + 1e-06)
        unit = raw * inverse
        grad = grad_heads[:, cut]
        low_projected[here, cut] = (inverse * (grad - unit * head_sums(grad * unit))).astype(
            jnp.bfloat16
        )
    low_projected[here, 2 * width :] = grad_heads[:, 2 * width :].astype(jnp.bfloat16)
    grad_projected = low_projected[here, :]
    sums_ref[4:5, :width] += jnp.sum(
        grad_projected[:, :width].astype(jnp.float32), axis=0, keepdims=True
    )
    sums_ref[5:6, :width] += jnp.sum(
        grad_projected[:, 2 * width :].astype(jnp.float32), axis=0, keepdims=True
    )
    inputs_ref[...] = (total + dot_cols(grad_projected, weight_ref[:, : 3 * width])).astype(
        jnp.bfloat16
    )

    @pl.when(step == pl.num_programs(0) - 1)
    def _():
        grad_qkv = dot_rows(tokens_ref[...], low_projected[...])
        grad_out = dot_rows(mixed_ref[...], low_attended[...])
        grad_dense = jnp.concatenate([grad_qkv, grad_out], axis=1)
        chips = keep_ref.shape[0]
        on_first = place_ref[0] == 0
        share = width // (2 * chips)
        for chip in range(chips):
            cuts = []
            for core in range(2):
                row = (chip // narrow * 2 * narrow + core * narrow + chip % narrow) * share
                rows = grad_dense[row : row + share]
                cuts.append(
                    jnp.concatenate([rows[:, : 2 * width], rows[:, 2 * width :]], axis=0)
                )
            keep_ref[chip] = jnp.where(on_first, cuts[0], cuts[1])
            send_ref[chip] = jnp.where(on_first, cuts[1], cuts[0]).astype(jnp.bfloat16)
        sums_ref[2:4, :width] = expert_ref[1:3, :]
        row = lax.broadcasted_iota(jnp.int32, (EXPERTS, width), 0)
        sums_ref[ROUTE_ROWS:, :width] = jnp.where(row == place_ref[1], expert_ref[3:4, :], 0.0)
        for group in range(grad_scale_ref.shape[0]):
            at = SCALE_ROWS + group
            sums_ref[at : at + 1, : GROUP * WIN] = grad_scale_ref[group]
        net_back(
            sum_offsets(grad_bias_ref), table_ref[...], coords_ref[...], net_ref, sums_ref
        )


def sum_offsets(grad_bias_ref):
    row = lax.broadcasted_iota(jnp.int32, (GROUP * WIN, TABLE), 0)
    lane = lax.broadcasted_iota(jnp.int32, (GROUP * WIN, TABLE), 1)
    query = row % WIN
    aim = TABLE_MID - STRIDE * (query // SIDE) - query % SIDE
    spreads = [
        jnp.where((lane == aim) & (row // WIN == h), 1.0, 0.0).astype(jnp.bfloat16)
        for h in range(GROUP)
    ]
    sums = []
    for group in range(grad_bias_ref.shape[0]):
        grad = grad_bias_ref[group]
        high = grad.astype(jnp.bfloat16)
        rest = grad - high.astype(jnp.float32)
        middle = rest.astype(jnp.bfloat16)
        last = (rest - middle.astype(jnp.float32)).astype(jnp.bfloat16)
        parts = jnp.concatenate([high, middle, last], axis=0)
        for h in range(GROUP):
            spread = dot(parts, spreads[h])
            spread = spread[:WIN] + spread[WIN : 2 * WIN] + spread[2 * WIN :]
            rows = spread[:SIDE]
            for r in range(1, SIDE):
                rows = rows + pltpu.roll(spread[SIDE * r : SIDE * r + SIDE], STRIDE * r, 1)
            rows = pltpu.roll(rows, 0, 1, stride=1, stride_axis=0)
            sums.append(jnp.sum(rows, axis=0, keepdims=True))
    return jnp.concatenate(sums, axis=0)


def net_back(grad, table, coords, net_ref, sums_ref):
    heads = table.shape[0]
    second, shift, first = net_ref[:heads], net_ref[heads : heads + 1], net_ref[heads + 1 : heads + 3]
    pre = coords[:, 0:1] * first[0:1] + coords[:, 1:2] * first[1:2] + shift
    hidden, slope = gelu_pair(pre)
    grad_logits = grad * table * (1.0 - table * (1.0 / 16.0))
    sums_ref[SECOND_ROWS : SECOND_ROWS + heads, :] = jnp.dot(
        grad_logits, hidden, precision=highest, preferred_element_type=jnp.float32
    )
    grad_pre = slope * lax.dot_general(
        grad_logits, second, contract_rows, precision=highest, preferred_element_type=jnp.float32
    )
    sums_ref[SHIFT_ROW : SHIFT_ROW + 1, :] = jnp.sum(grad_pre, axis=0, keepdims=True)
    for k in range(2):
        sums_ref[FIRST_ROWS + k : FIRST_ROWS + k + 1, :] = jnp.sum(
            grad_pre * coords[:, k : k + 1], axis=0, keepdims=True
        )


def call_back(
    images, dest, arrived, cotangent, tokens, gathered, rows, scale, attended, mixed, raw, heads, probs, sums_expert, table, net
):
    count, width = tokens.shape
    narrow = lax.axis_size("narrow")
    chips = narrow * lax.axis_size("wide") // 2
    share = width // (2 * chips)
    coords = jnp.asarray(offset_coords())
    place = jnp.stack([lax.axis_index("wide") % 2, lax.axis_index(("wide", "narrow"))])
    block = token_block(count)
    groups = width // GROUP_LANES
    return pl.pallas_call(
        functools.partial(back_kernel, narrow),
        grid=(count // block,),
        out_shape=(
            jax.ShapeDtypeStruct((count, width), jnp.bfloat16),
            jax.ShapeDtypeStruct((chips, 2 * share, 2 * width), jnp.bfloat16),
            jax.ShapeDtypeStruct((chips, 2 * share, 2 * width), jnp.float32),
            jax.ShapeDtypeStruct((ROUTE_ROWS + EXPERTS, SUM_LANES), jnp.float32),
        ),
        in_specs=[
            pl.BlockSpec(memory_space=pltpu.SMEM),
            pl.BlockSpec(memory_space=pltpu.SMEM),
            pl.BlockSpec((1, block), lambda i: (0, i)),
            whole(arrived.shape),
            by_rows(block, width),
            whole(tokens.shape),
            whole(gathered.shape),
            whole(rows.shape),
            whole(scale.shape),
            by_rows(block, width),
            whole(mixed.shape),
            by_rows(block, 2 * width),
            by_rows(block, 3 * width),
            pl.BlockSpec((block // WIN,) + probs.shape[1:], lambda i: (i, 0, 0, 0)),
            whole(sums_expert.shape),
            whole(table.shape),
            whole(coords.shape),
            whole(net.shape),
        ],
        out_specs=(
            by_rows(block, width),
            whole((chips, 2 * share, 2 * width)),
            whole((chips, 2 * share, 2 * width)),
            whole((ROUTE_ROWS + EXPERTS, SUM_LANES)),
        ),
        scratch_shapes=[
            pltpu.VMEM((groups, WIN, GROUP * WIN), jnp.float32),
            pltpu.VMEM((groups, 1, GROUP * WIN), jnp.float32),
            pltpu.VMEM((block, 3 * width), jnp.float32),
            pltpu.VMEM((count, width), jnp.bfloat16),
            pltpu.VMEM((count, 3 * width), jnp.bfloat16),
        ],
        cost_estimate=pl.CostEstimate(
            flops=2 * count * width * width * 16, bytes_accessed=20 * 10**6, transcendentals=0
        ),
        compiler_params=pltpu.CompilerParams(vmem_limit_bytes=VMEM_BYTES),
        name="back",
    )(
        images,
        place.astype(jnp.int32),
        dest,
        arrived,
        cotangent,
        tokens,
        gathered,
        rows,
        scale,
        attended,
        mixed,
        raw,
        heads,
        probs,
        sums_expert,
        table,
        coords,
        net,
    )


def layer_kernel(count_ref, dest_ref, branch_ref, section_ref, out_ref):
    block = out_ref.shape[0]
    place = lax.broadcasted_iota(jnp.int32, (block, 1), 0) + pl.program_id(0) * block
    live = jnp.where(place < count_ref[0] * IMG_TOK, 1.0, 0.0)
    branch = take_rows(dest_ref[...], branch_ref[...])
    out_ref[...] = ((section_ref[...] + branch) * live).astype(jnp.bfloat16)


def call_layer(images, dest, branch, section):
    count, width = section.shape
    block = token_block(count)
    return pl.pallas_call(
        layer_kernel,
        grid=(count // block,),
        out_shape=jax.ShapeDtypeStruct((count, width), jnp.bfloat16),
        in_specs=[
            pl.BlockSpec(memory_space=pltpu.SMEM),
            pl.BlockSpec((1, block), lambda i: (0, i)),
            whole(branch.shape),
            by_rows(block, width),
        ],
        out_specs=by_rows(block, width),
        cost_estimate=pl.CostEstimate(
            flops=2 * count * width * branch.shape[0], bytes_accessed=4 * 10**6, transcendentals=0
        ),
        compiler_params=pltpu.CompilerParams(vmem_limit_bytes=VMEM_BYTES),
        name="layer",
    )(images, dest, branch, section)


def expert_kernel(
    rows_ref,
    cot_ref,
    first_ref,
    second_ref,
    bias_one_ref,
    vecs_ref,
    branch_ref,
    back_ref,
    hidden_ref,
    grad_pre_ref,
    grad_result_ref,
    sums_ref,
    sum_pre_ref,
):
    @pl.when(pl.program_id(0) == 0)
    def _():
        sums_ref[...] = jnp.zeros_like(sums_ref)
        sum_pre_ref[...] = jnp.zeros_like(sum_pre_ref)

    low = rows_ref[...]
    rows = low.astype(jnp.float32)
    bias_two, gain, shift, route = (vecs_ref[i : i + 1, :] for i in range(4))
    hidden, slope = gelu_pair(dot(low, first_ref[...]) + bias_one_ref[...])
    hidden = hidden.astype(jnp.bfloat16)
    hidden_ref[...] = hidden
    result = (dot(hidden, second_ref[...]) + bias_two).astype(jnp.bfloat16).astype(jnp.float32)
    gating = jax.nn.sigmoid(jnp.sum(rows * route, axis=-1, keepdims=True))
    centred = result - jnp.mean(result, axis=-1, keepdims=True)
    spread = lax.rsqrt(jnp.mean(centred * centred, axis=-1, keepdims=True) + 1e-05)
    unit = centred * spread
    normed = unit * gain + shift
    branch_ref[...] = (normed * gating).astype(jnp.bfloat16)
    cot = cot_ref[...].astype(jnp.float32)
    grad_gate = jnp.sum(cot * normed, axis=-1, keepdims=True)
    gated = cot * gating
    grad_unit = gated * gain
    grad_result = (
        spread
        * (
            grad_unit
            - jnp.mean(grad_unit, axis=-1, keepdims=True)
            - unit * jnp.mean(grad_unit * unit, axis=-1, keepdims=True)
        )
    ).astype(jnp.bfloat16)
    grad_result_ref[...] = grad_result
    grad_logit = (
        (grad_gate * gating * (1.0 - gating)).astype(jnp.bfloat16).astype(jnp.float32)
    )
    sums_ref[0:1, :] += jnp.sum(grad_result.astype(jnp.float32), axis=0, keepdims=True)
    sums_ref[1:2, :] += jnp.sum(gated * unit, axis=0, keepdims=True)
    sums_ref[2:3, :] += jnp.sum(gated, axis=0, keepdims=True)
    sums_ref[3:4, :] += jnp.sum(rows * grad_logit, axis=0, keepdims=True)
    grad_pre = (dot_cols(grad_result, second_ref[...]) * slope).astype(jnp.bfloat16)
    grad_pre_ref[...] = grad_pre
    sum_pre_ref[...] += jnp.sum(grad_pre.astype(jnp.float32), axis=0, keepdims=True)
    back_ref[...] = (dot_cols(grad_pre, first_ref[...]) + grad_logit * route).astype(jnp.bfloat16)


def call_expert(rows, cot, first, second, bias_one, vecs):
    count, width = rows.shape
    ff = first.shape[1]
    block = math.gcd(count, 256)
    return pl.pallas_call(
        expert_kernel,
        grid=(count // block,),
        out_shape=(
            jax.ShapeDtypeStruct((count, width), jnp.bfloat16),
            jax.ShapeDtypeStruct((count, width), jnp.bfloat16),
            jax.ShapeDtypeStruct((count, ff), jnp.bfloat16),
            jax.ShapeDtypeStruct((count, ff), jnp.bfloat16),
            jax.ShapeDtypeStruct((count, width), jnp.bfloat16),
            jax.ShapeDtypeStruct((8, width), jnp.float32),
            jax.ShapeDtypeStruct((1, ff), jnp.float32),
        ),
        in_specs=[
            by_rows(block, width),
            by_rows(block, width),
            whole(first.shape),
            whole(second.shape),
            whole(bias_one.shape),
            whole(vecs.shape),
        ],
        out_specs=(
            by_rows(block, width),
            by_rows(block, width),
            by_rows(block, ff),
            by_rows(block, ff),
            by_rows(block, width),
            whole((8, width)),
            whole((1, ff)),
        ),
        cost_estimate=pl.CostEstimate(
            flops=8 * count * width * ff, bytes_accessed=16 * 10**6, transcendentals=count * ff
        ),
        compiler_params=pltpu.CompilerParams(vmem_limit_bytes=VMEM_BYTES),
        name="expert",
    )(rows, cot, first, second, bias_one, vecs)


def offset_coords():
    place = TABLE_MID - np.arange(TABLE)
    row = (place + STRIDE // 2 - 1) // STRIDE
    coords = np.stack([row, place - STRIDE * row], axis=1) * (8.0 / (SIDE - 1))
    return (np.sign(coords) * np.log2(np.abs(coords) + 1.0) / 3.0).astype(np.float32)


def bias_table(params):
    piece_collection = pieces(params)
    hidden = jax.nn.gelu(
        jnp.dot(offset_coords(), piece_collection[9], precision=highest) + piece_collection[8]
    )
    return 16.0 * jax.nn.sigmoid(jnp.dot(hidden, piece_collection[10], precision=highest)).T


def spread_bias(table):
    places = jnp.arange(WIN, dtype=jnp.int32)
    coded = STRIDE * (places // SIDE) + places % SIDE
    index = TABLE_MID + coded[:, None] - coded[None, :]
    lookup = (index.reshape(1, -1) == jnp.arange(TABLE, dtype=jnp.int32)[:, None]).astype(
        table.dtype
    )
    bias = jnp.dot(table, lookup, precision=highest).reshape(-1, GROUP, WIN, WIN)
    return bias.transpose(0, 2, 1, 3).reshape(-1, WIN, GROUP * WIN)


def per_device_split(
    tokens,
    cotangent,
    routes,
    images,
    dense_weight,
    dense_moment,
    dense_square,
    small_params,
    small_moment,
    small_square,
    inner_weight,
    inner_moment,
    inner_square,
    outer_weight,
    outer_moment,
    outer_square,
    expert_bias,
    bias_moment,
    bias_square,
):
    slices = lax.axis_size(("wide", "narrow"))
    split = slices // EXPERTS
    member = lax.axis_index(("wide", "narrow")) % split
    piece = MODEL_WIDTH // split
    ff_dev = inner_weight.shape[2]
    tok_rows = tokens.shape[0]
    capacity = (5 * tok_rows + 4 * EXPERTS - 1) // (4 * EXPERTS)
    slot_total = EXPERTS * capacity
    route_ids = routes[:, 0]
    live_rows, kept_rows, dest_slot = assign(route_ids, images[0], EXPERTS, capacity)
    live_f = live_rows.astype(jnp.float32)
    keep_f = kept_rows.astype(jnp.float32)
    clipped = jnp.minimum(dest_slot, slot_total - 1)
    gathered = gather_rows(dense_weight.astype(jnp.bfloat16))
    section_one, gating, expert_feed, kept = front_forward_split(
        tokens, gathered, small_params, route_ids
    )

    def fan_out(rows_value):
        placed_rows = (
            jnp.zeros((slot_total, MODEL_WIDTH), jnp.bfloat16)
            .at[dest_slot]
            .set(rows_value.astype(jnp.bfloat16), mode="drop")
        )
        copies = jnp.broadcast_to(
            placed_rows.reshape(EXPERTS, 1, capacity, MODEL_WIDTH),
            (EXPERTS, split, capacity, MODEL_WIDTH),
        )
        return trade_rows(copies.reshape(slices, capacity, MODEL_WIDTH)).reshape(
            slices * capacity, MODEL_WIDTH
        )

    def fan_in(partials):
        arrived = trade_rows(partials.reshape(slices, capacity, MODEL_WIDTH))
        summed = jnp.sum(
            arrived.reshape(EXPERTS, split, capacity, MODEL_WIDTH).astype(jnp.float32), axis=1
        ).reshape(slot_total, MODEL_WIDTH)
        return jnp.take(summed, clipped, axis=0) * keep_f[:, None]

    expert_rows = fan_out(expert_feed)
    first_matrix = inner_weight[0].astype(jnp.bfloat16)
    second_matrix = outer_weight[0].astype(jnp.bfloat16)
    pre_act = (
        jnp.dot(expert_rows, first_matrix, preferred_element_type=jnp.float32)
        + expert_bias[0, :ff_dev]
    )
    hidden = jax.nn.gelu(pre_act).astype(jnp.bfloat16)
    out_bias = lax.dynamic_update_slice(
        jnp.zeros((MODEL_WIDTH,), jnp.float32), expert_bias[0, ff_dev:], (member * piece,)
    )
    result = (jnp.dot(hidden, second_matrix, preferred_element_type=jnp.float32) + out_bias).astype(
        jnp.bfloat16
    )
    combined = fan_in(result)

    def tail_local(section_value, gate_value, combined_value, params):
        return finish_block(section_value, gate_value, combined_value, keep_f, live_f, params)

    layer_value, tail_back = jax.vjp(tail_local, section_one, gating, combined, small_params)
    grad_section, grad_gate, grad_combined, grad_small_tail = tail_back(
        cotangent.astype(jnp.float32)
    )
    grad_result = fan_out(grad_combined)
    grad_outer = lax.dot_general(
        hidden, grad_result, contract_rows, preferred_element_type=jnp.float32
    )
    grad_hidden = lax.dot_general(
        grad_result, second_matrix, contract_cols, preferred_element_type=jnp.float32
    )
    gelu_back = jax.vjp(jax.nn.gelu, pre_act)[1]
    grad_pre = gelu_back(grad_hidden)[0].astype(jnp.bfloat16)
    grad_inner = lax.dot_general(
        expert_rows, grad_pre, contract_rows, preferred_element_type=jnp.float32
    )
    column_total = jnp.sum(grad_result.astype(jnp.float32), axis=0)
    grad_bias = jnp.concatenate(
        [
            jnp.sum(grad_pre.astype(jnp.float32), axis=0),
            lax.dynamic_slice_in_dim(column_total, member * piece, piece, 0),
        ]
    )
    grad_rows = lax.dot_general(
        grad_pre, first_matrix, contract_cols, preferred_element_type=jnp.float32
    ).astype(jnp.bfloat16)
    grad_feed = fan_in(grad_rows)
    grad_inputs, grad_weights, grad_small_front = front_backward_split(
        tokens, gathered, small_params, kept, grad_section, grad_gate, grad_feed
    )
    grad_small = grad_small_front + grad_small_tail
    grad_dense, grad_small = sum_grads(grad_weights, grad_small)
    dense_out = adamw_step(
        dense_weight, grad_dense, dense_moment, dense_square, dense_rate, weight_decay
    )
    small_out = adamw_step(small_params, grad_small, small_moment, small_square, small_rate, 0.0)
    inner_out = adamw_step(
        inner_weight, grad_inner[None], inner_moment, inner_square, expert_rate, weight_decay
    )
    outer_out = adamw_step(
        outer_weight, grad_outer[None], outer_moment, outer_square, expert_rate, weight_decay
    )
    bias_out = adamw_step(expert_bias, grad_bias[None], bias_moment, bias_square, expert_rate, 0.0)
    return (
        layer_value.astype(jnp.bfloat16),
        grad_inputs.astype(jnp.bfloat16),
        dense_out[0],
        dense_out[1],
        dense_out[2],
        small_out[0],
        small_out[1],
        small_out[2],
        inner_out[0],
        inner_out[1],
        inner_out[2],
        inner_out[0].astype(jnp.bfloat16),
        outer_out[0],
        outer_out[1],
        outer_out[2],
        outer_out[0].astype(jnp.bfloat16),
        bias_out[0],
        bias_out[1],
        bias_out[2],
    )


def per_device(
    tokens,
    cotangent,
    routes,
    images,
    dense_weight,
    dense_moment,
    dense_square,
    small_params,
    small_moment,
    small_square,
    inner_weight,
    inner_moment,
    inner_square,
    outer_weight,
    outer_moment,
    outer_square,
    expert_bias,
    bias_moment,
    bias_square,
):
    slices = lax.axis_size(("wide", "narrow"))
    if slices != EXPERTS:
        return per_device_split(
            tokens,
            cotangent,
            routes,
            images,
            dense_weight,
            dense_moment,
            dense_square,
            small_params,
            small_moment,
            small_square,
            inner_weight,
            inner_moment,
            inner_square,
            outer_weight,
            outer_moment,
            outer_square,
            expert_bias,
            bias_moment,
            bias_square,
        )
    expert = lax.axis_index(("wide", "narrow"))
    ff_dev = inner_weight.shape[2]
    tok_rows = tokens.shape[0]
    capacity = (5 * tok_rows + 4 * EXPERTS - 1) // (4 * EXPERTS)
    slot_total = EXPERTS * capacity

    def trade(rows):
        traded = trade_rows(rows.reshape(slices, capacity, MODEL_WIDTH))
        return traded.reshape(slot_total, MODEL_WIDTH)

    scale_at = 7 * MODEL_WIDTH
    share = dense_weight.astype(jnp.bfloat16)
    (pair, depth), across = axis_bits("narrow")[1:], axis_bits("narrow")[0]
    held = join(share, pair)
    held, params = lax.optimization_barrier((held, small_params))
    table = bias_table(params)
    net_pieces = pieces(params)
    net = jnp.concatenate([net_pieces[10].T, net_pieces[8][None, :], net_pieces[9]])
    vectors = params[:scale_at].reshape(7, MODEL_WIDTH)
    scale_heads = jnp.exp(params[scale_at : scale_at + ATTENTION_HEADS])
    scale = jnp.repeat(scale_heads, WIN).reshape(-1, 1, GROUP * WIN)
    held = join(held, depth)
    held, table, vectors, scale, route_ids, cot = lax.optimization_barrier(
        (held, table, vectors, scale, routes, cotangent)
    )
    dest, placed_cot = call_assign(images, route_ids, cot, capacity)
    held = join(held, across, -2)
    held, table, placed_cot, dest = lax.optimization_barrier((held, table, placed_cot, dest))
    bias = spread_bias(table)
    core, *rest = axis_bits("wide")
    for step in rest:
        held = join(held, step)
    held, bias = lax.optimization_barrier((held, bias))
    gathered = join(held, core, len(rest)).reshape(-1, held.shape[-1])
    gathered, placed_cot = lax.optimization_barrier((gathered, placed_cot))
    cot_rows = trade(placed_cot)
    placed, section, attended, mixed, raw, heads, probs = call_front(
        dest, tokens, gathered, vectors, scale, bias, capacity
    )
    placed, cot_rows = lax.optimization_barrier((placed, cot_rows))
    expert_rows = trade(placed)
    first_matrix = inner_weight[0].astype(jnp.bfloat16)
    second_matrix = outer_weight[0].astype(jnp.bfloat16)
    route_row = lax.dynamic_slice_in_dim(gathered, 4 * MODEL_WIDTH + expert, 1, 1)
    vecs = jnp.concatenate(
        [expert_bias[:, ff_dev:], vectors[2:4], route_row.astype(jnp.float32).reshape(1, -1)]
    )
    branch, grad_rows, hidden, grad_pre, grad_result, sums_expert, sum_pre = call_expert(
        expert_rows, cot_rows, first_matrix, second_matrix, expert_bias[:, :ff_dev], vecs
    )
    arrived = trade(grad_rows)
    grad_outer = dot_rows(hidden, grad_result)
    grad_inner = dot_rows(expert_rows, grad_pre)
    grad_bias = jnp.concatenate([sum_pre, sums_expert[0:1]], axis=1)[0]
    inner_out = adamw_step(
        inner_weight, grad_inner[None], inner_moment, inner_square, expert_rate, weight_decay
    )
    outer_out = adamw_step(
        outer_weight, grad_outer[None], outer_moment, outer_square, expert_rate, weight_decay
    )
    inner_out += (inner_out[0].astype(jnp.bfloat16),)
    outer_out += (outer_out[0].astype(jnp.bfloat16),)
    branch, arrived, inner_out, outer_out = lax.optimization_barrier(
        (branch, arrived, inner_out, outer_out)
    )
    branch_rows = trade(branch)
    grad_inputs, send, keep, sums = call_back(
        images,
        dest,
        arrived,
        cotangent,
        tokens,
        gathered,
        vectors,
        scale,
        attended,
        mixed,
        raw,
        heads,
        probs,
        sums_expert,
        table,
        net,
    )
    held = sum_chip(send, keep)
    sums = sum_quads(sums, axis_bits("wide"))
    held, sums, branch_rows = lax.optimization_barrier((held, sums, branch_rows))
    grad_dense = sum_shares(held)
    layer_out = call_layer(images, dest, branch_rows, section)
    share_rows = dense_weight.shape[0]
    grad_dense = jnp.concatenate([grad_dense[:share_rows], grad_dense[share_rows:]], axis=1)
    sums = sum_quads(sums, axis_bits("narrow")[1:])
    sums = sums + swap(sums, across)
    grad_scale = sums[SCALE_ROWS : SCALE_ROWS + ATTENTION_HEADS // GROUP, : GROUP * WIN]
    grad_small = jnp.concatenate(
        [
            sums[:7, :MODEL_WIDTH].reshape(-1),
            jnp.sum(grad_scale.reshape(ATTENTION_HEADS, WIN), axis=1) * scale_heads,
            sums[SHIFT_ROW : FIRST_ROWS + 2].reshape(-1),
            sums[SECOND_ROWS : SECOND_ROWS + ATTENTION_HEADS].T.reshape(-1),
        ]
    )
    grad_route = lax.dynamic_slice_in_dim(
        sums[ROUTE_ROWS:, :MODEL_WIDTH], expert * share_rows, share_rows, 1
    ).T
    grad_dense = jnp.concatenate([grad_dense, grad_route], axis=1)
    dense_out = adamw_step(
        dense_weight, grad_dense, dense_moment, dense_square, dense_rate, weight_decay
    )
    small_out = adamw_step(small_params, grad_small, small_moment, small_square, small_rate, 0.0)
    bias_out = adamw_step(expert_bias, grad_bias[None], bias_moment, bias_square, expert_rate, 0.0)
    return (
        layer_out,
        grad_inputs,
        dense_out[0],
        dense_out[1],
        dense_out[2],
        small_out[0],
        small_out[1],
        small_out[2],
        inner_out[0],
        inner_out[1],
        inner_out[2],
        inner_out[3],
        outer_out[0],
        outer_out[1],
        outer_out[2],
        outer_out[3],
        bias_out[0],
        bias_out[1],
        bias_out[2],
    )


def solution(mesh):
    return jax.shard_map(
        per_device,
        mesh=mesh,
        in_specs=(
            P(("wide", "narrow"), None),
            P(("wide", "narrow"), None),
            P(("wide", "narrow"), None),
            P(("wide", "narrow")),
            P(("wide", "narrow"), None),
            P(("wide", "narrow"), None),
            P(("wide", "narrow"), None),
            P(),
            P(),
            P(),
            P(("wide", "narrow"), None, None),
            P(("wide", "narrow"), None, None),
            P(("wide", "narrow"), None, None),
            P(("wide", "narrow"), None, None),
            P(("wide", "narrow"), None, None),
            P(("wide", "narrow"), None, None),
            P(("wide", "narrow"), None),
            P(("wide", "narrow"), None),
            P(("wide", "narrow"), None),
        ),
        out_specs=(
            P(("wide", "narrow"), None),
            P(("wide", "narrow"), None),
            P(("wide", "narrow"), None),
            P(("wide", "narrow"), None),
            P(("wide", "narrow"), None),
            P(),
            P(),
            P(),
            P(("wide", "narrow"), None, None),
            P(("wide", "narrow"), None, None),
            P(("wide", "narrow"), None, None),
            P(("wide", "narrow"), None, None),
            P(("wide", "narrow"), None, None),
            P(("wide", "narrow"), None, None),
            P(("wide", "narrow"), None, None),
            P(("wide", "narrow"), None, None),
            P(("wide", "narrow"), None),
            P(("wide", "narrow"), None),
            P(("wide", "narrow"), None),
        ),
        check_vma=False,
    )
```

```python
import functools
import math

import jax
import jax.numpy as jnp
import numpy as np
from jax import lax
from jax.experimental import pallas as pl
from jax.experimental.pallas import tpu as pltpu
from jax.sharding import PartitionSpec as P

MODEL_WIDTH = 384
ATTENTION_HEADS = 12
HEAD_DIM = 32
BIAS_NET_HIDDEN = 512
EXPERTS = 32
SIDE = 8
IMG_TOK = 1024
STEP = 10
WIN = 64
GROUP = 4
GROUP_LANES = 128
VMEM_BYTES = 48 * 2**20
VMEM_MOST = 62 * 2**20
EXPERT_PARTS = 2
TABLE = 256
TABLE_MID = 119
STRIDE = 16
SUM_LANES = BIAS_NET_HIDDEN
SECOND_ROWS = 8
SHIFT_ROW = 20
FIRST_ROWS = 21
SCALE_ROWS = 24
SUM_ROWS = 32


highest = lax.Precision.HIGHEST
beta_one = 0.9
beta_two = 0.999
epsilon = 1e-08
dense_rate = 0.05
expert_rate = 0.05
small_rate = 0.3
weight_decay = 0.05
contract_rows = (((0,), (0,)), ((), ()))
contract_cols = (((1,), (1,)), ((), ()))


def pieces(small_params):
    length_list = (
        MODEL_WIDTH,
        MODEL_WIDTH,
        MODEL_WIDTH,
        MODEL_WIDTH,
        MODEL_WIDTH,
        MODEL_WIDTH,
        MODEL_WIDTH,
        ATTENTION_HEADS,
        BIAS_NET_HIDDEN,
        2 * BIAS_NET_HIDDEN,
        BIAS_NET_HIDDEN * ATTENTION_HEADS,
    )
    piece_collection = []
    offset = 0
    for length in length_list:
        piece_collection.append(small_params[offset : offset + length])
        offset = offset + length
    piece_collection[9] = piece_collection[9].reshape(2, BIAS_NET_HIDDEN)
    piece_collection[10] = piece_collection[10].reshape(BIAS_NET_HIDDEN, ATTENTION_HEADS)
    return piece_collection


def norm_rows(values, gain, shift):
    average = jnp.mean(values, axis=-1, keepdims=True)
    centred = values - average
    variance = jnp.mean(centred * centred, axis=-1, keepdims=True)
    return centred * lax.rsqrt(variance + 1e-05) * gain + shift


def position_bias(small_params):
    piece_collection = pieces(small_params)
    span = 2 * SIDE - 1
    offsets = jnp.arange(span, dtype=jnp.float32) - (SIDE - 1)
    coords = jnp.stack([jnp.repeat(offsets, span), jnp.tile(offsets, span)], axis=1) * (
        8.0 / (SIDE - 1)
    )
    coords = jnp.sign(coords) * jnp.log2(jnp.abs(coords) + 1.0) / 3.0
    hidden = jax.nn.gelu(
        jnp.dot(coords, piece_collection[9], precision=highest) + piece_collection[8]
    )
    table = 16.0 * jax.nn.sigmoid(jnp.dot(hidden, piece_collection[10], precision=highest))
    places = jnp.arange(WIN, dtype=jnp.int32)
    row_pos = places // SIDE
    col_pos = places % SIDE
    index = (row_pos[:, None] - row_pos[None, :] + SIDE - 1) * span + (
        col_pos[:, None] - col_pos[None, :] + SIDE - 1
    )
    lookup = (index.reshape(-1, 1) == jnp.arange(span * span, dtype=jnp.int32)[None, :]).astype(
        table.dtype
    )
    spread = jnp.dot(lookup, table, precision=highest)
    return spread.T.reshape(ATTENTION_HEADS, WIN, WIN)


def matmul_back(left_low, right_low, grad_low):
    grad_left = lax.dot_general(
        grad_low, right_low, contract_cols, preferred_element_type=jnp.float32
    )
    grad_right = lax.dot_general(
        left_low, grad_low, contract_rows, preferred_element_type=jnp.float32
    )
    return (grad_left, grad_right)


def add_joined_bias(raw, params):
    piece_collection = pieces(params)
    return raw + jnp.concatenate(
        [piece_collection[4], jnp.zeros_like(piece_collection[4]), piece_collection[5]]
    )


def add_out_bias(raw, params):
    return raw + pieces(params)[6]


def normalize_heads(projected):
    window_count = projected.shape[0] // WIN
    shaped = projected.reshape(window_count, WIN, 3, ATTENTION_HEADS, HEAD_DIM)
    queries = shaped[:, :, 0]
    key_vecs = shaped[:, :, 1]
    queries = queries * lax.rsqrt(jnp.sum(queries * queries, axis=-1, keepdims=True) + 1e-06)
    key_vecs = key_vecs * lax.rsqrt(jnp.sum(key_vecs * key_vecs, axis=-1, keepdims=True) + 1e-06)
    return (queries, key_vecs, shaped[:, :, 2])


def softmax_part(cosine, params):
    scale = jnp.exp(pieces(params)[7])[:, None, None]
    return jax.nn.softmax(cosine * scale + position_bias(params), axis=-1)


def front_forward_split(tokens_low, weights_low, params, route_ids):
    rows_here = tokens_low.shape[0]
    qkv_low = weights_low[:, : 3 * MODEL_WIDTH]
    out_low = weights_low[:, 3 * MODEL_WIDTH : 4 * MODEL_WIDTH]
    route_low = weights_low[:, 4 * MODEL_WIDTH :]
    raw_qkv = jnp.dot(tokens_low, qkv_low, preferred_element_type=jnp.float32)
    projected = add_joined_bias(raw_qkv, params)
    q_f, k_f, v_f = normalize_heads(projected)
    q_low = q_f.astype(jnp.bfloat16)
    k_low = k_f.astype(jnp.bfloat16)
    v_low = v_f.astype(jnp.bfloat16)
    cosine = jnp.einsum("wihd,wjhd->whij", q_low, k_low, preferred_element_type=jnp.float32)
    probs = softmax_part(cosine, params)
    probs_low = probs.astype(jnp.bfloat16)
    mixed_low = (
        jnp.einsum("whij,wjhd->wihd", probs_low, v_low, preferred_element_type=jnp.float32)
        .astype(jnp.bfloat16)
        .reshape(rows_here, MODEL_WIDTH)
    )
    attended = add_out_bias(jnp.dot(mixed_low, out_low, preferred_element_type=jnp.float32), params)
    piece_collection = pieces(params)
    section_one = tokens_low.astype(jnp.float32) + norm_rows(
        attended, piece_collection[0], piece_collection[1]
    )
    section_low = section_one.astype(jnp.bfloat16)
    logits = jnp.dot(section_low, route_low, preferred_element_type=jnp.float32)
    chosen_mask = (
        route_ids[:, None] == jnp.arange(logits.shape[1], dtype=jnp.int32)[None, :]
    ).astype(jnp.float32)
    gating = jax.nn.sigmoid(jnp.sum(logits * chosen_mask, axis=1))
    kept = (
        projected,
        q_low,
        k_low,
        v_low,
        cosine,
        probs_low,
        mixed_low,
        attended,
        section_low,
        logits,
        chosen_mask,
    )
    return (section_one, gating, section_low, kept)


def front_backward_split(tokens_low, weights_low, params, kept, grad_section, grad_gate, grad_feed):
    (
        projected,
        q_low,
        k_low,
        v_low,
        cosine,
        probs_low,
        mixed_low,
        attended,
        section_low,
        logits,
        chosen_mask,
    ) = kept
    rows_here = tokens_low.shape[0]
    window_count = rows_here // WIN
    qkv_low = weights_low[:, : 3 * MODEL_WIDTH]
    out_low = weights_low[:, 3 * MODEL_WIDTH : 4 * MODEL_WIDTH]
    route_low = weights_low[:, 4 * MODEL_WIDTH :]

    def gate_part(logit_values):
        return jax.nn.sigmoid(jnp.sum(logit_values * chosen_mask, axis=1))

    gate_back = jax.vjp(gate_part, logits)[1]
    grad_logits = gate_back(grad_gate)[0].astype(jnp.bfloat16)
    grad_from_route, grad_route = matmul_back(section_low, route_low, grad_logits)
    grad_total = grad_section + grad_feed + grad_from_route

    def section_part(attended_value, params_value):
        piece_collection = pieces(params_value)
        return norm_rows(attended_value, piece_collection[0], piece_collection[1])

    section_back = jax.vjp(section_part, attended, params)[1]
    grad_attended, grad_params_a = section_back(grad_total)
    grad_att_low = grad_attended.astype(jnp.bfloat16)
    grad_params_b = jax.vjp(add_out_bias, jnp.zeros_like(attended), params)[1](
        grad_att_low.astype(jnp.float32)
    )[1]
    grad_mixed, grad_out = matmul_back(mixed_low, out_low, grad_att_low)
    grad_mixed_low = grad_mixed.astype(jnp.bfloat16).reshape(
        window_count, WIN, ATTENTION_HEADS, HEAD_DIM
    )
    grad_probs = jnp.einsum(
        "wihd,wjhd->whij", grad_mixed_low, v_low, preferred_element_type=jnp.float32
    )
    grad_v = jnp.einsum(
        "whij,wihd->wjhd", probs_low, grad_mixed_low, preferred_element_type=jnp.float32
    )
    soft_back = jax.vjp(softmax_part, cosine, params)[1]
    grad_cosine, grad_params_c = soft_back(grad_probs)
    grad_cos_low = grad_cosine.astype(jnp.bfloat16)
    grad_q = jnp.einsum("whij,wjhd->wihd", grad_cos_low, k_low, preferred_element_type=jnp.float32)
    grad_k = jnp.einsum("whij,wihd->wjhd", grad_cos_low, q_low, preferred_element_type=jnp.float32)
    norm_back = jax.vjp(normalize_heads, projected)[1]
    grad_projected = norm_back((grad_q, grad_k, grad_v))[0]
    grad_proj_low = grad_projected.astype(jnp.bfloat16)
    grad_params_d = jax.vjp(add_joined_bias, jnp.zeros_like(projected), params)[1](
        grad_proj_low.astype(jnp.float32)
    )[1]
    grad_tokens, grad_qkv = matmul_back(tokens_low, qkv_low, grad_proj_low)
    grad_inputs = grad_total + grad_tokens
    grad_weights = jnp.concatenate([grad_qkv, grad_out, grad_route], axis=1)
    grad_params = grad_params_a + grad_params_b + grad_params_c + grad_params_d
    return (grad_inputs, grad_weights, grad_params)


def finish_block(section_one, gating, combined, kept_rows, live_rows, small_params):
    piece_collection = pieces(small_params)
    branch = (
        norm_rows(combined, piece_collection[2], piece_collection[3])
        * (gating * kept_rows)[:, None]
    )
    return (section_one + branch) * live_rows[:, None]


def assign(route_ids, count, experts, capacity):
    places = jnp.arange(route_ids.shape[0], dtype=jnp.int32)
    live_rows = places // IMG_TOK < count
    chosen = (
        (route_ids[:, None] == jnp.arange(experts, dtype=jnp.int32)[None, :]) & live_rows[:, None]
    ).astype(jnp.int32)
    before = jnp.cumsum(chosen, axis=0) - chosen
    slot = jnp.sum(before * chosen, axis=1)
    kept_rows = live_rows & (slot < capacity)
    dest_slot = jnp.where(kept_rows, route_ids * capacity + slot, experts * capacity)
    return (live_rows, kept_rows, dest_slot)


def adamw_step(weight, gradient, first, second, rate, decay):
    first_new = beta_one * first + (1.0 - beta_one) * gradient
    second_new = beta_two * second + (1.0 - beta_two) * gradient * gradient
    first_hat = first_new / (1.0 - beta_one**STEP)
    second_hat = second_new / (1.0 - beta_two**STEP)
    weight_new = weight - rate * (first_hat / (jnp.sqrt(second_hat) + epsilon) + decay * weight)
    return (weight_new, first_new, second_new)


def trade_rows(payload):
    arrived_rows = lax.all_to_all(
        payload, ("wide", "narrow"), split_axis=0, concat_axis=0, tiled=True
    )
    return arrived_rows


def axis_bits(axis):
    size = lax.axis_size(axis)
    return [(axis, 1 << k) for k in range(size.bit_length() - 1)]


def swap(value, step):
    axis, offset = step
    return lax.ppermute(value, axis, [(i, i ^ offset) for i in range(lax.axis_size(axis))])


def upper(step):
    axis, offset = step
    return (lax.axis_index(axis) & offset) > 0


def gather_rows(share):
    steps = axis_bits("narrow") + axis_bits("wide")
    first, rest = steps[0], steps[1:]
    other = swap(share, first)
    block = jnp.where(
        upper(first), jnp.concatenate([other, share]), jnp.concatenate([share, other])
    )
    held = block
    done = []
    core = ("wide", 1)
    for step in [s for s in rest if s != core] + [core]:
        place = sum(1 for d in done if rest.index(d) > rest.index(step))
        other = swap(held, step)
        held = jnp.where(
            upper(step), jnp.stack([other, held], place), jnp.stack([held, other], place)
        )
        done.append(step)
    return held.reshape(-1, share.shape[1])


def sum_grads(partial, small):
    steps = axis_bits("narrow") + axis_bits("wide")
    first, rest = steps[0], steps[1:]
    core = ("wide", 1)
    order = [core] + [s for s in rest[::-1] if s != core]
    count = lax.axis_size(("wide", "narrow"))
    share = partial.shape[0] // count
    held = partial.reshape((2,) * len(rest) + (2 * share, partial.shape[1]))
    left = rest[::-1]
    for step in order:
        place = left.index(step)
        side = upper(step).astype(jnp.int32)
        send = lax.dynamic_index_in_dim(held, 1 - side, place, keepdims=False)
        keep = lax.dynamic_index_in_dim(held, side, place, keepdims=False)
        other = swap(send.astype(jnp.bfloat16), step)
        small = small + swap(small, step)
        held = keep + other.astype(jnp.float32)
        left = [s for s in left if s != step]
    side = upper(first)
    send = jnp.where(side, held[:share], held[share:])
    keep = jnp.where(side, held[share:], held[:share])
    other = swap(send.astype(jnp.bfloat16), first)
    small = small + swap(small, first)
    return keep + other.astype(jnp.float32), small


def join(held, step, axis=None):
    other = swap(held, step)
    if axis is None or axis >= 0:
        both = functools.partial(jnp.stack, axis=axis or 0)
    else:
        both = functools.partial(jnp.concatenate, axis=axis)
    return jnp.where(upper(step), both([other, held]), both([held, other]))


def join_quad(held, steps):
    axis, low = steps[0]
    high = steps[1][1]
    near, far, last = (swap(held, (axis, offset)) for offset in (low, high, low + high))
    ahead = upper(steps[1])
    blocks = [
        jnp.where(ahead, second, first)
        for first, second in ((held, far), (near, last), (far, held), (last, near))
    ]
    return jnp.where(
        upper(steps[0]),
        jnp.stack([blocks[1], blocks[0], blocks[3], blocks[2]]),
        jnp.stack(blocks),
    )


def swap_flat(value, offset):
    axes = ("wide", "narrow")
    return lax.ppermute(value, axes, [(i, i ^ offset) for i in range(lax.axis_size(axes))])


def sum_quads(small, low, high):
    near = small + swap_flat(small, low)
    return near + (swap_flat(small, high) + swap_flat(small, low + high))


def sum_chip(send, keep):
    return (keep + swap(send, ("wide", 1)).astype(jnp.float32)).astype(jnp.bfloat16)


def sum_shares(held):
    wide, narrow = lax.axis_size("wide"), lax.axis_size("narrow")
    groups = [
        [w * narrow + n for w in range(core, wide, 2) for n in range(narrow)] for core in range(2)
    ]
    arrived = lax.all_to_all(held, ("wide", "narrow"), 0, 0, axis_index_groups=groups, tiled=True)
    return jnp.sum(arrived.astype(jnp.float32), axis=0)


def lane_masks(dtype):
    lane = lax.broadcasted_iota(jnp.int32, (1, GROUP_LANES), 1) // HEAD_DIM
    return [(lane == h).astype(jnp.float32).astype(dtype) for h in range(GROUP)]


def dot(left, right):
    return jnp.dot(left, right, preferred_element_type=jnp.float32)


def dot_cols(left, right):
    return lax.dot_general(left, right, contract_cols, preferred_element_type=jnp.float32)


def dot_rows(left, right):
    return lax.dot_general(left, right, contract_rows, preferred_element_type=jnp.float32)


def stack_heads(rows, masks):
    return jnp.concatenate([rows * m for m in masks], axis=0)


def pick_heads(blocks, masks):
    n = blocks.shape[0] // GROUP
    return sum(blocks[n * h : n * h + n] * masks[h] for h in range(GROUP))


def head_sums(values):
    row = lax.broadcasted_iota(jnp.int32, (2 * GROUP_LANES, GROUP_LANES), 0) % GROUP_LANES
    col = lax.broadcasted_iota(jnp.int32, (2 * GROUP_LANES, GROUP_LANES), 1)
    ones = (row // HEAD_DIM == col // HEAD_DIM).astype(jnp.float32).astype(jnp.bfloat16)
    high = values.astype(jnp.bfloat16)
    rest = (values - high.astype(jnp.float32)).astype(jnp.bfloat16)
    sums = []
    for start in range(0, values.shape[1], GROUP_LANES):
        cut = slice(start, start + GROUP_LANES)
        sums.append(dot(jnp.concatenate([high[:, cut], rest[:, cut]], axis=1), ones))
    return jnp.concatenate(sums, axis=1)


def send_rows(dest_row, rows, out_ref):
    total = out_ref.shape[0]
    block = math.gcd(total, 256)
    for start in range(0, total, block):
        slot = lax.broadcasted_iota(jnp.int32, (block, rows.shape[0]), 0) + start
        chosen = jnp.where(slot == dest_row, 1.0, 0.0).astype(jnp.bfloat16)
        out_ref[pl.ds(start, block), :] = dot(chosen, rows).astype(jnp.bfloat16)


def gelu_pair(pre):
    inner = math.sqrt(2.0 / math.pi)
    square = pre * pre
    bend = jnp.tanh(pre * (inner + (inner * 0.044715) * square))
    half = 0.5 + 0.5 * bend
    slope = half + pre * (half * (1.0 - bend)) * (inner + (3.0 * inner * 0.044715) * square)
    return pre * half, slope


def take_rows(dest_row, rows):
    count, total = dest_row.shape[1], rows.shape[0]
    places = jnp.broadcast_to(dest_row.astype(jnp.float32), (GROUP_LANES, count)).T
    lane = lax.broadcasted_iota(jnp.int32, (count, GROUP_LANES), 1).astype(jnp.float32)
    chosen = jnp.concatenate(
        [
            jnp.where(places == lane + float(start), 1.0, 0.0).astype(jnp.bfloat16)
            for start in range(0, total, GROUP_LANES)
        ],
        axis=1,
    )
    return dot(chosen, rows)


def assign_kernel(capacity, count_ref, route_ref, cot_ref, dest_ref, out_ref):
    tokens = route_ref.shape[1]
    total = out_ref.shape[0]
    span = GROUP_LANES
    live_end = count_ref[0] * IMG_TOK
    first = lax.broadcasted_iota(jnp.int32, (span, span), 0)
    second = lax.broadcasted_iota(jnp.int32, (span, span), 1)
    earlier = jnp.where(first < second, 1.0, 0.0).astype(jnp.bfloat16)
    whole = jnp.ones((span, span), jnp.bfloat16)
    carry = jnp.zeros((EXPERTS, span), jnp.float32)
    for start in range(0, tokens, span):
        route = route_ref[:, start : start + span]
        place = lax.broadcasted_iota(jnp.int32, (1, span), 1) + start
        expert = lax.broadcasted_iota(jnp.int32, (EXPERTS, span), 0)
        chosen = jnp.where((expert == route) & (place < live_end), 1.0, 0.0)
        low = chosen.astype(jnp.bfloat16)
        before = dot(low, earlier) + carry
        carry = carry + dot(low, whole)
        slot = jnp.sum(before * chosen, axis=0, keepdims=True).astype(jnp.int32)
        keep = (place < live_end) & (slot < capacity)
        dest_ref[:, start : start + span] = jnp.where(keep, route * capacity + slot, total)
    send_rows(dest_ref[...], cot_ref[...], out_ref)


def call_assign(images, routes, cotangent, capacity):
    tokens = routes.shape[0]
    total = EXPERTS * capacity
    return pl.pallas_call(
        functools.partial(assign_kernel, capacity),
        out_shape=(
            jax.ShapeDtypeStruct((1, tokens), jnp.int32),
            jax.ShapeDtypeStruct((total, MODEL_WIDTH), jnp.bfloat16),
        ),
        in_specs=[
            pl.BlockSpec(memory_space=pltpu.SMEM),
            pl.BlockSpec(memory_space=pltpu.VMEM),
            pl.BlockSpec(memory_space=pltpu.VMEM),
        ],
        out_specs=(
            pl.BlockSpec(memory_space=pltpu.VMEM),
            pl.BlockSpec(memory_space=pltpu.VMEM),
        ),
        cost_estimate=pl.CostEstimate(
            flops=2 * total * tokens * MODEL_WIDTH, bytes_accessed=4 * 10**6, transcendentals=0
        ),
        compiler_params=pltpu.CompilerParams(vmem_limit_bytes=VMEM_BYTES),
        name="assign",
    )(images, routes.reshape(1, tokens), cotangent)


def front_kernel(
    dest_ref,
    tokens_ref,
    weight_ref,
    rows_ref,
    scale_ref,
    bias_ref,
    placed_ref,
    section_ref,
    attended_ref,
    mixed_ref,
    raw_ref,
    heads_ref,
    probs_ref,
    low_ref,
):
    step = pl.program_id(0)
    block = tokens_ref.shape[0]
    width = MODEL_WIDTH
    tokens = tokens_ref[...]
    masks_low = lane_masks(jnp.bfloat16)
    masks = lane_masks(jnp.float32)
    projected = dot(tokens, weight_ref[:, : 3 * width])
    queries = projected[:, :width] + rows_ref[4:5, :]
    keys = projected[:, width : 2 * width]
    values = projected[:, 2 * width :] + rows_ref[5:6, :]
    raw_ref[:, :width] = queries
    raw_ref[:, width:] = keys
    heads_ref[:, :width] = (queries * lax.rsqrt(head_sums(queries * queries) + 1e-06)).astype(
        jnp.bfloat16
    )
    heads_ref[:, width : 2 * width] = (
        keys * lax.rsqrt(head_sums(keys * keys) + 1e-06)
    ).astype(jnp.bfloat16)
    heads_ref[:, 2 * width :] = values.astype(jnp.bfloat16)
    units = [
        (window, group)
        for window in range(block // WIN)
        for group in range(width // GROUP_LANES)
    ]

    def part(window, group, side):
        start = side * width + group * GROUP_LANES
        return heads_ref[window * WIN : window * WIN + WIN, start : start + GROUP_LANES]

    cosines = [dot_cols(part(w, g, 1), stack_heads(part(w, g, 0), masks_low)) for w, g in units]
    all_probs = []
    for (window, group), cosine in zip(units, cosines):
        scores = cosine * scale_ref[group] + bias_ref[group]
        powers = jnp.exp(scores - jnp.max(scores, axis=0, keepdims=True))
        probs = powers * (1.0 / jnp.sum(powers, axis=0, keepdims=True))
        probs_ref[window, group] = probs
        all_probs.append(probs.astype(jnp.bfloat16))
    mixes = [pick_heads(dot_rows(p, part(w, g, 2)), masks) for (w, g), p in zip(units, all_probs)]
    for (window, group), mixed in zip(units, mixes):
        mixed_ref[
            window * WIN : window * WIN + WIN,
            group * GROUP_LANES : group * GROUP_LANES + GROUP_LANES,
        ] = mixed.astype(jnp.bfloat16)
    attended = dot(mixed_ref[...], weight_ref[:, 3 * width : 4 * width]) + rows_ref[6:7, :]
    attended_ref[...] = attended
    section = tokens.astype(jnp.float32) + norm_rows(attended, rows_ref[0:1, :], rows_ref[1:2, :])
    section_ref[...] = section
    low_ref[pl.ds(pl.multiple_of(step * block, block), block), :] = section.astype(jnp.bfloat16)

    @pl.when(step == pl.num_programs(0) - 1)
    def _():
        send_rows(dest_ref[...], low_ref[...], placed_ref)


def token_block(tok_rows):
    return math.gcd(tok_rows, 256)


def whole(shape):
    return pl.BlockSpec(shape, lambda i: (0,) * len(shape))


def by_rows(block, width):
    return pl.BlockSpec((block, width), lambda i: (i, 0))


def call_front(dest, tokens, gathered, rows, scale, bias, capacity):
    count, width = tokens.shape
    total = EXPERTS * capacity
    block = token_block(count)
    groups = width // GROUP_LANES
    probs_shape = (count // WIN, groups, WIN, GROUP * WIN)
    return pl.pallas_call(
        front_kernel,
        grid=(count // block,),
        out_shape=(
            jax.ShapeDtypeStruct((total, width), jnp.bfloat16),
            jax.ShapeDtypeStruct((count, width), jnp.float32),
            jax.ShapeDtypeStruct((count, width), jnp.float32),
            jax.ShapeDtypeStruct((count, width), jnp.bfloat16),
            jax.ShapeDtypeStruct((count, 2 * width), jnp.float32),
            jax.ShapeDtypeStruct((count, 3 * width), jnp.bfloat16),
            jax.ShapeDtypeStruct(probs_shape, jnp.float32),
        ),
        in_specs=[
            whole(dest.shape),
            by_rows(block, width),
            whole(gathered.shape),
            whole(rows.shape),
            whole(scale.shape),
            whole(bias.shape),
        ],
        out_specs=(
            whole((total, width)),
            by_rows(block, width),
            by_rows(block, width),
            by_rows(block, width),
            by_rows(block, 2 * width),
            by_rows(block, 3 * width),
            pl.BlockSpec((block // WIN,) + probs_shape[1:], lambda i: (i, 0, 0, 0)),
        ),
        scratch_shapes=[pltpu.VMEM((count, width), jnp.bfloat16)],
        cost_estimate=pl.CostEstimate(
            flops=2 * count * width * width * 8, bytes_accessed=20 * 10**6, transcendentals=0
        ),
        compiler_params=pltpu.CompilerParams(vmem_limit_bytes=VMEM_BYTES),
        name="front",
    )(dest, tokens, gathered, rows, scale, bias)


def back_kernel(
    count_ref,
    dest_ref,
    arrived_ref,
    cot_ref,
    weight_ref,
    rows_ref,
    scale_ref,
    attended_ref,
    raw_ref,
    heads_ref,
    probs_ref,
    expert_ref,
    table_ref,
    coords_ref,
    net_ref,
    total_ref,
    low_attended,
    low_projected,
    sums_ref,
    grad_bias_ref,
    grad_scale_ref,
    grad_heads,
):
    step = pl.program_id(0)
    block = cot_ref.shape[0]
    width = MODEL_WIDTH
    start_row = pl.multiple_of(step * block, block)
    masks_low = lane_masks(jnp.bfloat16)
    masks = lane_masks(jnp.float32)

    @pl.when(step == 0)
    def _():
        sums_ref[...] = jnp.zeros_like(sums_ref)
        grad_bias_ref[...] = jnp.zeros_like(grad_bias_ref)
        grad_scale_ref[...] = jnp.zeros_like(grad_scale_ref)

    place = lax.broadcasted_iota(jnp.int32, (block, 1), 0) + start_row
    live = jnp.where(place < count_ref[0] * IMG_TOK, 1.0, 0.0)
    feed = take_rows(dest_ref[...], arrived_ref[...])
    total = cot_ref[...].astype(jnp.float32) * live + feed
    attended = attended_ref[...]
    centred = attended - jnp.mean(attended, axis=-1, keepdims=True)
    spread = lax.rsqrt(jnp.mean(centred * centred, axis=-1, keepdims=True) + 1e-05)
    unit = centred * spread
    grad_unit = total * rows_ref[0:1, :]
    grad_attended = spread * (
        grad_unit
        - jnp.mean(grad_unit, axis=-1, keepdims=True)
        - unit * jnp.mean(grad_unit * unit, axis=-1, keepdims=True)
    )
    grad_low = grad_attended.astype(jnp.bfloat16)
    total_ref[...] = total
    low_attended[...] = grad_low
    sums_ref[0:1, :width] += jnp.sum(total * unit, axis=0, keepdims=True)
    sums_ref[1:2, :width] += jnp.sum(total, axis=0, keepdims=True)
    sums_ref[6:7, :width] += jnp.sum(grad_low.astype(jnp.float32), axis=0, keepdims=True)
    grad_mixed = dot_cols(grad_low, weight_ref[:, 3 * width : 4 * width]).astype(jnp.bfloat16)
    units = [
        (window, group)
        for window in range(block // WIN)
        for group in range(width // GROUP_LANES)
    ]

    def cut(window, group, side):
        start = side * width + group * GROUP_LANES
        return slice(window * WIN, window * WIN + WIN), slice(start, start + GROUP_LANES)

    queries = [stack_heads(heads_ref[cut(w, g, 0)], masks_low) for w, g in units]
    grad_outs = [stack_heads(grad_mixed[cut(w, g, 0)], masks_low) for w, g in units]
    all_grad_probs = [
        dot_cols(heads_ref[cut(w, g, 2)], grad_out) for (w, g), grad_out in zip(units, grad_outs)
    ]
    cosines = [dot_cols(heads_ref[cut(w, g, 1)], query) for (w, g), query in zip(units, queries)]
    all_probs, grad_cosines = [], []
    for (window, group), grad_probs, cosine in zip(units, all_grad_probs, cosines):
        probs = probs_ref[window, group]
        all_probs.append(probs.astype(jnp.bfloat16))
        weighed = probs * grad_probs
        grad_scores = weighed - probs * jnp.sum(weighed, axis=0, keepdims=True)
        grad_bias_ref[group] += grad_scores
        grad_scale_ref[group] += jnp.sum(grad_scores * cosine, axis=0, keepdims=True)
        grad_cosines.append((grad_scores * scale_ref[group]).astype(jnp.bfloat16))
    for (w, g), probs, grad_out in zip(units, all_probs, grad_outs):
        grad_heads[cut(w, g, 2)] = dot(probs, grad_out)
    for (w, g), grad_cosine, query in zip(units, grad_cosines, queries):
        grad_heads[cut(w, g, 1)] = dot(grad_cosine, query)
    for (w, g), grad_cosine in zip(units, grad_cosines):
        grad_heads[cut(w, g, 0)] = pick_heads(
            dot_rows(grad_cosine, heads_ref[cut(w, g, 1)]), masks
        )
    for side in range(2):
        cut = slice(side * width, side * width + width)
        raw = raw_ref[:, cut]
        inverse = lax.rsqrt(head_sums(raw * raw) + 1e-06)
        unit = raw * inverse
        grad = grad_heads[:, cut]
        low_projected[:, cut] = (inverse * (grad - unit * head_sums(grad * unit))).astype(
            jnp.bfloat16
        )
    low_projected[:, 2 * width :] = grad_heads[:, 2 * width :].astype(jnp.bfloat16)
    grad_projected = low_projected[...]
    sums_ref[4:5, :width] += jnp.sum(
        grad_projected[:, :width].astype(jnp.float32), axis=0, keepdims=True
    )
    sums_ref[5:6, :width] += jnp.sum(
        grad_projected[:, 2 * width :].astype(jnp.float32), axis=0, keepdims=True
    )
    @pl.when(step == pl.num_programs(0) - 1)
    def _():
        sums_ref[2:4, :width] = expert_ref[1:3, :]
        for group in range(grad_scale_ref.shape[0]):
            at = SCALE_ROWS + group
            sums_ref[at : at + 1, : GROUP * WIN] = grad_scale_ref[group]
        net_back(
            sum_offsets(grad_bias_ref), table_ref[...], coords_ref[...], net_ref, sums_ref
        )


def sum_offsets(grad_bias_ref):
    row = lax.broadcasted_iota(jnp.int32, (GROUP * WIN, TABLE), 0)
    lane = lax.broadcasted_iota(jnp.int32, (GROUP * WIN, TABLE), 1)
    query = row % WIN
    aim = TABLE_MID - STRIDE * (query // SIDE) - query % SIDE
    spreads = [
        jnp.where((lane == aim) & (row // WIN == h), 1.0, 0.0).astype(jnp.bfloat16)
        for h in range(GROUP)
    ]
    sums = []
    for group in range(grad_bias_ref.shape[0]):
        grad = grad_bias_ref[group]
        high = grad.astype(jnp.bfloat16)
        rest = grad - high.astype(jnp.float32)
        middle = rest.astype(jnp.bfloat16)
        last = (rest - middle.astype(jnp.float32)).astype(jnp.bfloat16)
        parts = jnp.concatenate([high, middle, last], axis=0)
        for h in range(GROUP):
            spread = dot(parts, spreads[h])
            spread = spread[:WIN] + spread[WIN : 2 * WIN] + spread[2 * WIN :]
            rows = spread[:SIDE]
            for r in range(1, SIDE):
                rows = rows + pltpu.roll(spread[SIDE * r : SIDE * r + SIDE], STRIDE * r, 1)
            rows = pltpu.roll(rows, 0, 1, stride=1, stride_axis=0)
            sums.append(jnp.sum(rows, axis=0, keepdims=True))
    return jnp.concatenate(sums, axis=0)


def net_back(grad, table, coords, net_ref, sums_ref):
    heads = table.shape[0]
    second, shift, first = net_ref[:heads], net_ref[heads : heads + 1], net_ref[heads + 1 : heads + 3]
    pre = coords[:, 0:1] * first[0:1] + coords[:, 1:2] * first[1:2] + shift
    hidden, slope = gelu_pair(pre)
    grad_logits = grad * table * (1.0 - table * (1.0 / 16.0))
    sums_ref[SECOND_ROWS : SECOND_ROWS + heads, :] = jnp.dot(
        grad_logits, hidden, precision=highest, preferred_element_type=jnp.float32
    )
    grad_pre = slope * lax.dot_general(
        grad_logits, second, contract_rows, precision=highest, preferred_element_type=jnp.float32
    )
    sums_ref[SHIFT_ROW : SHIFT_ROW + 1, :] = jnp.sum(grad_pre, axis=0, keepdims=True)
    for k in range(2):
        sums_ref[FIRST_ROWS + k : FIRST_ROWS + k + 1, :] = jnp.sum(
            grad_pre * coords[:, k : k + 1], axis=0, keepdims=True
        )


def call_back(
    images, dest, arrived, cotangent, gathered, rows, scale, attended, raw, heads, probs,
    sums_expert, table, net,
):
    count, width = cotangent.shape
    block = token_block(count)
    groups = width // GROUP_LANES
    coords = jnp.asarray(offset_coords())
    return pl.pallas_call(
        back_kernel,
        grid=(count // block,),
        out_shape=(
            jax.ShapeDtypeStruct((count, width), jnp.float32),
            jax.ShapeDtypeStruct((count, width), jnp.bfloat16),
            jax.ShapeDtypeStruct((count, 3 * width), jnp.bfloat16),
            jax.ShapeDtypeStruct((SUM_ROWS, SUM_LANES), jnp.float32),
        ),
        in_specs=[
            pl.BlockSpec(memory_space=pltpu.SMEM),
            pl.BlockSpec((1, block), lambda i: (0, i)),
            whole(arrived.shape),
            by_rows(block, width),
            whole(gathered.shape),
            whole(rows.shape),
            whole(scale.shape),
            by_rows(block, width),
            by_rows(block, 2 * width),
            by_rows(block, 3 * width),
            pl.BlockSpec((block // WIN,) + probs.shape[1:], lambda i: (i, 0, 0, 0)),
            whole(sums_expert.shape),
            whole(table.shape),
            whole(coords.shape),
            whole(net.shape),
        ],
        out_specs=(
            by_rows(block, width),
            by_rows(block, width),
            by_rows(block, 3 * width),
            whole((SUM_ROWS, SUM_LANES)),
        ),
        scratch_shapes=[
            pltpu.VMEM((groups, WIN, GROUP * WIN), jnp.float32),
            pltpu.VMEM((groups, 1, GROUP * WIN), jnp.float32),
            pltpu.VMEM((block, 3 * width), jnp.float32),
        ],
        cost_estimate=pl.CostEstimate(
            flops=2 * count * width * width * 10, bytes_accessed=20 * 10**6, transcendentals=0
        ),
        compiler_params=pltpu.CompilerParams(vmem_limit_bytes=VMEM_MOST),
        name="back",
    )(
        images, dest, arrived, cotangent, gathered, rows, scale, attended, raw, heads, probs,
        sums_expert, table, coords, net,
    )


def dense_kernel(
    narrow,
    place_ref,
    tokens_ref,
    mixed_ref,
    attended_ref,
    projected_ref,
    expert_ref,
    send_ref,
    keep_ref,
):
    width = tokens_ref.shape[1]
    grad_dense = jnp.concatenate(
        [
            dot_rows(tokens_ref[...], projected_ref[...]),
            dot_rows(mixed_ref[...], attended_ref[...]),
        ],
        axis=1,
    )
    chips = keep_ref.shape[0]
    on_first = place_ref[0] == 0
    row = lax.broadcasted_iota(jnp.int32, (GROUP_LANES, width), 0)
    grad_route = jnp.where(row == place_ref[1], expert_ref[3:4, :], 0.0).T
    share = width // (2 * chips)
    for chip in range(chips):
        cuts = []
        for core in range(2):
            row = (chip // narrow * 2 * narrow + core * narrow + chip % narrow) * share
            rows, route = grad_dense[row : row + share], grad_route[row : row + share]
            halves = jnp.concatenate([rows[:, : 2 * width], rows[:, 2 * width :]], axis=0)
            route = jnp.concatenate([route, jnp.zeros_like(route)], axis=0)
            cuts.append(jnp.concatenate([halves, route], axis=1))
        keep_ref[chip] = jnp.where(on_first, cuts[0], cuts[1])
        send_ref[chip] = jnp.where(on_first, cuts[1], cuts[0]).astype(jnp.bfloat16)


def call_dense(tokens, mixed, attended, projected, sums_expert):
    count, width = tokens.shape
    narrow = lax.axis_size("narrow")
    chips = narrow * lax.axis_size("wide") // 2
    shape = (chips, width // chips, 2 * width + GROUP_LANES)
    place = jnp.stack([lax.axis_index("wide") % 2, lax.axis_index(("wide", "narrow"))])
    return pl.pallas_call(
        functools.partial(dense_kernel, narrow),
        out_shape=(
            jax.ShapeDtypeStruct(shape, jnp.bfloat16),
            jax.ShapeDtypeStruct(shape, jnp.float32),
        ),
        in_specs=[pl.BlockSpec(memory_space=pltpu.SMEM)]
        + [pl.BlockSpec(memory_space=pltpu.VMEM)] * 5,
        out_specs=(pl.BlockSpec(memory_space=pltpu.VMEM),) * 2,
        cost_estimate=pl.CostEstimate(
            flops=8 * count * width * width, bytes_accessed=7 * 10**6, transcendentals=0
        ),
        compiler_params=pltpu.CompilerParams(vmem_limit_bytes=VMEM_BYTES),
        name="dense",
    )(place.astype(jnp.int32), tokens, mixed, attended, projected, sums_expert)


def inputs_kernel(total_ref, projected_ref, weight_ref, out_ref):
    wide = projected_ref.shape[1]
    out_ref[...] = (
        total_ref[...] + dot_cols(projected_ref[...], weight_ref[:, :wide])
    ).astype(jnp.bfloat16)


def call_inputs(total, projected, gathered):
    count, width = total.shape
    block = token_block(count)
    return pl.pallas_call(
        inputs_kernel,
        grid=(count // block,),
        out_shape=jax.ShapeDtypeStruct((count, width), jnp.bfloat16),
        in_specs=[
            by_rows(block, width),
            by_rows(block, 3 * width),
            whole(gathered.shape),
        ],
        out_specs=by_rows(block, width),
        cost_estimate=pl.CostEstimate(
            flops=0, bytes_accessed=0, transcendentals=0
        ),
        compiler_params=pltpu.CompilerParams(vmem_limit_bytes=VMEM_BYTES),
        name="inputs",
    )(total, projected, gathered)


def layer_kernel(count_ref, dest_ref, branch_ref, section_ref, out_ref):
    block = out_ref.shape[0]
    place = lax.broadcasted_iota(jnp.int32, (block, 1), 0) + pl.program_id(0) * block
    live = jnp.where(place < count_ref[0] * IMG_TOK, 1.0, 0.0)
    branch = take_rows(dest_ref[...], branch_ref[...])
    out_ref[...] = ((section_ref[...] + branch) * live).astype(jnp.bfloat16)


def call_layer(images, dest, branch, section):
    count, width = section.shape
    block = token_block(count)
    return pl.pallas_call(
        layer_kernel,
        grid=(count // block,),
        out_shape=jax.ShapeDtypeStruct((count, width), jnp.bfloat16),
        in_specs=[
            pl.BlockSpec(memory_space=pltpu.SMEM),
            pl.BlockSpec((1, block), lambda i: (0, i)),
            whole(branch.shape),
            by_rows(block, width),
        ],
        out_specs=by_rows(block, width),
        cost_estimate=pl.CostEstimate(
            flops=0, bytes_accessed=0, transcendentals=0
        ),
        compiler_params=pltpu.CompilerParams(vmem_limit_bytes=VMEM_BYTES),
        name="layer",
    )(images, dest, branch, section)


def expert_kernel(
    rows_ref,
    cot_ref,
    first_ref,
    second_ref,
    bias_one_ref,
    vecs_ref,
    branch_ref,
    back_ref,
    hidden_ref,
    grad_pre_ref,
    grad_result_ref,
    sums_ref,
    sum_pre_ref,
):
    @pl.when(pl.program_id(0) == 0)
    def _():
        sums_ref[...] = jnp.zeros_like(sums_ref)
        sum_pre_ref[...] = jnp.zeros_like(sum_pre_ref)

    bias_two, gain, shift, route = (vecs_ref[i : i + 1, :] for i in range(4))
    count = rows_ref.shape[0]
    size = count // EXPERT_PARTS
    cuts = [slice(start, start + size) for start in range(0, count, size)]
    pres = [dot(rows_ref[cut, :], first_ref[...]) + bias_one_ref[...] for cut in cuts]
    pairs = [gelu_pair(pre) for pre in pres]
    hiddens = [hidden.astype(jnp.bfloat16) for hidden, _ in pairs]
    raws = [dot(hidden, second_ref[...]) + bias_two for hidden in hiddens]
    grads = []
    for cut, hidden, raw in zip(cuts, hiddens, raws):
        hidden_ref[cut, :] = hidden
        rows = rows_ref[cut, :].astype(jnp.float32)
        result = raw.astype(jnp.bfloat16).astype(jnp.float32)
        gating = jax.nn.sigmoid(jnp.sum(rows * route, axis=-1, keepdims=True))
        centred = result - jnp.mean(result, axis=-1, keepdims=True)
        spread = lax.rsqrt(jnp.mean(centred * centred, axis=-1, keepdims=True) + 1e-05)
        unit = centred * spread
        normed = unit * gain + shift
        branch_ref[cut, :] = (normed * gating).astype(jnp.bfloat16)
        cot = cot_ref[cut, :].astype(jnp.float32)
        grad_gate = jnp.sum(cot * normed, axis=-1, keepdims=True)
        gated = cot * gating
        grad_unit = gated * gain
        grad_result = (
            spread
            * (
                grad_unit
                - jnp.mean(grad_unit, axis=-1, keepdims=True)
                - unit * jnp.mean(grad_unit * unit, axis=-1, keepdims=True)
            )
        ).astype(jnp.bfloat16)
        grad_result_ref[cut, :] = grad_result
        grad_logit = (
            (grad_gate * gating * (1.0 - gating)).astype(jnp.bfloat16).astype(jnp.float32)
        )
        sums_ref[0:1, :] += jnp.sum(grad_result.astype(jnp.float32), axis=0, keepdims=True)
        sums_ref[1:2, :] += jnp.sum(gated * unit, axis=0, keepdims=True)
        sums_ref[2:3, :] += jnp.sum(gated, axis=0, keepdims=True)
        sums_ref[3:4, :] += jnp.sum(rows * grad_logit, axis=0, keepdims=True)
        grads.append((grad_result, grad_logit))
    grad_hiddens = [dot_cols(grad, second_ref[...]) for grad, _ in grads]
    grad_pres = [
        (grad * slope).astype(jnp.bfloat16) for grad, (_, slope) in zip(grad_hiddens, pairs)
    ]
    for cut, grad_pre, (_, grad_logit) in zip(cuts, grad_pres, grads):
        grad_pre_ref[cut, :] = grad_pre
        sum_pre_ref[...] += jnp.sum(grad_pre.astype(jnp.float32), axis=0, keepdims=True)
        back_ref[cut, :] = (dot_cols(grad_pre, first_ref[...]) + grad_logit * route).astype(
            jnp.bfloat16
        )


def call_expert(rows, cot, first, second, bias_one, vecs):
    count, width = rows.shape
    ff = first.shape[1]
    block = math.gcd(count, 640)
    return pl.pallas_call(
        expert_kernel,
        grid=(count // block,),
        out_shape=(
            jax.ShapeDtypeStruct((count, width), jnp.bfloat16),
            jax.ShapeDtypeStruct((count, width), jnp.bfloat16),
            jax.ShapeDtypeStruct((count, ff), jnp.bfloat16),
            jax.ShapeDtypeStruct((count, ff), jnp.bfloat16),
            jax.ShapeDtypeStruct((count, width), jnp.bfloat16),
            jax.ShapeDtypeStruct((8, width), jnp.float32),
            jax.ShapeDtypeStruct((1, ff), jnp.float32),
        ),
        in_specs=[
            by_rows(block, width),
            by_rows(block, width),
            whole(first.shape),
            whole(second.shape),
            whole(bias_one.shape),
            whole(vecs.shape),
        ],
        out_specs=(
            by_rows(block, width),
            by_rows(block, width),
            by_rows(block, ff),
            by_rows(block, ff),
            by_rows(block, width),
            whole((8, width)),
            whole((1, ff)),
        ),
        cost_estimate=pl.CostEstimate(
            flops=8 * count * width * ff, bytes_accessed=16 * 10**6, transcendentals=count * ff
        ),
        compiler_params=pltpu.CompilerParams(vmem_limit_bytes=VMEM_MOST),
        name="expert",
    )(rows, cot, first, second, bias_one, vecs)


def offset_coords():
    place = TABLE_MID - np.arange(TABLE)
    row = (place + STRIDE // 2 - 1) // STRIDE
    coords = np.stack([row, place - STRIDE * row], axis=1) * (8.0 / (SIDE - 1))
    return (np.sign(coords) * np.log2(np.abs(coords) + 1.0) / 3.0).astype(np.float32)


def bias_table(params):
    piece_collection = pieces(params)
    hidden = jax.nn.gelu(
        jnp.dot(offset_coords(), piece_collection[9], precision=highest) + piece_collection[8]
    )
    return 16.0 * jax.nn.sigmoid(jnp.dot(hidden, piece_collection[10], precision=highest)).T


def spread_bias(table):
    places = jnp.arange(WIN, dtype=jnp.int32)
    coded = STRIDE * (places // SIDE) + places % SIDE
    index = TABLE_MID + coded[:, None] - coded[None, :]
    lookup = (index.reshape(1, -1) == jnp.arange(TABLE, dtype=jnp.int32)[:, None]).astype(
        table.dtype
    )
    bias = jnp.dot(table, lookup, precision=highest).reshape(-1, GROUP, WIN, WIN)
    return bias.transpose(0, 2, 1, 3).reshape(-1, WIN, GROUP * WIN)


def per_device_split(
    tokens,
    cotangent,
    routes,
    images,
    dense_weight,
    dense_moment,
    dense_square,
    small_params,
    small_moment,
    small_square,
    inner_weight,
    inner_moment,
    inner_square,
    outer_weight,
    outer_moment,
    outer_square,
    expert_bias,
    bias_moment,
    bias_square,
):
    slices = lax.axis_size(("wide", "narrow"))
    split = slices // EXPERTS
    member = lax.axis_index(("wide", "narrow")) % split
    piece = MODEL_WIDTH // split
    ff_dev = inner_weight.shape[2]
    tok_rows = tokens.shape[0]
    capacity = (5 * tok_rows + 4 * EXPERTS - 1) // (4 * EXPERTS)
    slot_total = EXPERTS * capacity
    route_ids = routes[:, 0]
    live_rows, kept_rows, dest_slot = assign(route_ids, images[0], EXPERTS, capacity)
    live_f = live_rows.astype(jnp.float32)
    keep_f = kept_rows.astype(jnp.float32)
    clipped = jnp.minimum(dest_slot, slot_total - 1)
    gathered = gather_rows(dense_weight.astype(jnp.bfloat16))
    section_one, gating, expert_feed, kept = front_forward_split(
        tokens, gathered, small_params, route_ids
    )

    def fan_out(rows_value):
        placed_rows = (
            jnp.zeros((slot_total, MODEL_WIDTH), jnp.bfloat16)
            .at[dest_slot]
            .set(rows_value.astype(jnp.bfloat16), mode="drop")
        )
        copies = jnp.broadcast_to(
            placed_rows.reshape(EXPERTS, 1, capacity, MODEL_WIDTH),
            (EXPERTS, split, capacity, MODEL_WIDTH),
        )
        return trade_rows(copies.reshape(slices, capacity, MODEL_WIDTH)).reshape(
            slices * capacity, MODEL_WIDTH
        )

    def fan_in(partials):
        arrived = trade_rows(partials.reshape(slices, capacity, MODEL_WIDTH))
        summed = jnp.sum(
            arrived.reshape(EXPERTS, split, capacity, MODEL_WIDTH).astype(jnp.float32), axis=1
        ).reshape(slot_total, MODEL_WIDTH)
        return jnp.take(summed, clipped, axis=0) * keep_f[:, None]

    expert_rows = fan_out(expert_feed)
    first_matrix = inner_weight[0].astype(jnp.bfloat16)
    second_matrix = outer_weight[0].astype(jnp.bfloat16)
    pre_act = (
        jnp.dot(expert_rows, first_matrix, preferred_element_type=jnp.float32)
        + expert_bias[0, :ff_dev]
    )
    hidden = jax.nn.gelu(pre_act).astype(jnp.bfloat16)
    out_bias = lax.dynamic_update_slice(
        jnp.zeros((MODEL_WIDTH,), jnp.float32), expert_bias[0, ff_dev:], (member * piece,)
    )
    result = (jnp.dot(hidden, second_matrix, preferred_element_type=jnp.float32) + out_bias).astype(
        jnp.bfloat16
    )
    combined = fan_in(result)

    def tail_local(section_value, gate_value, combined_value, params):
        return finish_block(section_value, gate_value, combined_value, keep_f, live_f, params)

    layer_value, tail_back = jax.vjp(tail_local, section_one, gating, combined, small_params)
    grad_section, grad_gate, grad_combined, grad_small_tail = tail_back(
        cotangent.astype(jnp.float32)
    )
    grad_result = fan_out(grad_combined)
    grad_outer = lax.dot_general(
        hidden, grad_result, contract_rows, preferred_element_type=jnp.float32
    )
    grad_hidden = lax.dot_general(
        grad_result, second_matrix, contract_cols, preferred_element_type=jnp.float32
    )
    gelu_back = jax.vjp(jax.nn.gelu, pre_act)[1]
    grad_pre = gelu_back(grad_hidden)[0].astype(jnp.bfloat16)
    grad_inner = lax.dot_general(
        expert_rows, grad_pre, contract_rows, preferred_element_type=jnp.float32
    )
    column_total = jnp.sum(grad_result.astype(jnp.float32), axis=0)
    grad_bias = jnp.concatenate(
        [
            jnp.sum(grad_pre.astype(jnp.float32), axis=0),
            lax.dynamic_slice_in_dim(column_total, member * piece, piece, 0),
        ]
    )
    grad_rows = lax.dot_general(
        grad_pre, first_matrix, contract_cols, preferred_element_type=jnp.float32
    ).astype(jnp.bfloat16)
    grad_feed = fan_in(grad_rows)
    grad_inputs, grad_weights, grad_small_front = front_backward_split(
        tokens, gathered, small_params, kept, grad_section, grad_gate, grad_feed
    )
    grad_small = grad_small_front + grad_small_tail
    grad_dense, grad_small = sum_grads(grad_weights, grad_small)
    dense_out = adamw_step(
        dense_weight, grad_dense, dense_moment, dense_square, dense_rate, weight_decay
    )
    small_out = adamw_step(small_params, grad_small, small_moment, small_square, small_rate, 0.0)
    inner_out = adamw_step(
        inner_weight, grad_inner[None], inner_moment, inner_square, expert_rate, weight_decay
    )
    outer_out = adamw_step(
        outer_weight, grad_outer[None], outer_moment, outer_square, expert_rate, weight_decay
    )
    bias_out = adamw_step(expert_bias, grad_bias[None], bias_moment, bias_square, expert_rate, 0.0)
    return (
        layer_value.astype(jnp.bfloat16),
        grad_inputs.astype(jnp.bfloat16),
        dense_out[0],
        dense_out[1],
        dense_out[2],
        small_out[0],
        small_out[1],
        small_out[2],
        inner_out[0],
        inner_out[1],
        inner_out[2],
        inner_out[0].astype(jnp.bfloat16),
        outer_out[0],
        outer_out[1],
        outer_out[2],
        outer_out[0].astype(jnp.bfloat16),
        bias_out[0],
        bias_out[1],
        bias_out[2],
    )


def per_device(
    tokens,
    cotangent,
    routes,
    images,
    dense_weight,
    dense_moment,
    dense_square,
    small_params,
    small_moment,
    small_square,
    inner_weight,
    inner_moment,
    inner_square,
    outer_weight,
    outer_moment,
    outer_square,
    expert_bias,
    bias_moment,
    bias_square,
):
    slices = lax.axis_size(("wide", "narrow"))
    if slices != EXPERTS:
        return per_device_split(
            tokens,
            cotangent,
            routes,
            images,
            dense_weight,
            dense_moment,
            dense_square,
            small_params,
            small_moment,
            small_square,
            inner_weight,
            inner_moment,
            inner_square,
            outer_weight,
            outer_moment,
            outer_square,
            expert_bias,
            bias_moment,
            bias_square,
        )
    expert = lax.axis_index(("wide", "narrow"))
    ff_dev = inner_weight.shape[2]
    tok_rows = tokens.shape[0]
    capacity = (5 * tok_rows + 4 * EXPERTS - 1) // (4 * EXPERTS)
    slot_total = EXPERTS * capacity

    def trade(rows):
        traded = trade_rows(rows.reshape(slices, capacity, MODEL_WIDTH))
        return traded.reshape(slot_total, MODEL_WIDTH)

    scale_at = 7 * MODEL_WIDTH
    share = dense_weight.astype(jnp.bfloat16)
    across, *deep = axis_bits("narrow")
    held = join_quad(share, deep)
    held, route_ids, cot = lax.optimization_barrier((held, routes, cotangent))
    dest, placed_cot = call_assign(images, route_ids, cot, capacity)
    held = join(held, across, -2)
    held, placed_cot, dest = lax.optimization_barrier((held, placed_cot, dest))
    core, *rest = axis_bits("wide")
    for step in rest:
        held = join(held, step)
    gathered = join(held, core, len(rest)).reshape(-1, share.shape[-1])
    gathered, placed_cot, params = lax.optimization_barrier((gathered, placed_cot, small_params))
    cot_rows = trade(placed_cot)
    table = bias_table(params)
    net_pieces = pieces(params)
    net = jnp.concatenate([net_pieces[10].T, net_pieces[8][None, :], net_pieces[9]])
    vectors = params[:scale_at].reshape(7, MODEL_WIDTH)
    scale_heads = jnp.exp(params[scale_at : scale_at + ATTENTION_HEADS])
    scale = jnp.repeat(scale_heads, WIN).reshape(-1, 1, GROUP * WIN)
    bias = spread_bias(table)
    placed, section, attended, mixed, raw, heads, probs = call_front(
        dest, tokens, gathered, vectors, scale, bias, capacity
    )
    placed, cot_rows = lax.optimization_barrier((placed, cot_rows))
    expert_rows = trade(placed)
    first_matrix = inner_weight[0].astype(jnp.bfloat16)
    second_matrix = outer_weight[0].astype(jnp.bfloat16)
    route_row = lax.dynamic_slice_in_dim(gathered, 4 * MODEL_WIDTH + expert, 1, 1)
    vecs = jnp.concatenate(
        [expert_bias[:, ff_dev:], vectors[2:4], route_row.astype(jnp.float32).reshape(1, -1)]
    )
    branch, grad_rows, hidden, grad_pre, grad_result, sums_expert, sum_pre = call_expert(
        expert_rows, cot_rows, first_matrix, second_matrix, expert_bias[:, :ff_dev], vecs
    )
    arrived = trade(grad_rows)
    grad_outer = dot_rows(hidden, grad_result)
    grad_inner = dot_rows(expert_rows, grad_pre)
    grad_bias = jnp.concatenate([sum_pre, sums_expert[0:1]], axis=1)[0]
    inner_out = adamw_step(
        inner_weight, grad_inner[None], inner_moment, inner_square, expert_rate, weight_decay
    )
    outer_out = adamw_step(
        outer_weight, grad_outer[None], outer_moment, outer_square, expert_rate, weight_decay
    )
    inner_out += (inner_out[0].astype(jnp.bfloat16),)
    outer_out += (outer_out[0].astype(jnp.bfloat16),)
    branch, arrived, inner_out, outer_out = lax.optimization_barrier(
        (branch, arrived, inner_out, outer_out)
    )
    branch_rows = trade(branch)
    total, low_attended, low_projected, sums = call_back(
        images,
        dest,
        arrived,
        cotangent,
        gathered,
        vectors,
        scale,
        attended,
        raw,
        heads,
        probs,
        sums_expert,
        table,
        net,
    )
    send, keep = call_dense(tokens, mixed, low_attended, low_projected, sums_expert)
    grad_inputs = call_inputs(total, low_projected, gathered)
    held = sum_chip(send, keep)
    narrow = lax.axis_size("narrow")
    sums = sums + swap_flat(sums, narrow)
    held, sums, branch_rows, grad_inputs = lax.optimization_barrier(
        (held, sums, branch_rows, grad_inputs)
    )
    grad_dense = sum_shares(held)
    sums = sum_quads(sum_quads(sums, 2, 4), 1, 2 * narrow)
    layer_out = call_layer(images, dest, branch_rows, section)
    share_rows = dense_weight.shape[0]
    half = 2 * MODEL_WIDTH
    grad_dense = jnp.concatenate(
        [
            grad_dense[:share_rows, :half],
            grad_dense[share_rows:, :half],
            grad_dense[:share_rows, half : half + EXPERTS],
        ],
        axis=1,
    )
    grad_scale = sums[SCALE_ROWS : SCALE_ROWS + ATTENTION_HEADS // GROUP, : GROUP * WIN]
    grad_small = jnp.concatenate(
        [
            sums[:7, :MODEL_WIDTH].reshape(-1),
            jnp.sum(grad_scale.reshape(ATTENTION_HEADS, WIN), axis=1) * scale_heads,
            sums[SHIFT_ROW : FIRST_ROWS + 2].reshape(-1),
            sums[SECOND_ROWS : SECOND_ROWS + ATTENTION_HEADS].T.reshape(-1),
        ]
    )
    dense_out = adamw_step(
        dense_weight, grad_dense, dense_moment, dense_square, dense_rate, weight_decay
    )
    small_out = adamw_step(small_params, grad_small, small_moment, small_square, small_rate, 0.0)
    bias_out = adamw_step(expert_bias, grad_bias[None], bias_moment, bias_square, expert_rate, 0.0)
    return (
        layer_out,
        grad_inputs,
        dense_out[0],
        dense_out[1],
        dense_out[2],
        small_out[0],
        small_out[1],
        small_out[2],
        inner_out[0],
        inner_out[1],
        inner_out[2],
        inner_out[3],
        outer_out[0],
        outer_out[1],
        outer_out[2],
        outer_out[3],
        bias_out[0],
        bias_out[1],
        bias_out[2],
    )


def solution(mesh):
    return jax.shard_map(
        per_device,
        mesh=mesh,
        in_specs=(
            P(("wide", "narrow"), None),
            P(("wide", "narrow"), None),
            P(("wide", "narrow"), None),
            P(("wide", "narrow")),
            P(("wide", "narrow"), None),
            P(("wide", "narrow"), None),
            P(("wide", "narrow"), None),
            P(),
            P(),
            P(),
            P(("wide", "narrow"), None, None),
            P(("wide", "narrow"), None, None),
            P(("wide", "narrow"), None, None),
            P(("wide", "narrow"), None, None),
            P(("wide", "narrow"), None, None),
            P(("wide", "narrow"), None, None),
            P(("wide", "narrow"), None),
            P(("wide", "narrow"), None),
            P(("wide", "narrow"), None),
        ),
        out_specs=(
            P(("wide", "narrow"), None),
            P(("wide", "narrow"), None),
            P(("wide", "narrow"), None),
            P(("wide", "narrow"), None),
            P(("wide", "narrow"), None),
            P(),
            P(),
            P(),
            P(("wide", "narrow"), None, None),
            P(("wide", "narrow"), None, None),
            P(("wide", "narrow"), None, None),
            P(("wide", "narrow"), None, None),
            P(("wide", "narrow"), None, None),
            P(("wide", "narrow"), None, None),
            P(("wide", "narrow"), None, None),
            P(("wide", "narrow"), None, None),
            P(("wide", "narrow"), None),
            P(("wide", "narrow"), None),
            P(("wide", "narrow"), None),
        ),
        check_vma=False,
    )
```

```python
import functools
import math

import jax
import jax.numpy as jnp
import numpy as np
from jax import lax
from jax.experimental import pallas as pl
from jax.experimental.pallas import tpu as pltpu
from jax.sharding import PartitionSpec as P

MODEL_WIDTH = 384
ATTENTION_HEADS = 12
HEAD_DIM = 32
BIAS_NET_HIDDEN = 512
EXPERTS = 32
SIDE = 8
IMG_TOK = 1024
STEP = 10
WIN = 64
GROUP = 4
GROUP_LANES = 128
VMEM_BYTES = 48 * 2**20
VMEM_MOST = 62 * 2**20
EXPERT_PARTS = 2
TABLE = 256
TABLE_MID = 119
STRIDE = 16
SUM_LANES = BIAS_NET_HIDDEN
SECOND_ROWS = 8
SHIFT_ROW = 20
FIRST_ROWS = 21
SCALE_ROWS = 24
SUM_ROWS = 32


highest = lax.Precision.HIGHEST
beta_one = 0.9
beta_two = 0.999
epsilon = 1e-08
dense_rate = 0.05
expert_rate = 0.05
small_rate = 0.3
weight_decay = 0.05
contract_rows = (((0,), (0,)), ((), ()))
contract_cols = (((1,), (1,)), ((), ()))


def pieces(small_params):
    length_list = (
        MODEL_WIDTH,
        MODEL_WIDTH,
        MODEL_WIDTH,
        MODEL_WIDTH,
        MODEL_WIDTH,
        MODEL_WIDTH,
        MODEL_WIDTH,
        ATTENTION_HEADS,
        BIAS_NET_HIDDEN,
        2 * BIAS_NET_HIDDEN,
        BIAS_NET_HIDDEN * ATTENTION_HEADS,
    )
    piece_collection = []
    offset = 0
    for length in length_list:
        piece_collection.append(small_params[offset : offset + length])
        offset = offset + length
    piece_collection[9] = piece_collection[9].reshape(2, BIAS_NET_HIDDEN)
    piece_collection[10] = piece_collection[10].reshape(BIAS_NET_HIDDEN, ATTENTION_HEADS)
    return piece_collection


def norm_rows(values, gain, shift):
    average = jnp.mean(values, axis=-1, keepdims=True)
    centred = values - average
    variance = jnp.mean(centred * centred, axis=-1, keepdims=True)
    return centred * lax.rsqrt(variance + 1e-05) * gain + shift


def position_bias(small_params):
    piece_collection = pieces(small_params)
    span = 2 * SIDE - 1
    offsets = jnp.arange(span, dtype=jnp.float32) - (SIDE - 1)
    coords = jnp.stack([jnp.repeat(offsets, span), jnp.tile(offsets, span)], axis=1) * (
        8.0 / (SIDE - 1)
    )
    coords = jnp.sign(coords) * jnp.log2(jnp.abs(coords) + 1.0) / 3.0
    hidden = jax.nn.gelu(
        jnp.dot(coords, piece_collection[9], precision=highest) + piece_collection[8]
    )
    table = 16.0 * jax.nn.sigmoid(jnp.dot(hidden, piece_collection[10], precision=highest))
    places = jnp.arange(WIN, dtype=jnp.int32)
    row_pos = places // SIDE
    col_pos = places % SIDE
    index = (row_pos[:, None] - row_pos[None, :] + SIDE - 1) * span + (
        col_pos[:, None] - col_pos[None, :] + SIDE - 1
    )
    lookup = (index.reshape(-1, 1) == jnp.arange(span * span, dtype=jnp.int32)[None, :]).astype(
        table.dtype
    )
    spread = jnp.dot(lookup, table, precision=highest)
    return spread.T.reshape(ATTENTION_HEADS, WIN, WIN)


def matmul_back(left_low, right_low, grad_low):
    grad_left = lax.dot_general(
        grad_low, right_low, contract_cols, preferred_element_type=jnp.float32
    )
    grad_right = lax.dot_general(
        left_low, grad_low, contract_rows, preferred_element_type=jnp.float32
    )
    return (grad_left, grad_right)


def add_joined_bias(raw, params):
    piece_collection = pieces(params)
    return raw + jnp.concatenate(
        [piece_collection[4], jnp.zeros_like(piece_collection[4]), piece_collection[5]]
    )


def add_out_bias(raw, params):
    return raw + pieces(params)[6]


def normalize_heads(projected):
    window_count = projected.shape[0] // WIN
    shaped = projected.reshape(window_count, WIN, 3, ATTENTION_HEADS, HEAD_DIM)
    queries = shaped[:, :, 0]
    key_vecs = shaped[:, :, 1]
    queries = queries * lax.rsqrt(jnp.sum(queries * queries, axis=-1, keepdims=True) + 1e-06)
    key_vecs = key_vecs * lax.rsqrt(jnp.sum(key_vecs * key_vecs, axis=-1, keepdims=True) + 1e-06)
    return (queries, key_vecs, shaped[:, :, 2])


def softmax_part(cosine, params):
    scale = jnp.exp(pieces(params)[7])[:, None, None]
    return jax.nn.softmax(cosine * scale + position_bias(params), axis=-1)


def front_forward_split(tokens_low, weights_low, params, route_ids):
    rows_here = tokens_low.shape[0]
    qkv_low = weights_low[:, : 3 * MODEL_WIDTH]
    out_low = weights_low[:, 3 * MODEL_WIDTH : 4 * MODEL_WIDTH]
    route_low = weights_low[:, 4 * MODEL_WIDTH :]
    raw_qkv = jnp.dot(tokens_low, qkv_low, preferred_element_type=jnp.float32)
    projected = add_joined_bias(raw_qkv, params)
    q_f, k_f, v_f = normalize_heads(projected)
    q_low = q_f.astype(jnp.bfloat16)
    k_low = k_f.astype(jnp.bfloat16)
    v_low = v_f.astype(jnp.bfloat16)
    cosine = jnp.einsum("wihd,wjhd->whij", q_low, k_low, preferred_element_type=jnp.float32)
    probs = softmax_part(cosine, params)
    probs_low = probs.astype(jnp.bfloat16)
    mixed_low = (
        jnp.einsum("whij,wjhd->wihd", probs_low, v_low, preferred_element_type=jnp.float32)
        .astype(jnp.bfloat16)
        .reshape(rows_here, MODEL_WIDTH)
    )
    attended = add_out_bias(jnp.dot(mixed_low, out_low, preferred_element_type=jnp.float32), params)
    piece_collection = pieces(params)
    section_one = tokens_low.astype(jnp.float32) + norm_rows(
        attended, piece_collection[0], piece_collection[1]
    )
    section_low = section_one.astype(jnp.bfloat16)
    logits = jnp.dot(section_low, route_low, preferred_element_type=jnp.float32)
    chosen_mask = (
        route_ids[:, None] == jnp.arange(logits.shape[1], dtype=jnp.int32)[None, :]
    ).astype(jnp.float32)
    gating = jax.nn.sigmoid(jnp.sum(logits * chosen_mask, axis=1))
    kept = (
        projected,
        q_low,
        k_low,
        v_low,
        cosine,
        probs_low,
        mixed_low,
        attended,
        section_low,
        logits,
        chosen_mask,
    )
    return (section_one, gating, section_low, kept)


def front_backward_split(tokens_low, weights_low, params, kept, grad_section, grad_gate, grad_feed):
    (
        projected,
        q_low,
        k_low,
        v_low,
        cosine,
        probs_low,
        mixed_low,
        attended,
        section_low,
        logits,
        chosen_mask,
    ) = kept
    rows_here = tokens_low.shape[0]
    window_count = rows_here // WIN
    qkv_low = weights_low[:, : 3 * MODEL_WIDTH]
    out_low = weights_low[:, 3 * MODEL_WIDTH : 4 * MODEL_WIDTH]
    route_low = weights_low[:, 4 * MODEL_WIDTH :]

    def gate_part(logit_values):
        return jax.nn.sigmoid(jnp.sum(logit_values * chosen_mask, axis=1))

    gate_back = jax.vjp(gate_part, logits)[1]
    grad_logits = gate_back(grad_gate)[0].astype(jnp.bfloat16)
    grad_from_route, grad_route = matmul_back(section_low, route_low, grad_logits)
    grad_total = grad_section + grad_feed + grad_from_route

    def section_part(attended_value, params_value):
        piece_collection = pieces(params_value)
        return norm_rows(attended_value, piece_collection[0], piece_collection[1])

    section_back = jax.vjp(section_part, attended, params)[1]
    grad_attended, grad_params_a = section_back(grad_total)
    grad_att_low = grad_attended.astype(jnp.bfloat16)
    grad_params_b = jax.vjp(add_out_bias, jnp.zeros_like(attended), params)[1](
        grad_att_low.astype(jnp.float32)
    )[1]
    grad_mixed, grad_out = matmul_back(mixed_low, out_low, grad_att_low)
    grad_mixed_low = grad_mixed.astype(jnp.bfloat16).reshape(
        window_count, WIN, ATTENTION_HEADS, HEAD_DIM
    )
    grad_probs = jnp.einsum(
        "wihd,wjhd->whij", grad_mixed_low, v_low, preferred_element_type=jnp.float32
    )
    grad_v = jnp.einsum(
        "whij,wihd->wjhd", probs_low, grad_mixed_low, preferred_element_type=jnp.float32
    )
    soft_back = jax.vjp(softmax_part, cosine, params)[1]
    grad_cosine, grad_params_c = soft_back(grad_probs)
    grad_cos_low = grad_cosine.astype(jnp.bfloat16)
    grad_q = jnp.einsum("whij,wjhd->wihd", grad_cos_low, k_low, preferred_element_type=jnp.float32)
    grad_k = jnp.einsum("whij,wihd->wjhd", grad_cos_low, q_low, preferred_element_type=jnp.float32)
    norm_back = jax.vjp(normalize_heads, projected)[1]
    grad_projected = norm_back((grad_q, grad_k, grad_v))[0]
    grad_proj_low = grad_projected.astype(jnp.bfloat16)
    grad_params_d = jax.vjp(add_joined_bias, jnp.zeros_like(projected), params)[1](
        grad_proj_low.astype(jnp.float32)
    )[1]
    grad_tokens, grad_qkv = matmul_back(tokens_low, qkv_low, grad_proj_low)
    grad_inputs = grad_total + grad_tokens
    grad_weights = jnp.concatenate([grad_qkv, grad_out, grad_route], axis=1)
    grad_params = grad_params_a + grad_params_b + grad_params_c + grad_params_d
    return (grad_inputs, grad_weights, grad_params)


def finish_block(section_one, gating, combined, kept_rows, live_rows, small_params):
    piece_collection = pieces(small_params)
    branch = (
        norm_rows(combined, piece_collection[2], piece_collection[3])
        * (gating * kept_rows)[:, None]
    )
    return (section_one + branch) * live_rows[:, None]


def assign(route_ids, count, experts, capacity):
    places = jnp.arange(route_ids.shape[0], dtype=jnp.int32)
    live_rows = places // IMG_TOK < count
    chosen = (
        (route_ids[:, None] == jnp.arange(experts, dtype=jnp.int32)[None, :]) & live_rows[:, None]
    ).astype(jnp.int32)
    before = jnp.cumsum(chosen, axis=0) - chosen
    slot = jnp.sum(before * chosen, axis=1)
    kept_rows = live_rows & (slot < capacity)
    dest_slot = jnp.where(kept_rows, route_ids * capacity + slot, experts * capacity)
    return (live_rows, kept_rows, dest_slot)


def adamw_step(weight, gradient, first, second, rate, decay):
    first_new = beta_one * first + (1.0 - beta_one) * gradient
    second_new = beta_two * second + (1.0 - beta_two) * gradient * gradient
    first_hat = first_new / (1.0 - beta_one**STEP)
    second_hat = second_new / (1.0 - beta_two**STEP)
    weight_new = weight - rate * (first_hat / (jnp.sqrt(second_hat) + epsilon) + decay * weight)
    return (weight_new, first_new, second_new)


def trade_rows(payload):
    arrived_rows = lax.all_to_all(
        payload, ("wide", "narrow"), split_axis=0, concat_axis=0, tiled=True
    )
    return arrived_rows


def axis_bits(axis):
    size = lax.axis_size(axis)
    return [(axis, 1 << k) for k in range(size.bit_length() - 1)]


def swap(value, step):
    axis, offset = step
    return lax.ppermute(value, axis, [(i, i ^ offset) for i in range(lax.axis_size(axis))])


def upper(step):
    axis, offset = step
    return (lax.axis_index(axis) & offset) > 0


def gather_rows(share):
    steps = axis_bits("narrow") + axis_bits("wide")
    first, rest = steps[0], steps[1:]
    other = swap(share, first)
    block = jnp.where(
        upper(first), jnp.concatenate([other, share]), jnp.concatenate([share, other])
    )
    held = block
    done = []
    core = ("wide", 1)
    for step in [s for s in rest if s != core] + [core]:
        place = sum(1 for d in done if rest.index(d) > rest.index(step))
        other = swap(held, step)
        held = jnp.where(
            upper(step), jnp.stack([other, held], place), jnp.stack([held, other], place)
        )
        done.append(step)
    return held.reshape(-1, share.shape[1])


def sum_grads(partial, small):
    steps = axis_bits("narrow") + axis_bits("wide")
    first, rest = steps[0], steps[1:]
    core = ("wide", 1)
    order = [core] + [s for s in rest[::-1] if s != core]
    count = lax.axis_size(("wide", "narrow"))
    share = partial.shape[0] // count
    held = partial.reshape((2,) * len(rest) + (2 * share, partial.shape[1]))
    left = rest[::-1]
    for step in order:
        place = left.index(step)
        side = upper(step).astype(jnp.int32)
        send = lax.dynamic_index_in_dim(held, 1 - side, place, keepdims=False)
        keep = lax.dynamic_index_in_dim(held, side, place, keepdims=False)
        other = swap(send.astype(jnp.bfloat16), step)
        small = small + swap(small, step)
        held = keep + other.astype(jnp.float32)
        left = [s for s in left if s != step]
    side = upper(first)
    send = jnp.where(side, held[:share], held[share:])
    keep = jnp.where(side, held[share:], held[:share])
    other = swap(send.astype(jnp.bfloat16), first)
    small = small + swap(small, first)
    return keep + other.astype(jnp.float32), small


def join(held, step, axis=None):
    other = swap(held, step)
    if axis is None or axis >= 0:
        both = functools.partial(jnp.stack, axis=axis or 0)
    else:
        both = functools.partial(jnp.concatenate, axis=axis)
    return jnp.where(upper(step), both([other, held]), both([held, other]))


def join_quad(held, steps):
    axis, low = steps[0]
    high = steps[1][1]
    near, far, last = (swap(held, (axis, offset)) for offset in (low, high, low + high))
    ahead = upper(steps[1])
    blocks = [
        jnp.where(ahead, second, first)
        for first, second in ((held, far), (near, last), (far, held), (last, near))
    ]
    return jnp.where(
        upper(steps[0]),
        jnp.stack([blocks[1], blocks[0], blocks[3], blocks[2]]),
        jnp.stack(blocks),
    )


def swap_flat(value, offset):
    axes = ("wide", "narrow")
    return lax.ppermute(value, axes, [(i, i ^ offset) for i in range(lax.axis_size(axes))])


def sum_quads(small, low, high):
    near = small + swap_flat(small, low)
    return near + (swap_flat(small, high) + swap_flat(small, low + high))


def sum_chip(send, keep):
    return (keep + swap(send, ("wide", 1)).astype(jnp.float32)).astype(jnp.bfloat16)


def sum_shares(held):
    wide, narrow = lax.axis_size("wide"), lax.axis_size("narrow")
    groups = [
        [w * narrow + n for w in range(core, wide, 2) for n in range(narrow)] for core in range(2)
    ]
    arrived = lax.all_to_all(held, ("wide", "narrow"), 0, 0, axis_index_groups=groups, tiled=True)
    return jnp.sum(arrived.astype(jnp.float32), axis=0)


def lane_masks(dtype):
    lane = lax.broadcasted_iota(jnp.int32, (1, GROUP_LANES), 1) // HEAD_DIM
    return [(lane == h).astype(jnp.float32).astype(dtype) for h in range(GROUP)]


def dot(left, right):
    return jnp.dot(left, right, preferred_element_type=jnp.float32)


def dot_cols(left, right):
    return lax.dot_general(left, right, contract_cols, preferred_element_type=jnp.float32)


def dot_rows(left, right):
    return lax.dot_general(left, right, contract_rows, preferred_element_type=jnp.float32)


def stack_heads(rows, masks):
    return jnp.concatenate([rows * m for m in masks], axis=0)


def pick_heads(blocks, masks):
    n = blocks.shape[0] // GROUP
    return sum(blocks[n * h : n * h + n] * masks[h] for h in range(GROUP))


def head_sums(values):
    row = lax.broadcasted_iota(jnp.int32, (2 * GROUP_LANES, GROUP_LANES), 0) % GROUP_LANES
    col = lax.broadcasted_iota(jnp.int32, (2 * GROUP_LANES, GROUP_LANES), 1)
    ones = (row // HEAD_DIM == col // HEAD_DIM).astype(jnp.float32).astype(jnp.bfloat16)
    high = values.astype(jnp.bfloat16)
    rest = (values - high.astype(jnp.float32)).astype(jnp.bfloat16)
    sums = []
    for start in range(0, values.shape[1], GROUP_LANES):
        cut = slice(start, start + GROUP_LANES)
        sums.append(dot(jnp.concatenate([high[:, cut], rest[:, cut]], axis=1), ones))
    return jnp.concatenate(sums, axis=1)


def send_rows(dest_row, rows, out_ref):
    total = out_ref.shape[0]
    block = math.gcd(total, 256)
    for start in range(0, total, block):
        slot = lax.broadcasted_iota(jnp.int32, (block, rows.shape[0]), 0) + start
        chosen = jnp.where(slot == dest_row, 1.0, 0.0).astype(jnp.bfloat16)
        out_ref[pl.ds(start, block), :] = dot(chosen, rows).astype(jnp.bfloat16)


def gelu_pair(pre):
    inner = math.sqrt(2.0 / math.pi)
    square = pre * pre
    bend = jnp.tanh(pre * (inner + (inner * 0.044715) * square))
    half = 0.5 + 0.5 * bend
    slope = half + pre * (half * (1.0 - bend)) * (inner + (3.0 * inner * 0.044715) * square)
    return pre * half, slope


def take_rows(dest_row, rows):
    count, total = dest_row.shape[1], rows.shape[0]
    places = jnp.broadcast_to(dest_row.astype(jnp.float32), (GROUP_LANES, count)).T
    lane = lax.broadcasted_iota(jnp.int32, (count, GROUP_LANES), 1).astype(jnp.float32)
    chosen = jnp.concatenate(
        [
            jnp.where(places == lane + float(start), 1.0, 0.0).astype(jnp.bfloat16)
            for start in range(0, total, GROUP_LANES)
        ],
        axis=1,
    )
    return dot(chosen, rows)


def assign_kernel(capacity, count_ref, route_ref, cot_ref, dest_ref, out_ref):
    tokens = route_ref.shape[1]
    total = out_ref.shape[0]
    span = GROUP_LANES
    live_end = count_ref[0] * IMG_TOK
    first = lax.broadcasted_iota(jnp.int32, (span, span), 0)
    second = lax.broadcasted_iota(jnp.int32, (span, span), 1)
    earlier = jnp.where(first < second, 1.0, 0.0).astype(jnp.bfloat16)
    whole = jnp.ones((span, span), jnp.bfloat16)
    carry = jnp.zeros((EXPERTS, span), jnp.float32)
    for start in range(0, tokens, span):
        route = route_ref[:, start : start + span]
        place = lax.broadcasted_iota(jnp.int32, (1, span), 1) + start
        expert = lax.broadcasted_iota(jnp.int32, (EXPERTS, span), 0)
        chosen = jnp.where((expert == route) & (place < live_end), 1.0, 0.0)
        low = chosen.astype(jnp.bfloat16)
        before = dot(low, earlier) + carry
        carry = carry + dot(low, whole)
        slot = jnp.sum(before * chosen, axis=0, keepdims=True).astype(jnp.int32)
        keep = (place < live_end) & (slot < capacity)
        dest_ref[:, start : start + span] = jnp.where(keep, route * capacity + slot, total)
    send_rows(dest_ref[...], cot_ref[...], out_ref)


def call_assign(images, routes, cotangent, capacity):
    tokens = routes.shape[0]
    total = EXPERTS * capacity
    return pl.pallas_call(
        functools.partial(assign_kernel, capacity),
        out_shape=(
            jax.ShapeDtypeStruct((1, tokens), jnp.int32),
            jax.ShapeDtypeStruct((total, MODEL_WIDTH), jnp.bfloat16),
        ),
        in_specs=[
            pl.BlockSpec(memory_space=pltpu.SMEM),
            pl.BlockSpec(memory_space=pltpu.VMEM),
            pl.BlockSpec(memory_space=pltpu.VMEM),
        ],
        out_specs=(
            pl.BlockSpec(memory_space=pltpu.VMEM),
            pl.BlockSpec(memory_space=pltpu.VMEM),
        ),
        cost_estimate=pl.CostEstimate(
            flops=2 * total * tokens * MODEL_WIDTH, bytes_accessed=4 * 10**6, transcendentals=0
        ),
        compiler_params=pltpu.CompilerParams(vmem_limit_bytes=VMEM_BYTES),
        name="assign",
    )(images, routes.reshape(1, tokens), cotangent)


def front_kernel(
    dest_ref,
    tokens_ref,
    weight_ref,
    rows_ref,
    scale_ref,
    bias_ref,
    placed_ref,
    section_ref,
    attended_ref,
    mixed_ref,
    raw_ref,
    heads_ref,
    probs_ref,
    low_ref,
):
    step = pl.program_id(0)
    block = tokens_ref.shape[0]
    width = MODEL_WIDTH
    tokens = tokens_ref[...]
    masks_low = lane_masks(jnp.bfloat16)
    masks = lane_masks(jnp.float32)
    projected = dot(tokens, weight_ref[:, : 3 * width])
    queries = projected[:, :width] + rows_ref[4:5, :]
    keys = projected[:, width : 2 * width]
    values = projected[:, 2 * width :] + rows_ref[5:6, :]
    raw_ref[:, :width] = queries
    raw_ref[:, width:] = keys
    heads_ref[:, :width] = (queries * lax.rsqrt(head_sums(queries * queries) + 1e-06)).astype(
        jnp.bfloat16
    )
    heads_ref[:, width : 2 * width] = (
        keys * lax.rsqrt(head_sums(keys * keys) + 1e-06)
    ).astype(jnp.bfloat16)
    heads_ref[:, 2 * width :] = values.astype(jnp.bfloat16)
    units = [
        (window, group)
        for window in range(block // WIN)
        for group in range(width // GROUP_LANES)
    ]

    def part(window, group, side):
        start = side * width + group * GROUP_LANES
        return heads_ref[window * WIN : window * WIN + WIN, start : start + GROUP_LANES]

    cosines = [dot_cols(part(w, g, 1), stack_heads(part(w, g, 0), masks_low)) for w, g in units]
    all_probs = []
    for (window, group), cosine in zip(units, cosines):
        scores = cosine * scale_ref[group] + bias_ref[group]
        powers = jnp.exp(scores - jnp.max(scores, axis=0, keepdims=True))
        probs = powers * (1.0 / jnp.sum(powers, axis=0, keepdims=True))
        probs_ref[window, group] = probs
        all_probs.append(probs.astype(jnp.bfloat16))
    mixes = [pick_heads(dot_rows(p, part(w, g, 2)), masks) for (w, g), p in zip(units, all_probs)]
    for (window, group), mixed in zip(units, mixes):
        mixed_ref[
            window * WIN : window * WIN + WIN,
            group * GROUP_LANES : group * GROUP_LANES + GROUP_LANES,
        ] = mixed.astype(jnp.bfloat16)
    attended = dot(mixed_ref[...], weight_ref[:, 3 * width : 4 * width]) + rows_ref[6:7, :]
    attended_ref[...] = attended
    section = tokens.astype(jnp.float32) + norm_rows(attended, rows_ref[0:1, :], rows_ref[1:2, :])
    section_ref[...] = section
    low_ref[pl.ds(pl.multiple_of(step * block, block), block), :] = section.astype(jnp.bfloat16)

    @pl.when(step == pl.num_programs(0) - 1)
    def _():
        send_rows(dest_ref[...], low_ref[...], placed_ref)


def token_block(tok_rows):
    return math.gcd(tok_rows, 256)


def whole(shape):
    return pl.BlockSpec(shape, lambda i: (0,) * len(shape))


def by_rows(block, width):
    return pl.BlockSpec((block, width), lambda i: (i, 0))


def call_front(dest, tokens, gathered, rows, scale, bias, capacity):
    count, width = tokens.shape
    total = EXPERTS * capacity
    block = token_block(count)
    groups = width // GROUP_LANES
    probs_shape = (count // WIN, groups, WIN, GROUP * WIN)
    return pl.pallas_call(
        front_kernel,
        grid=(count // block,),
        out_shape=(
            jax.ShapeDtypeStruct((total, width), jnp.bfloat16),
            jax.ShapeDtypeStruct((count, width), jnp.float32),
            jax.ShapeDtypeStruct((count, width), jnp.float32),
            jax.ShapeDtypeStruct((count, width), jnp.bfloat16),
            jax.ShapeDtypeStruct((count, 2 * width), jnp.float32),
            jax.ShapeDtypeStruct((count, 3 * width), jnp.bfloat16),
            jax.ShapeDtypeStruct(probs_shape, jnp.float32),
        ),
        in_specs=[
            whole(dest.shape),
            by_rows(block, width),
            whole(gathered.shape),
            whole(rows.shape),
            whole(scale.shape),
            whole(bias.shape),
        ],
        out_specs=(
            whole((total, width)),
            by_rows(block, width),
            by_rows(block, width),
            by_rows(block, width),
            by_rows(block, 2 * width),
            by_rows(block, 3 * width),
            pl.BlockSpec((block // WIN,) + probs_shape[1:], lambda i: (i, 0, 0, 0)),
        ),
        scratch_shapes=[pltpu.VMEM((count, width), jnp.bfloat16)],
        cost_estimate=pl.CostEstimate(
            flops=2 * count * width * width * 8, bytes_accessed=20 * 10**6, transcendentals=0
        ),
        compiler_params=pltpu.CompilerParams(vmem_limit_bytes=VMEM_BYTES),
        name="front",
    )(dest, tokens, gathered, rows, scale, bias)


def back_kernel(
    count_ref,
    dest_ref,
    arrived_ref,
    cot_ref,
    weight_ref,
    rows_ref,
    scale_ref,
    attended_ref,
    raw_ref,
    heads_ref,
    probs_ref,
    expert_ref,
    table_ref,
    coords_ref,
    net_ref,
    total_ref,
    low_attended,
    low_projected,
    sums_ref,
    grad_bias_ref,
    grad_scale_ref,
    grad_heads,
):
    step = pl.program_id(0)
    block = cot_ref.shape[0]
    width = MODEL_WIDTH
    start_row = pl.multiple_of(step * block, block)
    masks_low = lane_masks(jnp.bfloat16)
    masks = lane_masks(jnp.float32)

    @pl.when(step == 0)
    def _():
        sums_ref[...] = jnp.zeros_like(sums_ref)
        grad_bias_ref[...] = jnp.zeros_like(grad_bias_ref)
        grad_scale_ref[...] = jnp.zeros_like(grad_scale_ref)

    place = lax.broadcasted_iota(jnp.int32, (block, 1), 0) + start_row
    live = jnp.where(place < count_ref[0] * IMG_TOK, 1.0, 0.0)
    feed = take_rows(dest_ref[...], arrived_ref[...])
    total = cot_ref[...].astype(jnp.float32) * live + feed
    attended = attended_ref[...]
    centred = attended - jnp.mean(attended, axis=-1, keepdims=True)
    spread = lax.rsqrt(jnp.mean(centred * centred, axis=-1, keepdims=True) + 1e-05)
    unit = centred * spread
    grad_unit = total * rows_ref[0:1, :]
    grad_attended = spread * (
        grad_unit
        - jnp.mean(grad_unit, axis=-1, keepdims=True)
        - unit * jnp.mean(grad_unit * unit, axis=-1, keepdims=True)
    )
    grad_low = grad_attended.astype(jnp.bfloat16)
    total_ref[...] = total
    low_attended[...] = grad_low
    sums_ref[0:1, :width] += jnp.sum(total * unit, axis=0, keepdims=True)
    sums_ref[1:2, :width] += jnp.sum(total, axis=0, keepdims=True)
    sums_ref[6:7, :width] += jnp.sum(grad_low.astype(jnp.float32), axis=0, keepdims=True)
    grad_mixed = dot_cols(grad_low, weight_ref[:, 3 * width : 4 * width]).astype(jnp.bfloat16)
    units = [
        (window, group)
        for window in range(block // WIN)
        for group in range(width // GROUP_LANES)
    ]

    def cut(window, group, side):
        start = side * width + group * GROUP_LANES
        return slice(window * WIN, window * WIN + WIN), slice(start, start + GROUP_LANES)

    queries = [stack_heads(heads_ref[cut(w, g, 0)], masks_low) for w, g in units]
    grad_outs = [stack_heads(grad_mixed[cut(w, g, 0)], masks_low) for w, g in units]
    all_grad_probs = [
        dot_cols(heads_ref[cut(w, g, 2)], grad_out) for (w, g), grad_out in zip(units, grad_outs)
    ]
    cosines = [dot_cols(heads_ref[cut(w, g, 1)], query) for (w, g), query in zip(units, queries)]
    all_probs, grad_cosines = [], []
    for (window, group), grad_probs, cosine in zip(units, all_grad_probs, cosines):
        probs = probs_ref[window, group]
        all_probs.append(probs.astype(jnp.bfloat16))
        weighed = probs * grad_probs
        grad_scores = weighed - probs * jnp.sum(weighed, axis=0, keepdims=True)
        grad_bias_ref[group] += grad_scores
        grad_scale_ref[group] += jnp.sum(grad_scores * cosine, axis=0, keepdims=True)
        grad_cosines.append((grad_scores * scale_ref[group]).astype(jnp.bfloat16))
    for (w, g), probs, grad_out in zip(units, all_probs, grad_outs):
        grad_heads[cut(w, g, 2)] = dot(probs, grad_out)
    for (w, g), grad_cosine, query in zip(units, grad_cosines, queries):
        grad_heads[cut(w, g, 1)] = dot(grad_cosine, query)
    for (w, g), grad_cosine in zip(units, grad_cosines):
        grad_heads[cut(w, g, 0)] = pick_heads(
            dot_rows(grad_cosine, heads_ref[cut(w, g, 1)]), masks
        )
    for side in range(2):
        cut = slice(side * width, side * width + width)
        raw = raw_ref[:, cut]
        inverse = lax.rsqrt(head_sums(raw * raw) + 1e-06)
        unit = raw * inverse
        grad = grad_heads[:, cut]
        low_projected[:, cut] = (inverse * (grad - unit * head_sums(grad * unit))).astype(
            jnp.bfloat16
        )
    low_projected[:, 2 * width :] = grad_heads[:, 2 * width :].astype(jnp.bfloat16)
    grad_projected = low_projected[...]
    sums_ref[4:5, :width] += jnp.sum(
        grad_projected[:, :width].astype(jnp.float32), axis=0, keepdims=True
    )
    sums_ref[5:6, :width] += jnp.sum(
        grad_projected[:, 2 * width :].astype(jnp.float32), axis=0, keepdims=True
    )
    @pl.when(step == pl.num_programs(0) - 1)
    def _():
        sums_ref[2:4, :width] = expert_ref[1:3, :]
        for group in range(grad_scale_ref.shape[0]):
            at = SCALE_ROWS + group
            sums_ref[at : at + 1, : GROUP * WIN] = grad_scale_ref[group]
        net_back(
            sum_offsets(grad_bias_ref), table_ref[...], coords_ref[...], net_ref, sums_ref
        )


def sum_offsets(grad_bias_ref):
    row = lax.broadcasted_iota(jnp.int32, (GROUP * WIN, TABLE), 0)
    lane = lax.broadcasted_iota(jnp.int32, (GROUP * WIN, TABLE), 1)
    query = row % WIN
    aim = TABLE_MID - STRIDE * (query // SIDE) - query % SIDE
    spreads = [
        jnp.where((lane == aim) & (row // WIN == h), 1.0, 0.0).astype(jnp.bfloat16)
        for h in range(GROUP)
    ]
    sums = []
    for group in range(grad_bias_ref.shape[0]):
        grad = grad_bias_ref[group]
        high = grad.astype(jnp.bfloat16)
        rest = grad - high.astype(jnp.float32)
        middle = rest.astype(jnp.bfloat16)
        last = (rest - middle.astype(jnp.float32)).astype(jnp.bfloat16)
        parts = jnp.concatenate([high, middle, last], axis=0)
        for h in range(GROUP):
            spread = dot(parts, spreads[h])
            spread = spread[:WIN] + spread[WIN : 2 * WIN] + spread[2 * WIN :]
            rows = spread[:SIDE]
            for r in range(1, SIDE):
                rows = rows + pltpu.roll(spread[SIDE * r : SIDE * r + SIDE], STRIDE * r, 1)
            rows = pltpu.roll(rows, 0, 1, stride=1, stride_axis=0)
            sums.append(jnp.sum(rows, axis=0, keepdims=True))
    return jnp.concatenate(sums, axis=0)


def net_back(grad, table, coords, net_ref, sums_ref):
    heads = table.shape[0]
    second, shift, first = net_ref[:heads], net_ref[heads : heads + 1], net_ref[heads + 1 : heads + 3]
    pre = coords[:, 0:1] * first[0:1] + coords[:, 1:2] * first[1:2] + shift
    hidden, slope = gelu_pair(pre)
    grad_logits = grad * table * (1.0 - table * (1.0 / 16.0))
    sums_ref[SECOND_ROWS : SECOND_ROWS + heads, :] = jnp.dot(
        grad_logits, hidden, precision=highest, preferred_element_type=jnp.float32
    )
    grad_pre = slope * lax.dot_general(
        grad_logits, second, contract_rows, precision=highest, preferred_element_type=jnp.float32
    )
    sums_ref[SHIFT_ROW : SHIFT_ROW + 1, :] = jnp.sum(grad_pre, axis=0, keepdims=True)
    for k in range(2):
        sums_ref[FIRST_ROWS + k : FIRST_ROWS + k + 1, :] = jnp.sum(
            grad_pre * coords[:, k : k + 1], axis=0, keepdims=True
        )


def call_back(
    images, dest, arrived, cotangent, gathered, rows, scale, attended, raw, heads, probs,
    sums_expert, table, net,
):
    count, width = cotangent.shape
    block = token_block(count)
    groups = width // GROUP_LANES
    coords = jnp.asarray(offset_coords())
    return pl.pallas_call(
        back_kernel,
        grid=(count // block,),
        out_shape=(
            jax.ShapeDtypeStruct((count, width), jnp.float32),
            jax.ShapeDtypeStruct((count, width), jnp.bfloat16),
            jax.ShapeDtypeStruct((count, 3 * width), jnp.bfloat16),
            jax.ShapeDtypeStruct((SUM_ROWS, SUM_LANES), jnp.float32),
        ),
        in_specs=[
            pl.BlockSpec(memory_space=pltpu.SMEM),
            pl.BlockSpec((1, block), lambda i: (0, i)),
            whole(arrived.shape),
            by_rows(block, width),
            whole(gathered.shape),
            whole(rows.shape),
            whole(scale.shape),
            by_rows(block, width),
            by_rows(block, 2 * width),
            by_rows(block, 3 * width),
            pl.BlockSpec((block // WIN,) + probs.shape[1:], lambda i: (i, 0, 0, 0)),
            whole(sums_expert.shape),
            whole(table.shape),
            whole(coords.shape),
            whole(net.shape),
        ],
        out_specs=(
            by_rows(block, width),
            by_rows(block, width),
            by_rows(block, 3 * width),
            whole((SUM_ROWS, SUM_LANES)),
        ),
        scratch_shapes=[
            pltpu.VMEM((groups, WIN, GROUP * WIN), jnp.float32),
            pltpu.VMEM((groups, 1, GROUP * WIN), jnp.float32),
            pltpu.VMEM((block, 3 * width), jnp.float32),
        ],
        cost_estimate=pl.CostEstimate(
            flops=2 * count * width * width * 10, bytes_accessed=20 * 10**6, transcendentals=0
        ),
        compiler_params=pltpu.CompilerParams(vmem_limit_bytes=VMEM_MOST),
        name="back",
    )(
        images, dest, arrived, cotangent, gathered, rows, scale, attended, raw, heads, probs,
        sums_expert, table, coords, net,
    )


def dense_kernel(
    narrow,
    place_ref,
    tokens_ref,
    mixed_ref,
    attended_ref,
    projected_ref,
    expert_ref,
    send_ref,
    keep_ref,
):
    width = tokens_ref.shape[1]
    grad_dense = jnp.concatenate(
        [
            dot_rows(tokens_ref[...], projected_ref[...]),
            dot_rows(mixed_ref[...], attended_ref[...]),
        ],
        axis=1,
    )
    chips = keep_ref.shape[0]
    on_first = place_ref[0] == 0
    row = lax.broadcasted_iota(jnp.int32, (GROUP_LANES, width), 0)
    grad_route = jnp.where(row == place_ref[1], expert_ref[3:4, :], 0.0).T
    share = width // (2 * chips)
    for chip in range(chips):
        cuts = []
        for core in range(2):
            row = (chip // narrow * 2 * narrow + core * narrow + chip % narrow) * share
            rows, route = grad_dense[row : row + share], grad_route[row : row + share]
            halves = jnp.concatenate([rows[:, : 2 * width], rows[:, 2 * width :]], axis=0)
            route = jnp.concatenate([route, jnp.zeros_like(route)], axis=0)
            cuts.append(jnp.concatenate([halves, route], axis=1))
        keep_ref[chip] = jnp.where(on_first, cuts[0], cuts[1])
        send_ref[chip] = jnp.where(on_first, cuts[1], cuts[0]).astype(jnp.bfloat16)


def call_dense(tokens, mixed, attended, projected, sums_expert):
    count, width = tokens.shape
    narrow = lax.axis_size("narrow")
    chips = narrow * lax.axis_size("wide") // 2
    shape = (chips, width // chips, 2 * width + GROUP_LANES)
    place = jnp.stack([lax.axis_index("wide") % 2, lax.axis_index(("wide", "narrow"))])
    return pl.pallas_call(
        functools.partial(dense_kernel, narrow),
        out_shape=(
            jax.ShapeDtypeStruct(shape, jnp.bfloat16),
            jax.ShapeDtypeStruct(shape, jnp.float32),
        ),
        in_specs=[pl.BlockSpec(memory_space=pltpu.SMEM)]
        + [pl.BlockSpec(memory_space=pltpu.VMEM)] * 5,
        out_specs=(pl.BlockSpec(memory_space=pltpu.VMEM),) * 2,
        cost_estimate=pl.CostEstimate(
            flops=8 * count * width * width, bytes_accessed=7 * 10**6, transcendentals=0
        ),
        compiler_params=pltpu.CompilerParams(vmem_limit_bytes=VMEM_BYTES),
        name="dense",
    )(place.astype(jnp.int32), tokens, mixed, attended, projected, sums_expert)


def inputs_kernel(total_ref, projected_ref, weight_ref, out_ref):
    wide = projected_ref.shape[1]
    out_ref[...] = (
        total_ref[...] + dot_cols(projected_ref[...], weight_ref[:, :wide])
    ).astype(jnp.bfloat16)


def call_inputs(total, projected, gathered):
    count, width = total.shape
    block = token_block(count)
    return pl.pallas_call(
        inputs_kernel,
        grid=(count // block,),
        out_shape=jax.ShapeDtypeStruct((count, width), jnp.bfloat16),
        in_specs=[
            by_rows(block, width),
            by_rows(block, 3 * width),
            whole(gathered.shape),
        ],
        out_specs=by_rows(block, width),
        cost_estimate=pl.CostEstimate(
            flops=0, bytes_accessed=0, transcendentals=0
        ),
        compiler_params=pltpu.CompilerParams(vmem_limit_bytes=VMEM_BYTES),
        name="inputs",
    )(total, projected, gathered)


def layer_kernel(count_ref, dest_ref, branch_ref, section_ref, out_ref):
    block = out_ref.shape[0]
    place = lax.broadcasted_iota(jnp.int32, (block, 1), 0) + pl.program_id(0) * block
    live = jnp.where(place < count_ref[0] * IMG_TOK, 1.0, 0.0)
    branch = take_rows(dest_ref[...], branch_ref[...])
    out_ref[...] = ((section_ref[...] + branch) * live).astype(jnp.bfloat16)


def call_layer(images, dest, branch, section):
    count, width = section.shape
    block = token_block(count)
    return pl.pallas_call(
        layer_kernel,
        grid=(count // block,),
        out_shape=jax.ShapeDtypeStruct((count, width), jnp.bfloat16),
        in_specs=[
            pl.BlockSpec(memory_space=pltpu.SMEM),
            pl.BlockSpec((1, block), lambda i: (0, i)),
            whole(branch.shape),
            by_rows(block, width),
        ],
        out_specs=by_rows(block, width),
        cost_estimate=pl.CostEstimate(
            flops=0, bytes_accessed=0, transcendentals=0
        ),
        compiler_params=pltpu.CompilerParams(vmem_limit_bytes=VMEM_BYTES),
        name="layer",
    )(images, dest, branch, section)


def expert_kernel(
    rows_ref,
    cot_ref,
    first_ref,
    second_ref,
    bias_one_ref,
    vecs_ref,
    branch_ref,
    back_ref,
    hidden_ref,
    grad_pre_ref,
    grad_result_ref,
    sums_ref,
    sum_pre_ref,
):
    @pl.when(pl.program_id(0) == 0)
    def _():
        sums_ref[...] = jnp.zeros_like(sums_ref)
        sum_pre_ref[...] = jnp.zeros_like(sum_pre_ref)

    bias_two, gain, shift, route = (vecs_ref[i : i + 1, :] for i in range(4))
    count = rows_ref.shape[0]
    size = count // EXPERT_PARTS
    cuts = [slice(start, start + size) for start in range(0, count, size)]
    pres = [dot(rows_ref[cut, :], first_ref[...]) + bias_one_ref[...] for cut in cuts]
    pairs = [gelu_pair(pre) for pre in pres]
    hiddens = [hidden.astype(jnp.bfloat16) for hidden, _ in pairs]
    raws = [dot(hidden, second_ref[...]) + bias_two for hidden in hiddens]
    grads = []
    for cut, hidden, raw in zip(cuts, hiddens, raws):
        hidden_ref[cut, :] = hidden
        rows = rows_ref[cut, :].astype(jnp.float32)
        result = raw.astype(jnp.bfloat16).astype(jnp.float32)
        gating = jax.nn.sigmoid(jnp.sum(rows * route, axis=-1, keepdims=True))
        centred = result - jnp.mean(result, axis=-1, keepdims=True)
        spread = lax.rsqrt(jnp.mean(centred * centred, axis=-1, keepdims=True) + 1e-05)
        unit = centred * spread
        normed = unit * gain + shift
        branch_ref[cut, :] = (normed * gating).astype(jnp.bfloat16)
        cot = cot_ref[cut, :].astype(jnp.float32)
        grad_gate = jnp.sum(cot * normed, axis=-1, keepdims=True)
        gated = cot * gating
        grad_unit = gated * gain
        grad_result = (
            spread
            * (
                grad_unit
                - jnp.mean(grad_unit, axis=-1, keepdims=True)
                - unit * jnp.mean(grad_unit * unit, axis=-1, keepdims=True)
            )
        ).astype(jnp.bfloat16)
        grad_result_ref[cut, :] = grad_result
        grad_logit = (
            (grad_gate * gating * (1.0 - gating)).astype(jnp.bfloat16).astype(jnp.float32)
        )
        sums_ref[0:1, :] += jnp.sum(grad_result.astype(jnp.float32), axis=0, keepdims=True)
        sums_ref[1:2, :] += jnp.sum(gated * unit, axis=0, keepdims=True)
        sums_ref[2:3, :] += jnp.sum(gated, axis=0, keepdims=True)
        sums_ref[3:4, :] += jnp.sum(rows * grad_logit, axis=0, keepdims=True)
        grads.append((grad_result, grad_logit))
    grad_hiddens = [dot_cols(grad, second_ref[...]) for grad, _ in grads]
    grad_pres = [
        (grad * slope).astype(jnp.bfloat16) for grad, (_, slope) in zip(grad_hiddens, pairs)
    ]
    for cut, grad_pre, (_, grad_logit) in zip(cuts, grad_pres, grads):
        grad_pre_ref[cut, :] = grad_pre
        sum_pre_ref[...] += jnp.sum(grad_pre.astype(jnp.float32), axis=0, keepdims=True)
        back_ref[cut, :] = (dot_cols(grad_pre, first_ref[...]) + grad_logit * route).astype(
            jnp.bfloat16
        )


def call_expert(rows, cot, first, second, bias_one, vecs):
    count, width = rows.shape
    ff = first.shape[1]
    block = math.gcd(count, 640)
    return pl.pallas_call(
        expert_kernel,
        grid=(count // block,),
        out_shape=(
            jax.ShapeDtypeStruct((count, width), jnp.bfloat16),
            jax.ShapeDtypeStruct((count, width), jnp.bfloat16),
            jax.ShapeDtypeStruct((count, ff), jnp.bfloat16),
            jax.ShapeDtypeStruct((count, ff), jnp.bfloat16),
            jax.ShapeDtypeStruct((count, width), jnp.bfloat16),
            jax.ShapeDtypeStruct((8, width), jnp.float32),
            jax.ShapeDtypeStruct((1, ff), jnp.float32),
        ),
        in_specs=[
            by_rows(block, width),
            by_rows(block, width),
            whole(first.shape),
            whole(second.shape),
            whole(bias_one.shape),
            whole(vecs.shape),
        ],
        out_specs=(
            by_rows(block, width),
            by_rows(block, width),
            by_rows(block, ff),
            by_rows(block, ff),
            by_rows(block, width),
            whole((8, width)),
            whole((1, ff)),
        ),
        cost_estimate=pl.CostEstimate(
            flops=8 * count * width * ff, bytes_accessed=16 * 10**6, transcendentals=count * ff
        ),
        compiler_params=pltpu.CompilerParams(vmem_limit_bytes=VMEM_MOST),
        name="expert",
    )(rows, cot, first, second, bias_one, vecs)


def offset_coords():
    place = TABLE_MID - np.arange(TABLE)
    row = (place + STRIDE // 2 - 1) // STRIDE
    coords = np.stack([row, place - STRIDE * row], axis=1) * (8.0 / (SIDE - 1))
    return (np.sign(coords) * np.log2(np.abs(coords) + 1.0) / 3.0).astype(np.float32)


def bias_table(params):
    piece_collection = pieces(params)
    hidden = jax.nn.gelu(
        jnp.dot(offset_coords(), piece_collection[9], precision=highest) + piece_collection[8]
    )
    return 16.0 * jax.nn.sigmoid(jnp.dot(hidden, piece_collection[10], precision=highest)).T


def spread_bias(table):
    places = jnp.arange(WIN, dtype=jnp.int32)
    coded = STRIDE * (places // SIDE) + places % SIDE
    index = TABLE_MID + coded[:, None] - coded[None, :]
    lookup = (index.reshape(1, -1) == jnp.arange(TABLE, dtype=jnp.int32)[:, None]).astype(
        table.dtype
    )
    bias = jnp.dot(table, lookup, precision=highest).reshape(-1, GROUP, WIN, WIN)
    return bias.transpose(0, 2, 1, 3).reshape(-1, WIN, GROUP * WIN)


def per_device_split(
    tokens,
    cotangent,
    routes,
    images,
    dense_weight,
    dense_moment,
    dense_square,
    small_params,
    small_moment,
    small_square,
    inner_weight,
    inner_moment,
    inner_square,
    outer_weight,
    outer_moment,
    outer_square,
    expert_bias,
    bias_moment,
    bias_square,
):
    slices = lax.axis_size(("wide", "narrow"))
    split = slices // EXPERTS
    member = lax.axis_index(("wide", "narrow")) % split
    piece = MODEL_WIDTH // split
    ff_dev = inner_weight.shape[2]
    tok_rows = tokens.shape[0]
    capacity = (5 * tok_rows + 4 * EXPERTS - 1) // (4 * EXPERTS)
    slot_total = EXPERTS * capacity
    route_ids = routes[:, 0]
    live_rows, kept_rows, dest_slot = assign(route_ids, images[0], EXPERTS, capacity)
    live_f = live_rows.astype(jnp.float32)
    keep_f = kept_rows.astype(jnp.float32)
    clipped = jnp.minimum(dest_slot, slot_total - 1)
    gathered = gather_rows(dense_weight.astype(jnp.bfloat16))
    section_one, gating, expert_feed, kept = front_forward_split(
        tokens, gathered, small_params, route_ids
    )

    def fan_out(rows_value):
        placed_rows = (
            jnp.zeros((slot_total, MODEL_WIDTH), jnp.bfloat16)
            .at[dest_slot]
            .set(rows_value.astype(jnp.bfloat16), mode="drop")
        )
        copies = jnp.broadcast_to(
            placed_rows.reshape(EXPERTS, 1, capacity, MODEL_WIDTH),
            (EXPERTS, split, capacity, MODEL_WIDTH),
        )
        return trade_rows(copies.reshape(slices, capacity, MODEL_WIDTH)).reshape(
            slices * capacity, MODEL_WIDTH
        )

    def fan_in(partials):
        arrived = trade_rows(partials.reshape(slices, capacity, MODEL_WIDTH))
        summed = jnp.sum(
            arrived.reshape(EXPERTS, split, capacity, MODEL_WIDTH).astype(jnp.float32), axis=1
        ).reshape(slot_total, MODEL_WIDTH)
        return jnp.take(summed, clipped, axis=0) * keep_f[:, None]

    expert_rows = fan_out(expert_feed)
    first_matrix = inner_weight[0].astype(jnp.bfloat16)
    second_matrix = outer_weight[0].astype(jnp.bfloat16)
    pre_act = (
        jnp.dot(expert_rows, first_matrix, preferred_element_type=jnp.float32)
        + expert_bias[0, :ff_dev]
    )
    hidden = jax.nn.gelu(pre_act).astype(jnp.bfloat16)
    out_bias = lax.dynamic_update_slice(
        jnp.zeros((MODEL_WIDTH,), jnp.float32), expert_bias[0, ff_dev:], (member * piece,)
    )
    result = (jnp.dot(hidden, second_matrix, preferred_element_type=jnp.float32) + out_bias).astype(
        jnp.bfloat16
    )
    combined = fan_in(result)

    def tail_local(section_value, gate_value, combined_value, params):
        return finish_block(section_value, gate_value, combined_value, keep_f, live_f, params)

    layer_value, tail_back = jax.vjp(tail_local, section_one, gating, combined, small_params)
    grad_section, grad_gate, grad_combined, grad_small_tail = tail_back(
        cotangent.astype(jnp.float32)
    )
    grad_result = fan_out(grad_combined)
    grad_outer = lax.dot_general(
        hidden, grad_result, contract_rows, preferred_element_type=jnp.float32
    )
    grad_hidden = lax.dot_general(
        grad_result, second_matrix, contract_cols, preferred_element_type=jnp.float32
    )
    gelu_back = jax.vjp(jax.nn.gelu, pre_act)[1]
    grad_pre = gelu_back(grad_hidden)[0].astype(jnp.bfloat16)
    grad_inner = lax.dot_general(
        expert_rows, grad_pre, contract_rows, preferred_element_type=jnp.float32
    )
    column_total = jnp.sum(grad_result.astype(jnp.float32), axis=0)
    grad_bias = jnp.concatenate(
        [
            jnp.sum(grad_pre.astype(jnp.float32), axis=0),
            lax.dynamic_slice_in_dim(column_total, member * piece, piece, 0),
        ]
    )
    grad_rows = lax.dot_general(
        grad_pre, first_matrix, contract_cols, preferred_element_type=jnp.float32
    ).astype(jnp.bfloat16)
    grad_feed = fan_in(grad_rows)
    grad_inputs, grad_weights, grad_small_front = front_backward_split(
        tokens, gathered, small_params, kept, grad_section, grad_gate, grad_feed
    )
    grad_small = grad_small_front + grad_small_tail
    grad_dense, grad_small = sum_grads(grad_weights, grad_small)
    dense_out = adamw_step(
        dense_weight, grad_dense, dense_moment, dense_square, dense_rate, weight_decay
    )
    small_out = adamw_step(small_params, grad_small, small_moment, small_square, small_rate, 0.0)
    inner_out = adamw_step(
        inner_weight, grad_inner[None], inner_moment, inner_square, expert_rate, weight_decay
    )
    outer_out = adamw_step(
        outer_weight, grad_outer[None], outer_moment, outer_square, expert_rate, weight_decay
    )
    bias_out = adamw_step(expert_bias, grad_bias[None], bias_moment, bias_square, expert_rate, 0.0)
    return (
        layer_value.astype(jnp.bfloat16),
        grad_inputs.astype(jnp.bfloat16),
        dense_out[0],
        dense_out[1],
        dense_out[2],
        small_out[0],
        small_out[1],
        small_out[2],
        inner_out[0],
        inner_out[1],
        inner_out[2],
        inner_out[0].astype(jnp.bfloat16),
        outer_out[0],
        outer_out[1],
        outer_out[2],
        outer_out[0].astype(jnp.bfloat16),
        bias_out[0],
        bias_out[1],
        bias_out[2],
    )


def per_device(
    tokens,
    cotangent,
    routes,
    images,
    dense_weight,
    dense_moment,
    dense_square,
    small_params,
    small_moment,
    small_square,
    inner_weight,
    inner_moment,
    inner_square,
    outer_weight,
    outer_moment,
    outer_square,
    expert_bias,
    bias_moment,
    bias_square,
):
    slices = lax.axis_size(("wide", "narrow"))
    if slices != EXPERTS:
        return per_device_split(
            tokens,
            cotangent,
            routes,
            images,
            dense_weight,
            dense_moment,
            dense_square,
            small_params,
            small_moment,
            small_square,
            inner_weight,
            inner_moment,
            inner_square,
            outer_weight,
            outer_moment,
            outer_square,
            expert_bias,
            bias_moment,
            bias_square,
        )
    expert = lax.axis_index(("wide", "narrow"))
    ff_dev = inner_weight.shape[2]
    tok_rows = tokens.shape[0]
    capacity = (5 * tok_rows + 4 * EXPERTS - 1) // (4 * EXPERTS)
    slot_total = EXPERTS * capacity

    def trade(rows):
        traded = trade_rows(rows.reshape(slices, capacity, MODEL_WIDTH))
        return traded.reshape(slot_total, MODEL_WIDTH)

    scale_at = 7 * MODEL_WIDTH
    share = dense_weight.astype(jnp.bfloat16)
    across, *deep = axis_bits("narrow")
    held = join_quad(share, deep)
    held = join(held, across, -2)
    held, route_ids, cot = lax.optimization_barrier((held, routes, cotangent))
    dest, placed_cot = call_assign(images, route_ids, cot, capacity)
    cot_rows = trade(placed_cot)
    core, *rest = axis_bits("wide")
    for step in rest:
        held = join(held, step)
    held, params = lax.optimization_barrier((held, small_params))
    gathered = join(held, core, len(rest)).reshape(-1, share.shape[-1])
    table = bias_table(params)
    net_pieces = pieces(params)
    net = jnp.concatenate([net_pieces[10].T, net_pieces[8][None, :], net_pieces[9]])
    vectors = params[:scale_at].reshape(7, MODEL_WIDTH)
    scale_heads = jnp.exp(params[scale_at : scale_at + ATTENTION_HEADS])
    scale = jnp.repeat(scale_heads, WIN).reshape(-1, 1, GROUP * WIN)
    bias = spread_bias(table)
    placed, section, attended, mixed, raw, heads, probs = call_front(
        dest, tokens, gathered, vectors, scale, bias, capacity
    )
    placed, cot_rows = lax.optimization_barrier((placed, cot_rows))
    expert_rows = trade(placed)
    first_matrix = inner_weight[0].astype(jnp.bfloat16)
    second_matrix = outer_weight[0].astype(jnp.bfloat16)
    route_row = lax.dynamic_slice_in_dim(gathered, 4 * MODEL_WIDTH + expert, 1, 1)
    vecs = jnp.concatenate(
        [expert_bias[:, ff_dev:], vectors[2:4], route_row.astype(jnp.float32).reshape(1, -1)]
    )
    branch, grad_rows, hidden, grad_pre, grad_result, sums_expert, sum_pre = call_expert(
        expert_rows, cot_rows, first_matrix, second_matrix, expert_bias[:, :ff_dev], vecs
    )
    arrived = trade(grad_rows)
    grad_outer = dot_rows(hidden, grad_result)
    grad_inner = dot_rows(expert_rows, grad_pre)
    grad_bias = jnp.concatenate([sum_pre, sums_expert[0:1]], axis=1)[0]
    inner_out = adamw_step(
        inner_weight, grad_inner[None], inner_moment, inner_square, expert_rate, weight_decay
    )
    outer_out = adamw_step(
        outer_weight, grad_outer[None], outer_moment, outer_square, expert_rate, weight_decay
    )
    inner_out += (inner_out[0].astype(jnp.bfloat16),)
    outer_out += (outer_out[0].astype(jnp.bfloat16),)
    branch, arrived, inner_out, outer_out = lax.optimization_barrier(
        (branch, arrived, inner_out, outer_out)
    )
    branch_rows = trade(branch)
    total, low_attended, low_projected, sums = call_back(
        images,
        dest,
        arrived,
        cotangent,
        gathered,
        vectors,
        scale,
        attended,
        raw,
        heads,
        probs,
        sums_expert,
        table,
        net,
    )
    send, keep = call_dense(tokens, mixed, low_attended, low_projected, sums_expert)
    grad_inputs = call_inputs(total, low_projected, gathered)
    held = sum_chip(send, keep)
    narrow = lax.axis_size("narrow")
    sums = sums + swap_flat(sums, narrow)
    held, sums, branch_rows = lax.optimization_barrier((held, sums, branch_rows))
    grad_dense = sum_shares(held)
    sums = sum_quads(sum_quads(sums, 2, 4), 1, 2 * narrow)
    layer_out = call_layer(images, dest, branch_rows, section)
    share_rows = dense_weight.shape[0]
    half = 2 * MODEL_WIDTH
    grad_dense = jnp.concatenate(
        [
            grad_dense[:share_rows, :half],
            grad_dense[share_rows:, :half],
            grad_dense[:share_rows, half : half + EXPERTS],
        ],
        axis=1,
    )
    grad_scale = sums[SCALE_ROWS : SCALE_ROWS + ATTENTION_HEADS // GROUP, : GROUP * WIN]
    grad_small = jnp.concatenate(
        [
            sums[:7, :MODEL_WIDTH].reshape(-1),
            jnp.sum(grad_scale.reshape(ATTENTION_HEADS, WIN), axis=1) * scale_heads,
            sums[SHIFT_ROW : FIRST_ROWS + 2].reshape(-1),
            sums[SECOND_ROWS : SECOND_ROWS + ATTENTION_HEADS].T.reshape(-1),
        ]
    )
    dense_out = adamw_step(
        dense_weight, grad_dense, dense_moment, dense_square, dense_rate, weight_decay
    )
    small_out = adamw_step(small_params, grad_small, small_moment, small_square, small_rate, 0.0)
    bias_out = adamw_step(expert_bias, grad_bias[None], bias_moment, bias_square, expert_rate, 0.0)
    return (
        layer_out,
        grad_inputs,
        dense_out[0],
        dense_out[1],
        dense_out[2],
        small_out[0],
        small_out[1],
        small_out[2],
        inner_out[0],
        inner_out[1],
        inner_out[2],
        inner_out[3],
        outer_out[0],
        outer_out[1],
        outer_out[2],
        outer_out[3],
        bias_out[0],
        bias_out[1],
        bias_out[2],
    )


def solution(mesh):
    return jax.shard_map(
        per_device,
        mesh=mesh,
        in_specs=(
            P(("wide", "narrow"), None),
            P(("wide", "narrow"), None),
            P(("wide", "narrow"), None),
            P(("wide", "narrow")),
            P(("wide", "narrow"), None),
            P(("wide", "narrow"), None),
            P(("wide", "narrow"), None),
            P(),
            P(),
            P(),
            P(("wide", "narrow"), None, None),
            P(("wide", "narrow"), None, None),
            P(("wide", "narrow"), None, None),
            P(("wide", "narrow"), None, None),
            P(("wide", "narrow"), None, None),
            P(("wide", "narrow"), None, None),
            P(("wide", "narrow"), None),
            P(("wide", "narrow"), None),
            P(("wide", "narrow"), None),
        ),
        out_specs=(
            P(("wide", "narrow"), None),
            P(("wide", "narrow"), None),
            P(("wide", "narrow"), None),
            P(("wide", "narrow"), None),
            P(("wide", "narrow"), None),
            P(),
            P(),
            P(),
            P(("wide", "narrow"), None, None),
            P(("wide", "narrow"), None, None),
            P(("wide", "narrow"), None, None),
            P(("wide", "narrow"), None, None),
            P(("wide", "narrow"), None, None),
            P(("wide", "narrow"), None, None),
            P(("wide", "narrow"), None, None),
            P(("wide", "narrow"), None, None),
            P(("wide", "narrow"), None),
            P(("wide", "narrow"), None),
            P(("wide", "narrow"), None),
        ),
        check_vma=False,
    )
```

```python
import functools
import math

import jax
import jax.numpy as jnp
import numpy as np
from jax import lax
from jax.experimental import pallas as pl
from jax.experimental.pallas import tpu as pltpu
from jax.sharding import PartitionSpec as P

MODEL_WIDTH = 384
ATTENTION_HEADS = 12
HEAD_DIM = 32
BIAS_NET_HIDDEN = 512
EXPERTS = 32
SIDE = 8
IMG_TOK = 1024
STEP = 10
WIN = 64
GROUP = 4
GROUP_LANES = 128
VMEM_BYTES = 48 * 2**20
VMEM_MOST = 62 * 2**20
EXPERT_PARTS = 2
TABLE = 256
TABLE_MID = 119
STRIDE = 16
SUM_LANES = BIAS_NET_HIDDEN
SECOND_ROWS = 8
SHIFT_ROW = 20
FIRST_ROWS = 21
SCALE_ROWS = 24
SUM_ROWS = 32


highest = lax.Precision.HIGHEST
beta_one = 0.9
beta_two = 0.999
epsilon = 1e-08
dense_rate = 0.05
expert_rate = 0.05
small_rate = 0.3
weight_decay = 0.05
contract_rows = (((0,), (0,)), ((), ()))
contract_cols = (((1,), (1,)), ((), ()))


def pieces(small_params):
    length_list = (
        MODEL_WIDTH,
        MODEL_WIDTH,
        MODEL_WIDTH,
        MODEL_WIDTH,
        MODEL_WIDTH,
        MODEL_WIDTH,
        MODEL_WIDTH,
        ATTENTION_HEADS,
        BIAS_NET_HIDDEN,
        2 * BIAS_NET_HIDDEN,
        BIAS_NET_HIDDEN * ATTENTION_HEADS,
    )
    piece_collection = []
    offset = 0
    for length in length_list:
        piece_collection.append(small_params[offset : offset + length])
        offset = offset + length
    piece_collection[9] = piece_collection[9].reshape(2, BIAS_NET_HIDDEN)
    piece_collection[10] = piece_collection[10].reshape(BIAS_NET_HIDDEN, ATTENTION_HEADS)
    return piece_collection


def norm_rows(values, gain, shift):
    average = jnp.mean(values, axis=-1, keepdims=True)
    centred = values - average
    variance = jnp.mean(centred * centred, axis=-1, keepdims=True)
    return centred * lax.rsqrt(variance + 1e-05) * gain + shift


def position_bias(small_params):
    piece_collection = pieces(small_params)
    span = 2 * SIDE - 1
    offsets = jnp.arange(span, dtype=jnp.float32) - (SIDE - 1)
    coords = jnp.stack([jnp.repeat(offsets, span), jnp.tile(offsets, span)], axis=1) * (
        8.0 / (SIDE - 1)
    )
    coords = jnp.sign(coords) * jnp.log2(jnp.abs(coords) + 1.0) / 3.0
    hidden = jax.nn.gelu(
        jnp.dot(coords, piece_collection[9], precision=highest) + piece_collection[8]
    )
    table = 16.0 * jax.nn.sigmoid(jnp.dot(hidden, piece_collection[10], precision=highest))
    places = jnp.arange(WIN, dtype=jnp.int32)
    row_pos = places // SIDE
    col_pos = places % SIDE
    index = (row_pos[:, None] - row_pos[None, :] + SIDE - 1) * span + (
        col_pos[:, None] - col_pos[None, :] + SIDE - 1
    )
    lookup = (index.reshape(-1, 1) == jnp.arange(span * span, dtype=jnp.int32)[None, :]).astype(
        table.dtype
    )
    spread = jnp.dot(lookup, table, precision=highest)
    return spread.T.reshape(ATTENTION_HEADS, WIN, WIN)


def matmul_back(left_low, right_low, grad_low):
    grad_left = lax.dot_general(
        grad_low, right_low, contract_cols, preferred_element_type=jnp.float32
    )
    grad_right = lax.dot_general(
        left_low, grad_low, contract_rows, preferred_element_type=jnp.float32
    )
    return (grad_left, grad_right)


def add_joined_bias(raw, params):
    piece_collection = pieces(params)
    return raw + jnp.concatenate(
        [piece_collection[4], jnp.zeros_like(piece_collection[4]), piece_collection[5]]
    )


def add_out_bias(raw, params):
    return raw + pieces(params)[6]


def normalize_heads(projected):
    window_count = projected.shape[0] // WIN
    shaped = projected.reshape(window_count, WIN, 3, ATTENTION_HEADS, HEAD_DIM)
    queries = shaped[:, :, 0]
    key_vecs = shaped[:, :, 1]
    queries = queries * lax.rsqrt(jnp.sum(queries * queries, axis=-1, keepdims=True) + 1e-06)
    key_vecs = key_vecs * lax.rsqrt(jnp.sum(key_vecs * key_vecs, axis=-1, keepdims=True) + 1e-06)
    return (queries, key_vecs, shaped[:, :, 2])


def softmax_part(cosine, params):
    scale = jnp.exp(pieces(params)[7])[:, None, None]
    return jax.nn.softmax(cosine * scale + position_bias(params), axis=-1)


def front_forward_split(tokens_low, weights_low, params, route_ids):
    rows_here = tokens_low.shape[0]
    qkv_low = weights_low[:, : 3 * MODEL_WIDTH]
    out_low = weights_low[:, 3 * MODEL_WIDTH : 4 * MODEL_WIDTH]
    route_low = weights_low[:, 4 * MODEL_WIDTH :]
    raw_qkv = jnp.dot(tokens_low, qkv_low, preferred_element_type=jnp.float32)
    projected = add_joined_bias(raw_qkv, params)
    q_f, k_f, v_f = normalize_heads(projected)
    q_low = q_f.astype(jnp.bfloat16)
    k_low = k_f.astype(jnp.bfloat16)
    v_low = v_f.astype(jnp.bfloat16)
    cosine = jnp.einsum("wihd,wjhd->whij", q_low, k_low, preferred_element_type=jnp.float32)
    probs = softmax_part(cosine, params)
    probs_low = probs.astype(jnp.bfloat16)
    mixed_low = (
        jnp.einsum("whij,wjhd->wihd", probs_low, v_low, preferred_element_type=jnp.float32)
        .astype(jnp.bfloat16)
        .reshape(rows_here, MODEL_WIDTH)
    )
    attended = add_out_bias(jnp.dot(mixed_low, out_low, preferred_element_type=jnp.float32), params)
    piece_collection = pieces(params)
    section_one = tokens_low.astype(jnp.float32) + norm_rows(
        attended, piece_collection[0], piece_collection[1]
    )
    section_low = section_one.astype(jnp.bfloat16)
    logits = jnp.dot(section_low, route_low, preferred_element_type=jnp.float32)
    chosen_mask = (
        route_ids[:, None] == jnp.arange(logits.shape[1], dtype=jnp.int32)[None, :]
    ).astype(jnp.float32)
    gating = jax.nn.sigmoid(jnp.sum(logits * chosen_mask, axis=1))
    kept = (
        projected,
        q_low,
        k_low,
        v_low,
        cosine,
        probs_low,
        mixed_low,
        attended,
        section_low,
        logits,
        chosen_mask,
    )
    return (section_one, gating, section_low, kept)


def front_backward_split(tokens_low, weights_low, params, kept, grad_section, grad_gate, grad_feed):
    (
        projected,
        q_low,
        k_low,
        v_low,
        cosine,
        probs_low,
        mixed_low,
        attended,
        section_low,
        logits,
        chosen_mask,
    ) = kept
    rows_here = tokens_low.shape[0]
    window_count = rows_here // WIN
    qkv_low = weights_low[:, : 3 * MODEL_WIDTH]
    out_low = weights_low[:, 3 * MODEL_WIDTH : 4 * MODEL_WIDTH]
    route_low = weights_low[:, 4 * MODEL_WIDTH :]

    def gate_part(logit_values):
        return jax.nn.sigmoid(jnp.sum(logit_values * chosen_mask, axis=1))

    gate_back = jax.vjp(gate_part, logits)[1]
    grad_logits = gate_back(grad_gate)[0].astype(jnp.bfloat16)
    grad_from_route, grad_route = matmul_back(section_low, route_low, grad_logits)
    grad_total = grad_section + grad_feed + grad_from_route

    def section_part(attended_value, params_value):
        piece_collection = pieces(params_value)
        return norm_rows(attended_value, piece_collection[0], piece_collection[1])

    section_back = jax.vjp(section_part, attended, params)[1]
    grad_attended, grad_params_a = section_back(grad_total)
    grad_att_low = grad_attended.astype(jnp.bfloat16)
    grad_params_b = jax.vjp(add_out_bias, jnp.zeros_like(attended), params)[1](
        grad_att_low.astype(jnp.float32)
    )[1]
    grad_mixed, grad_out = matmul_back(mixed_low, out_low, grad_att_low)
    grad_mixed_low = grad_mixed.astype(jnp.bfloat16).reshape(
        window_count, WIN, ATTENTION_HEADS, HEAD_DIM
    )
    grad_probs = jnp.einsum(
        "wihd,wjhd->whij", grad_mixed_low, v_low, preferred_element_type=jnp.float32
    )
    grad_v = jnp.einsum(
        "whij,wihd->wjhd", probs_low, grad_mixed_low, preferred_element_type=jnp.float32
    )
    soft_back = jax.vjp(softmax_part, cosine, params)[1]
    grad_cosine, grad_params_c = soft_back(grad_probs)
    grad_cos_low = grad_cosine.astype(jnp.bfloat16)
    grad_q = jnp.einsum("whij,wjhd->wihd", grad_cos_low, k_low, preferred_element_type=jnp.float32)
    grad_k = jnp.einsum("whij,wihd->wjhd", grad_cos_low, q_low, preferred_element_type=jnp.float32)
    norm_back = jax.vjp(normalize_heads, projected)[1]
    grad_projected = norm_back((grad_q, grad_k, grad_v))[0]
    grad_proj_low = grad_projected.astype(jnp.bfloat16)
    grad_params_d = jax.vjp(add_joined_bias, jnp.zeros_like(projected), params)[1](
        grad_proj_low.astype(jnp.float32)
    )[1]
    grad_tokens, grad_qkv = matmul_back(tokens_low, qkv_low, grad_proj_low)
    grad_inputs = grad_total + grad_tokens
    grad_weights = jnp.concatenate([grad_qkv, grad_out, grad_route], axis=1)
    grad_params = grad_params_a + grad_params_b + grad_params_c + grad_params_d
    return (grad_inputs, grad_weights, grad_params)


def finish_block(section_one, gating, combined, kept_rows, live_rows, small_params):
    piece_collection = pieces(small_params)
    branch = (
        norm_rows(combined, piece_collection[2], piece_collection[3])
        * (gating * kept_rows)[:, None]
    )
    return (section_one + branch) * live_rows[:, None]


def assign(route_ids, count, experts, capacity):
    places = jnp.arange(route_ids.shape[0], dtype=jnp.int32)
    live_rows = places // IMG_TOK < count
    chosen = (
        (route_ids[:, None] == jnp.arange(experts, dtype=jnp.int32)[None, :]) & live_rows[:, None]
    ).astype(jnp.int32)
    before = jnp.cumsum(chosen, axis=0) - chosen
    slot = jnp.sum(before * chosen, axis=1)
    kept_rows = live_rows & (slot < capacity)
    dest_slot = jnp.where(kept_rows, route_ids * capacity + slot, experts * capacity)
    return (live_rows, kept_rows, dest_slot)


def adamw_step(weight, gradient, first, second, rate, decay):
    first_new = beta_one * first + (1.0 - beta_one) * gradient
    second_new = beta_two * second + (1.0 - beta_two) * gradient * gradient
    first_hat = first_new / (1.0 - beta_one**STEP)
    second_hat = second_new / (1.0 - beta_two**STEP)
    weight_new = weight - rate * (first_hat / (jnp.sqrt(second_hat) + epsilon) + decay * weight)
    return (weight_new, first_new, second_new)


def trade_rows(payload):
    arrived_rows = lax.all_to_all(
        payload, ("wide", "narrow"), split_axis=0, concat_axis=0, tiled=True
    )
    return arrived_rows


def axis_bits(axis):
    size = lax.axis_size(axis)
    return [(axis, 1 << k) for k in range(size.bit_length() - 1)]


def swap(value, step):
    axis, offset = step
    return lax.ppermute(value, axis, [(i, i ^ offset) for i in range(lax.axis_size(axis))])


def upper(step):
    axis, offset = step
    return (lax.axis_index(axis) & offset) > 0


def gather_rows(share):
    steps = axis_bits("narrow") + axis_bits("wide")
    first, rest = steps[0], steps[1:]
    other = swap(share, first)
    block = jnp.where(
        upper(first), jnp.concatenate([other, share]), jnp.concatenate([share, other])
    )
    held = block
    done = []
    core = ("wide", 1)
    for step in [s for s in rest if s != core] + [core]:
        place = sum(1 for d in done if rest.index(d) > rest.index(step))
        other = swap(held, step)
        held = jnp.where(
            upper(step), jnp.stack([other, held], place), jnp.stack([held, other], place)
        )
        done.append(step)
    return held.reshape(-1, share.shape[1])


def sum_grads(partial, small):
    steps = axis_bits("narrow") + axis_bits("wide")
    first, rest = steps[0], steps[1:]
    core = ("wide", 1)
    order = [core] + [s for s in rest[::-1] if s != core]
    count = lax.axis_size(("wide", "narrow"))
    share = partial.shape[0] // count
    held = partial.reshape((2,) * len(rest) + (2 * share, partial.shape[1]))
    left = rest[::-1]
    for step in order:
        place = left.index(step)
        side = upper(step).astype(jnp.int32)
        send = lax.dynamic_index_in_dim(held, 1 - side, place, keepdims=False)
        keep = lax.dynamic_index_in_dim(held, side, place, keepdims=False)
        other = swap(send.astype(jnp.bfloat16), step)
        small = small + swap(small, step)
        held = keep + other.astype(jnp.float32)
        left = [s for s in left if s != step]
    side = upper(first)
    send = jnp.where(side, held[:share], held[share:])
    keep = jnp.where(side, held[share:], held[:share])
    other = swap(send.astype(jnp.bfloat16), first)
    small = small + swap(small, first)
    return keep + other.astype(jnp.float32), small


def join(held, step, axis=None):
    other = swap(held, step)
    if axis is None or axis >= 0:
        both = functools.partial(jnp.stack, axis=axis or 0)
    else:
        both = functools.partial(jnp.concatenate, axis=axis)
    return jnp.where(upper(step), both([other, held]), both([held, other]))


def join_quad(held, steps):
    axis, low = steps[0]
    high = steps[1][1]
    near, far, last = (swap(held, (axis, offset)) for offset in (low, high, low + high))
    ahead = upper(steps[1])
    blocks = [
        jnp.where(ahead, second, first)
        for first, second in ((held, far), (near, last), (far, held), (last, near))
    ]
    return jnp.where(
        upper(steps[0]),
        jnp.stack([blocks[1], blocks[0], blocks[3], blocks[2]]),
        jnp.stack(blocks),
    )


def swap_flat(value, offset):
    axes = ("wide", "narrow")
    return lax.ppermute(value, axes, [(i, i ^ offset) for i in range(lax.axis_size(axes))])


def sum_quads(small, low, high):
    near = small + swap_flat(small, low)
    return near + (swap_flat(small, high) + swap_flat(small, low + high))


def sum_chip(send, keep):
    return (keep + swap(send, ("wide", 1)).astype(jnp.float32)).astype(jnp.bfloat16)


def sum_shares(held):
    wide, narrow = lax.axis_size("wide"), lax.axis_size("narrow")
    groups = [
        [w * narrow + n for w in range(core, wide, 2) for n in range(narrow)] for core in range(2)
    ]
    arrived = lax.all_to_all(held, ("wide", "narrow"), 0, 0, axis_index_groups=groups, tiled=True)
    return jnp.sum(arrived.astype(jnp.float32), axis=0)


def lane_masks(dtype):
    lane = lax.broadcasted_iota(jnp.int32, (1, GROUP_LANES), 1) // HEAD_DIM
    return [(lane == h).astype(jnp.float32).astype(dtype) for h in range(GROUP)]


def dot(left, right):
    return jnp.dot(left, right, preferred_element_type=jnp.float32)


def dot_cols(left, right):
    return lax.dot_general(left, right, contract_cols, preferred_element_type=jnp.float32)


def dot_rows(left, right):
    return lax.dot_general(left, right, contract_rows, preferred_element_type=jnp.float32)


def stack_heads(rows, masks):
    return jnp.concatenate([rows * m for m in masks], axis=0)


def pick_heads(blocks, masks):
    n = blocks.shape[0] // GROUP
    return sum(blocks[n * h : n * h + n] * masks[h] for h in range(GROUP))


def head_sums(values):
    row = lax.broadcasted_iota(jnp.int32, (2 * GROUP_LANES, GROUP_LANES), 0) % GROUP_LANES
    col = lax.broadcasted_iota(jnp.int32, (2 * GROUP_LANES, GROUP_LANES), 1)
    ones = (row // HEAD_DIM == col // HEAD_DIM).astype(jnp.float32).astype(jnp.bfloat16)
    high = values.astype(jnp.bfloat16)
    rest = (values - high.astype(jnp.float32)).astype(jnp.bfloat16)
    sums = []
    for start in range(0, values.shape[1], GROUP_LANES):
        cut = slice(start, start + GROUP_LANES)
        sums.append(dot(jnp.concatenate([high[:, cut], rest[:, cut]], axis=1), ones))
    return jnp.concatenate(sums, axis=1)


def send_rows(dest_row, rows, out_ref):
    total = out_ref.shape[0]
    block = math.gcd(total, 256)
    for start in range(0, total, block):
        slot = lax.broadcasted_iota(jnp.int32, (block, rows.shape[0]), 0) + start
        chosen = jnp.where(slot == dest_row, 1.0, 0.0).astype(jnp.bfloat16)
        out_ref[pl.ds(start, block), :] = dot(chosen, rows).astype(jnp.bfloat16)


def gelu_pair(pre):
    inner = math.sqrt(2.0 / math.pi)
    square = pre * pre
    bend = jnp.tanh(pre * (inner + (inner * 0.044715) * square))
    half = 0.5 + 0.5 * bend
    slope = half + pre * (half * (1.0 - bend)) * (inner + (3.0 * inner * 0.044715) * square)
    return pre * half, slope


def take_rows(dest_row, rows):
    count, total = dest_row.shape[1], rows.shape[0]
    places = jnp.broadcast_to(dest_row.astype(jnp.float32), (GROUP_LANES, count)).T
    lane = lax.broadcasted_iota(jnp.int32, (count, GROUP_LANES), 1).astype(jnp.float32)
    chosen = jnp.concatenate(
        [
            jnp.where(places == lane + float(start), 1.0, 0.0).astype(jnp.bfloat16)
            for start in range(0, total, GROUP_LANES)
        ],
        axis=1,
    )
    return dot(chosen, rows)


def assign_kernel(capacity, count_ref, route_ref, cot_ref, dest_ref, out_ref):
    tokens = route_ref.shape[1]
    total = out_ref.shape[0]
    span = GROUP_LANES
    live_end = count_ref[0] * IMG_TOK
    first = lax.broadcasted_iota(jnp.int32, (span, span), 0)
    second = lax.broadcasted_iota(jnp.int32, (span, span), 1)
    earlier = jnp.where(first < second, 1.0, 0.0).astype(jnp.bfloat16)
    whole = jnp.ones((span, span), jnp.bfloat16)
    carry = jnp.zeros((EXPERTS, span), jnp.float32)
    for start in range(0, tokens, span):
        route = route_ref[:, start : start + span]
        place = lax.broadcasted_iota(jnp.int32, (1, span), 1) + start
        expert = lax.broadcasted_iota(jnp.int32, (EXPERTS, span), 0)
        chosen = jnp.where((expert == route) & (place < live_end), 1.0, 0.0)
        low = chosen.astype(jnp.bfloat16)
        before = dot(low, earlier) + carry
        carry = carry + dot(low, whole)
        slot = jnp.sum(before * chosen, axis=0, keepdims=True).astype(jnp.int32)
        keep = (place < live_end) & (slot < capacity)
        dest_ref[:, start : start + span] = jnp.where(keep, route * capacity + slot, total)
    send_rows(dest_ref[...], cot_ref[...], out_ref)


def call_assign(images, routes, cotangent, capacity):
    tokens = routes.shape[0]
    total = EXPERTS * capacity
    return pl.pallas_call(
        functools.partial(assign_kernel, capacity),
        out_shape=(
            jax.ShapeDtypeStruct((1, tokens), jnp.int32),
            jax.ShapeDtypeStruct((total, MODEL_WIDTH), jnp.bfloat16),
        ),
        in_specs=[
            pl.BlockSpec(memory_space=pltpu.SMEM),
            pl.BlockSpec(memory_space=pltpu.VMEM),
            pl.BlockSpec(memory_space=pltpu.VMEM),
        ],
        out_specs=(
            pl.BlockSpec(memory_space=pltpu.VMEM),
            pl.BlockSpec(memory_space=pltpu.VMEM),
        ),
        cost_estimate=pl.CostEstimate(
            flops=2 * total * tokens * MODEL_WIDTH, bytes_accessed=4 * 10**6, transcendentals=0
        ),
        compiler_params=pltpu.CompilerParams(vmem_limit_bytes=VMEM_BYTES),
        name="assign",
    )(images, routes.reshape(1, tokens), cotangent)


def front_kernel(
    dest_ref,
    tokens_ref,
    weight_ref,
    rows_ref,
    scale_ref,
    bias_ref,
    placed_ref,
    section_ref,
    attended_ref,
    mixed_ref,
    raw_ref,
    heads_ref,
    probs_ref,
    low_ref,
):
    step = pl.program_id(0)
    block = tokens_ref.shape[0]
    width = MODEL_WIDTH
    tokens = tokens_ref[...]
    masks_low = lane_masks(jnp.bfloat16)
    masks = lane_masks(jnp.float32)
    projected = dot(tokens, weight_ref[:, : 3 * width])
    queries = projected[:, :width] + rows_ref[4:5, :]
    keys = projected[:, width : 2 * width]
    values = projected[:, 2 * width :] + rows_ref[5:6, :]
    raw_ref[:, :width] = queries
    raw_ref[:, width:] = keys
    heads_ref[:, :width] = (queries * lax.rsqrt(head_sums(queries * queries) + 1e-06)).astype(
        jnp.bfloat16
    )
    heads_ref[:, width : 2 * width] = (
        keys * lax.rsqrt(head_sums(keys * keys) + 1e-06)
    ).astype(jnp.bfloat16)
    heads_ref[:, 2 * width :] = values.astype(jnp.bfloat16)
    units = [
        (window, group)
        for window in range(block // WIN)
        for group in range(width // GROUP_LANES)
    ]

    def part(window, group, side):
        start = side * width + group * GROUP_LANES
        return heads_ref[window * WIN : window * WIN + WIN, start : start + GROUP_LANES]

    cosines = [dot_cols(part(w, g, 1), stack_heads(part(w, g, 0), masks_low)) for w, g in units]
    all_probs = []
    for (window, group), cosine in zip(units, cosines):
        scores = cosine * scale_ref[group] + bias_ref[group]
        powers = jnp.exp(scores - jnp.max(scores, axis=0, keepdims=True))
        probs = powers * (1.0 / jnp.sum(powers, axis=0, keepdims=True))
        probs_ref[window, group] = probs
        all_probs.append(probs.astype(jnp.bfloat16))
    mixes = [pick_heads(dot_rows(p, part(w, g, 2)), masks) for (w, g), p in zip(units, all_probs)]
    for (window, group), mixed in zip(units, mixes):
        mixed_ref[
            window * WIN : window * WIN + WIN,
            group * GROUP_LANES : group * GROUP_LANES + GROUP_LANES,
        ] = mixed.astype(jnp.bfloat16)
    attended = dot(mixed_ref[...], weight_ref[:, 3 * width : 4 * width]) + rows_ref[6:7, :]
    attended_ref[...] = attended
    section = tokens.astype(jnp.float32) + norm_rows(attended, rows_ref[0:1, :], rows_ref[1:2, :])
    section_ref[...] = section
    low_ref[pl.ds(pl.multiple_of(step * block, block), block), :] = section.astype(jnp.bfloat16)

    @pl.when(step == pl.num_programs(0) - 1)
    def _():
        send_rows(dest_ref[...], low_ref[...], placed_ref)


def token_block(tok_rows):
    return math.gcd(tok_rows, 512)


def whole(shape):
    return pl.BlockSpec(shape, lambda i: (0,) * len(shape))


def by_rows(block, width):
    return pl.BlockSpec((block, width), lambda i: (i, 0))


def call_front(dest, tokens, gathered, rows, scale, bias, capacity):
    count, width = tokens.shape
    total = EXPERTS * capacity
    block = token_block(count)
    groups = width // GROUP_LANES
    probs_shape = (count // WIN, groups, WIN, GROUP * WIN)
    return pl.pallas_call(
        front_kernel,
        grid=(count // block,),
        out_shape=(
            jax.ShapeDtypeStruct((total, width), jnp.bfloat16),
            jax.ShapeDtypeStruct((count, width), jnp.float32),
            jax.ShapeDtypeStruct((count, width), jnp.float32),
            jax.ShapeDtypeStruct((count, width), jnp.bfloat16),
            jax.ShapeDtypeStruct((count, 2 * width), jnp.float32),
            jax.ShapeDtypeStruct((count, 3 * width), jnp.bfloat16),
            jax.ShapeDtypeStruct(probs_shape, jnp.float32),
        ),
        in_specs=[
            whole(dest.shape),
            by_rows(block, width),
            whole(gathered.shape),
            whole(rows.shape),
            whole(scale.shape),
            whole(bias.shape),
        ],
        out_specs=(
            whole((total, width)),
            by_rows(block, width),
            by_rows(block, width),
            by_rows(block, width),
            by_rows(block, 2 * width),
            by_rows(block, 3 * width),
            pl.BlockSpec((block // WIN,) + probs_shape[1:], lambda i: (i, 0, 0, 0)),
        ),
        scratch_shapes=[pltpu.VMEM((count, width), jnp.bfloat16)],
        cost_estimate=pl.CostEstimate(
            flops=2 * count * width * width * 8, bytes_accessed=20 * 10**6, transcendentals=0
        ),
        compiler_params=pltpu.CompilerParams(vmem_limit_bytes=VMEM_BYTES),
        name="front",
    )(dest, tokens, gathered, rows, scale, bias)


def back_kernel(
    count_ref,
    dest_ref,
    arrived_ref,
    cot_ref,
    weight_ref,
    rows_ref,
    scale_ref,
    attended_ref,
    raw_ref,
    heads_ref,
    probs_ref,
    expert_ref,
    table_ref,
    coords_ref,
    net_ref,
    total_ref,
    low_attended,
    low_projected,
    sums_ref,
    grad_bias_ref,
    grad_scale_ref,
    grad_heads,
):
    step = pl.program_id(0)
    block = cot_ref.shape[0]
    width = MODEL_WIDTH
    start_row = pl.multiple_of(step * block, block)
    masks_low = lane_masks(jnp.bfloat16)
    masks = lane_masks(jnp.float32)

    @pl.when(step == 0)
    def _():
        sums_ref[...] = jnp.zeros_like(sums_ref)
        grad_bias_ref[...] = jnp.zeros_like(grad_bias_ref)
        grad_scale_ref[...] = jnp.zeros_like(grad_scale_ref)

    place = lax.broadcasted_iota(jnp.int32, (block, 1), 0) + start_row
    live = jnp.where(place < count_ref[0] * IMG_TOK, 1.0, 0.0)
    feed = take_rows(dest_ref[...], arrived_ref[...])
    total = cot_ref[...].astype(jnp.float32) * live + feed
    attended = attended_ref[...]
    centred = attended - jnp.mean(attended, axis=-1, keepdims=True)
    spread = lax.rsqrt(jnp.mean(centred * centred, axis=-1, keepdims=True) + 1e-05)
    unit = centred * spread
    grad_unit = total * rows_ref[0:1, :]
    grad_attended = spread * (
        grad_unit
        - jnp.mean(grad_unit, axis=-1, keepdims=True)
        - unit * jnp.mean(grad_unit * unit, axis=-1, keepdims=True)
    )
    grad_low = grad_attended.astype(jnp.bfloat16)
    total_ref[...] = total
    low_attended[...] = grad_low
    sums_ref[0:1, :width] += jnp.sum(total * unit, axis=0, keepdims=True)
    sums_ref[1:2, :width] += jnp.sum(total, axis=0, keepdims=True)
    sums_ref[6:7, :width] += jnp.sum(grad_low.astype(jnp.float32), axis=0, keepdims=True)
    grad_mixed = dot_cols(grad_low, weight_ref[:, 3 * width : 4 * width]).astype(jnp.bfloat16)
    units = [
        (window, group)
        for window in range(block // WIN)
        for group in range(width // GROUP_LANES)
    ]

    def cut(window, group, side):
        start = side * width + group * GROUP_LANES
        return slice(window * WIN, window * WIN + WIN), slice(start, start + GROUP_LANES)

    queries = [stack_heads(heads_ref[cut(w, g, 0)], masks_low) for w, g in units]
    grad_outs = [stack_heads(grad_mixed[cut(w, g, 0)], masks_low) for w, g in units]
    all_grad_probs = [
        dot_cols(heads_ref[cut(w, g, 2)], grad_out) for (w, g), grad_out in zip(units, grad_outs)
    ]
    cosines = [dot_cols(heads_ref[cut(w, g, 1)], query) for (w, g), query in zip(units, queries)]
    all_probs, grad_cosines = [], []
    for (window, group), grad_probs, cosine in zip(units, all_grad_probs, cosines):
        probs = probs_ref[window, group]
        all_probs.append(probs.astype(jnp.bfloat16))
        weighed = probs * grad_probs
        grad_scores = weighed - probs * jnp.sum(weighed, axis=0, keepdims=True)
        grad_bias_ref[group] += grad_scores
        grad_scale_ref[group] += jnp.sum(grad_scores * cosine, axis=0, keepdims=True)
        grad_cosines.append((grad_scores * scale_ref[group]).astype(jnp.bfloat16))
    for (w, g), probs, grad_out in zip(units, all_probs, grad_outs):
        grad_heads[cut(w, g, 2)] = dot(probs, grad_out)
    for (w, g), grad_cosine, query in zip(units, grad_cosines, queries):
        grad_heads[cut(w, g, 1)] = dot(grad_cosine, query)
    for (w, g), grad_cosine in zip(units, grad_cosines):
        grad_heads[cut(w, g, 0)] = pick_heads(
            dot_rows(grad_cosine, heads_ref[cut(w, g, 1)]), masks
        )
    for side in range(2):
        cut = slice(side * width, side * width + width)
        raw = raw_ref[:, cut]
        inverse = lax.rsqrt(head_sums(raw * raw) + 1e-06)
        unit = raw * inverse
        grad = grad_heads[:, cut]
        low_projected[:, cut] = (inverse * (grad - unit * head_sums(grad * unit))).astype(
            jnp.bfloat16
        )
    low_projected[:, 2 * width :] = grad_heads[:, 2 * width :].astype(jnp.bfloat16)
    grad_projected = low_projected[...]
    sums_ref[4:5, :width] += jnp.sum(
        grad_projected[:, :width].astype(jnp.float32), axis=0, keepdims=True
    )
    sums_ref[5:6, :width] += jnp.sum(
        grad_projected[:, 2 * width :].astype(jnp.float32), axis=0, keepdims=True
    )
    @pl.when(step == pl.num_programs(0) - 1)
    def _():
        sums_ref[2:4, :width] = expert_ref[1:3, :]
        for group in range(grad_scale_ref.shape[0]):
            at = SCALE_ROWS + group
            sums_ref[at : at + 1, : GROUP * WIN] = grad_scale_ref[group]
        net_back(
            sum_offsets(grad_bias_ref), table_ref[...], coords_ref[...], net_ref, sums_ref
        )


def sum_offsets(grad_bias_ref):
    row = lax.broadcasted_iota(jnp.int32, (GROUP * WIN, TABLE), 0)
    lane = lax.broadcasted_iota(jnp.int32, (GROUP * WIN, TABLE), 1)
    query = row % WIN
    aim = TABLE_MID - STRIDE * (query // SIDE) - query % SIDE
    spreads = [
        jnp.where((lane == aim) & (row // WIN == h), 1.0, 0.0).astype(jnp.bfloat16)
        for h in range(GROUP)
    ]
    sums = []
    for group in range(grad_bias_ref.shape[0]):
        grad = grad_bias_ref[group]
        high = grad.astype(jnp.bfloat16)
        rest = grad - high.astype(jnp.float32)
        middle = rest.astype(jnp.bfloat16)
        last = (rest - middle.astype(jnp.float32)).astype(jnp.bfloat16)
        parts = jnp.concatenate([high, middle, last], axis=0)
        for h in range(GROUP):
            spread = dot(parts, spreads[h])
            spread = spread[:WIN] + spread[WIN : 2 * WIN] + spread[2 * WIN :]
            rows = spread[:SIDE]
            for r in range(1, SIDE):
                rows = rows + pltpu.roll(spread[SIDE * r : SIDE * r + SIDE], STRIDE * r, 1)
            rows = pltpu.roll(rows, 0, 1, stride=1, stride_axis=0)
            sums.append(jnp.sum(rows, axis=0, keepdims=True))
    return jnp.concatenate(sums, axis=0)


def net_back(grad, table, coords, net_ref, sums_ref):
    heads = table.shape[0]
    second, shift, first = net_ref[:heads], net_ref[heads : heads + 1], net_ref[heads + 1 : heads + 3]
    pre = coords[:, 0:1] * first[0:1] + coords[:, 1:2] * first[1:2] + shift
    hidden, slope = gelu_pair(pre)
    grad_logits = grad * table * (1.0 - table * (1.0 / 16.0))
    sums_ref[SECOND_ROWS : SECOND_ROWS + heads, :] = jnp.dot(
        grad_logits, hidden, precision=highest, preferred_element_type=jnp.float32
    )
    grad_pre = slope * lax.dot_general(
        grad_logits, second, contract_rows, precision=highest, preferred_element_type=jnp.float32
    )
    sums_ref[SHIFT_ROW : SHIFT_ROW + 1, :] = jnp.sum(grad_pre, axis=0, keepdims=True)
    for k in range(2):
        sums_ref[FIRST_ROWS + k : FIRST_ROWS + k + 1, :] = jnp.sum(
            grad_pre * coords[:, k : k + 1], axis=0, keepdims=True
        )


def call_back(
    images, dest, arrived, cotangent, gathered, rows, scale, attended, raw, heads, probs,
    sums_expert, table, net,
):
    count, width = cotangent.shape
    block = token_block(count)
    groups = width // GROUP_LANES
    coords = jnp.asarray(offset_coords())
    return pl.pallas_call(
        back_kernel,
        grid=(count // block,),
        out_shape=(
            jax.ShapeDtypeStruct((count, width), jnp.float32),
            jax.ShapeDtypeStruct((count, width), jnp.bfloat16),
            jax.ShapeDtypeStruct((count, 3 * width), jnp.bfloat16),
            jax.ShapeDtypeStruct((SUM_ROWS, SUM_LANES), jnp.float32),
        ),
        in_specs=[
            pl.BlockSpec(memory_space=pltpu.SMEM),
            pl.BlockSpec((1, block), lambda i: (0, i)),
            whole(arrived.shape),
            by_rows(block, width),
            whole(gathered.shape),
            whole(rows.shape),
            whole(scale.shape),
            by_rows(block, width),
            by_rows(block, 2 * width),
            by_rows(block, 3 * width),
            pl.BlockSpec((block // WIN,) + probs.shape[1:], lambda i: (i, 0, 0, 0)),
            whole(sums_expert.shape),
            whole(table.shape),
            whole(coords.shape),
            whole(net.shape),
        ],
        out_specs=(
            by_rows(block, width),
            by_rows(block, width),
            by_rows(block, 3 * width),
            whole((SUM_ROWS, SUM_LANES)),
        ),
        scratch_shapes=[
            pltpu.VMEM((groups, WIN, GROUP * WIN), jnp.float32),
            pltpu.VMEM((groups, 1, GROUP * WIN), jnp.float32),
            pltpu.VMEM((block, 3 * width), jnp.float32),
        ],
        cost_estimate=pl.CostEstimate(
            flops=2 * count * width * width * 10, bytes_accessed=20 * 10**6, transcendentals=0
        ),
        compiler_params=pltpu.CompilerParams(vmem_limit_bytes=VMEM_MOST),
        name="back",
    )(
        images, dest, arrived, cotangent, gathered, rows, scale, attended, raw, heads, probs,
        sums_expert, table, coords, net,
    )


def dense_kernel(
    narrow,
    place_ref,
    tokens_ref,
    mixed_ref,
    attended_ref,
    projected_ref,
    expert_ref,
    send_ref,
    keep_ref,
):
    width = tokens_ref.shape[1]
    grad_dense = jnp.concatenate(
        [
            dot_rows(tokens_ref[...], projected_ref[...]),
            dot_rows(mixed_ref[...], attended_ref[...]),
        ],
        axis=1,
    )
    chips = keep_ref.shape[0]
    on_first = place_ref[0] == 0
    row = lax.broadcasted_iota(jnp.int32, (GROUP_LANES, width), 0)
    grad_route = jnp.where(row == place_ref[1], expert_ref[3:4, :], 0.0).T
    share = width // (2 * chips)
    for chip in range(chips):
        cuts = []
        for core in range(2):
            row = (chip // narrow * 2 * narrow + core * narrow + chip % narrow) * share
            rows, route = grad_dense[row : row + share], grad_route[row : row + share]
            halves = jnp.concatenate([rows[:, : 2 * width], rows[:, 2 * width :]], axis=0)
            route = jnp.concatenate([route, jnp.zeros_like(route)], axis=0)
            cuts.append(jnp.concatenate([halves, route], axis=1))
        keep_ref[chip] = jnp.where(on_first, cuts[0], cuts[1])
        send_ref[chip] = jnp.where(on_first, cuts[1], cuts[0]).astype(jnp.bfloat16)


def call_dense(tokens, mixed, attended, projected, sums_expert):
    count, width = tokens.shape
    narrow = lax.axis_size("narrow")
    chips = narrow * lax.axis_size("wide") // 2
    shape = (chips, width // chips, 2 * width + GROUP_LANES)
    place = jnp.stack([lax.axis_index("wide") % 2, lax.axis_index(("wide", "narrow"))])
    return pl.pallas_call(
        functools.partial(dense_kernel, narrow),
        out_shape=(
            jax.ShapeDtypeStruct(shape, jnp.bfloat16),
            jax.ShapeDtypeStruct(shape, jnp.float32),
        ),
        in_specs=[pl.BlockSpec(memory_space=pltpu.SMEM)]
        + [pl.BlockSpec(memory_space=pltpu.VMEM)] * 5,
        out_specs=(pl.BlockSpec(memory_space=pltpu.VMEM),) * 2,
        cost_estimate=pl.CostEstimate(
            flops=8 * count * width * width, bytes_accessed=7 * 10**6, transcendentals=0
        ),
        compiler_params=pltpu.CompilerParams(vmem_limit_bytes=VMEM_BYTES),
        name="dense",
    )(place.astype(jnp.int32), tokens, mixed, attended, projected, sums_expert)


def inputs_kernel(total_ref, projected_ref, weight_ref, out_ref):
    wide = projected_ref.shape[1]
    out_ref[...] = (
        total_ref[...] + dot_cols(projected_ref[...], weight_ref[:, :wide])
    ).astype(jnp.bfloat16)


def call_inputs(total, projected, gathered):
    count, width = total.shape
    block = token_block(count)
    return pl.pallas_call(
        inputs_kernel,
        grid=(count // block,),
        out_shape=jax.ShapeDtypeStruct((count, width), jnp.bfloat16),
        in_specs=[
            by_rows(block, width),
            by_rows(block, 3 * width),
            whole(gathered.shape),
        ],
        out_specs=by_rows(block, width),
        cost_estimate=pl.CostEstimate(
            flops=0, bytes_accessed=0, transcendentals=0
        ),
        compiler_params=pltpu.CompilerParams(vmem_limit_bytes=VMEM_BYTES),
        name="inputs",
    )(total, projected, gathered)


def layer_kernel(count_ref, dest_ref, branch_ref, section_ref, out_ref):
    block = out_ref.shape[0]
    place = lax.broadcasted_iota(jnp.int32, (block, 1), 0) + pl.program_id(0) * block
    live = jnp.where(place < count_ref[0] * IMG_TOK, 1.0, 0.0)
    branch = take_rows(dest_ref[...], branch_ref[...])
    out_ref[...] = ((section_ref[...] + branch) * live).astype(jnp.bfloat16)


def call_layer(images, dest, branch, section):
    count, width = section.shape
    block = token_block(count)
    return pl.pallas_call(
        layer_kernel,
        grid=(count // block,),
        out_shape=jax.ShapeDtypeStruct((count, width), jnp.bfloat16),
        in_specs=[
            pl.BlockSpec(memory_space=pltpu.SMEM),
            pl.BlockSpec((1, block), lambda i: (0, i)),
            whole(branch.shape),
            by_rows(block, width),
        ],
        out_specs=by_rows(block, width),
        cost_estimate=pl.CostEstimate(
            flops=0, bytes_accessed=0, transcendentals=0
        ),
        compiler_params=pltpu.CompilerParams(vmem_limit_bytes=VMEM_BYTES),
        name="layer",
    )(images, dest, branch, section)


def expert_kernel(
    rows_ref,
    cot_ref,
    first_ref,
    second_ref,
    bias_one_ref,
    vecs_ref,
    branch_ref,
    back_ref,
    hidden_ref,
    grad_pre_ref,
    grad_result_ref,
    sums_ref,
    sum_pre_ref,
):
    @pl.when(pl.program_id(0) == 0)
    def _():
        sums_ref[...] = jnp.zeros_like(sums_ref)
        sum_pre_ref[...] = jnp.zeros_like(sum_pre_ref)

    bias_two, gain, shift, route = (vecs_ref[i : i + 1, :] for i in range(4))
    count = rows_ref.shape[0]
    size = count // EXPERT_PARTS
    cuts = [slice(start, start + size) for start in range(0, count, size)]
    pres = [dot(rows_ref[cut, :], first_ref[...]) + bias_one_ref[...] for cut in cuts]
    pairs = [gelu_pair(pre) for pre in pres]
    hiddens = [hidden.astype(jnp.bfloat16) for hidden, _ in pairs]
    raws = [dot(hidden, second_ref[...]) + bias_two for hidden in hiddens]
    grads = []
    for cut, hidden, raw in zip(cuts, hiddens, raws):
        hidden_ref[cut, :] = hidden
        rows = rows_ref[cut, :].astype(jnp.float32)
        result = raw.astype(jnp.bfloat16).astype(jnp.float32)
        gating = jax.nn.sigmoid(jnp.sum(rows * route, axis=-1, keepdims=True))
        centred = result - jnp.mean(result, axis=-1, keepdims=True)
        spread = lax.rsqrt(jnp.mean(centred * centred, axis=-1, keepdims=True) + 1e-05)
        unit = centred * spread
        normed = unit * gain + shift
        branch_ref[cut, :] = (normed * gating).astype(jnp.bfloat16)
        cot = cot_ref[cut, :].astype(jnp.float32)
        grad_gate = jnp.sum(cot * normed, axis=-1, keepdims=True)
        gated = cot * gating
        grad_unit = gated * gain
        grad_result = (
            spread
            * (
                grad_unit
                - jnp.mean(grad_unit, axis=-1, keepdims=True)
                - unit * jnp.mean(grad_unit * unit, axis=-1, keepdims=True)
            )
        ).astype(jnp.bfloat16)
        grad_result_ref[cut, :] = grad_result
        grad_logit = (
            (grad_gate * gating * (1.0 - gating)).astype(jnp.bfloat16).astype(jnp.float32)
        )
        sums_ref[0:1, :] += jnp.sum(grad_result.astype(jnp.float32), axis=0, keepdims=True)
        sums_ref[1:2, :] += jnp.sum(gated * unit, axis=0, keepdims=True)
        sums_ref[2:3, :] += jnp.sum(gated, axis=0, keepdims=True)
        sums_ref[3:4, :] += jnp.sum(rows * grad_logit, axis=0, keepdims=True)
        grads.append((grad_result, grad_logit))
    grad_hiddens = [dot_cols(grad, second_ref[...]) for grad, _ in grads]
    grad_pres = [
        (grad * slope).astype(jnp.bfloat16) for grad, (_, slope) in zip(grad_hiddens, pairs)
    ]
    for cut, grad_pre, (_, grad_logit) in zip(cuts, grad_pres, grads):
        grad_pre_ref[cut, :] = grad_pre
        sum_pre_ref[...] += jnp.sum(grad_pre.astype(jnp.float32), axis=0, keepdims=True)
        back_ref[cut, :] = (dot_cols(grad_pre, first_ref[...]) + grad_logit * route).astype(
            jnp.bfloat16
        )


def call_expert(rows, cot, first, second, bias_one, vecs):
    count, width = rows.shape
    ff = first.shape[1]
    block = math.gcd(count, 640)
    return pl.pallas_call(
        expert_kernel,
        grid=(count // block,),
        out_shape=(
            jax.ShapeDtypeStruct((count, width), jnp.bfloat16),
            jax.ShapeDtypeStruct((count, width), jnp.bfloat16),
            jax.ShapeDtypeStruct((count, ff), jnp.bfloat16),
            jax.ShapeDtypeStruct((count, ff), jnp.bfloat16),
            jax.ShapeDtypeStruct((count, width), jnp.bfloat16),
            jax.ShapeDtypeStruct((8, width), jnp.float32),
            jax.ShapeDtypeStruct((1, ff), jnp.float32),
        ),
        in_specs=[
            by_rows(block, width),
            by_rows(block, width),
            whole(first.shape),
            whole(second.shape),
            whole(bias_one.shape),
            whole(vecs.shape),
        ],
        out_specs=(
            by_rows(block, width),
            by_rows(block, width),
            by_rows(block, ff),
            by_rows(block, ff),
            by_rows(block, width),
            whole((8, width)),
            whole((1, ff)),
        ),
        cost_estimate=pl.CostEstimate(
            flops=8 * count * width * ff, bytes_accessed=16 * 10**6, transcendentals=count * ff
        ),
        compiler_params=pltpu.CompilerParams(vmem_limit_bytes=VMEM_MOST),
        name="expert",
    )(rows, cot, first, second, bias_one, vecs)


def offset_coords():
    place = TABLE_MID - np.arange(TABLE)
    row = (place + STRIDE // 2 - 1) // STRIDE
    coords = np.stack([row, place - STRIDE * row], axis=1) * (8.0 / (SIDE - 1))
    return (np.sign(coords) * np.log2(np.abs(coords) + 1.0) / 3.0).astype(np.float32)


def bias_table(params):
    piece_collection = pieces(params)
    hidden = jax.nn.gelu(
        jnp.dot(offset_coords(), piece_collection[9], precision=highest) + piece_collection[8]
    )
    return 16.0 * jax.nn.sigmoid(jnp.dot(hidden, piece_collection[10], precision=highest)).T


def spread_bias(table):
    places = jnp.arange(WIN, dtype=jnp.int32)
    coded = STRIDE * (places // SIDE) + places % SIDE
    index = TABLE_MID + coded[:, None] - coded[None, :]
    lookup = (index.reshape(1, -1) == jnp.arange(TABLE, dtype=jnp.int32)[:, None]).astype(
        table.dtype
    )
    bias = jnp.dot(table, lookup, precision=highest).reshape(-1, GROUP, WIN, WIN)
    return bias.transpose(0, 2, 1, 3).reshape(-1, WIN, GROUP * WIN)


def per_device_split(
    tokens,
    cotangent,
    routes,
    images,
    dense_weight,
    dense_moment,
    dense_square,
    small_params,
    small_moment,
    small_square,
    inner_weight,
    inner_moment,
    inner_square,
    outer_weight,
    outer_moment,
    outer_square,
    expert_bias,
    bias_moment,
    bias_square,
):
    slices = lax.axis_size(("wide", "narrow"))
    split = slices // EXPERTS
    member = lax.axis_index(("wide", "narrow")) % split
    piece = MODEL_WIDTH // split
    ff_dev = inner_weight.shape[2]
    tok_rows = tokens.shape[0]
    capacity = (5 * tok_rows + 4 * EXPERTS - 1) // (4 * EXPERTS)
    slot_total = EXPERTS * capacity
    route_ids = routes[:, 0]
    live_rows, kept_rows, dest_slot = assign(route_ids, images[0], EXPERTS, capacity)
    live_f = live_rows.astype(jnp.float32)
    keep_f = kept_rows.astype(jnp.float32)
    clipped = jnp.minimum(dest_slot, slot_total - 1)
    gathered = gather_rows(dense_weight.astype(jnp.bfloat16))
    section_one, gating, expert_feed, kept = front_forward_split(
        tokens, gathered, small_params, route_ids
    )

    def fan_out(rows_value):
        placed_rows = (
            jnp.zeros((slot_total, MODEL_WIDTH), jnp.bfloat16)
            .at[dest_slot]
            .set(rows_value.astype(jnp.bfloat16), mode="drop")
        )
        copies = jnp.broadcast_to(
            placed_rows.reshape(EXPERTS, 1, capacity, MODEL_WIDTH),
            (EXPERTS, split, capacity, MODEL_WIDTH),
        )
        return trade_rows(copies.reshape(slices, capacity, MODEL_WIDTH)).reshape(
            slices * capacity, MODEL_WIDTH
        )

    def fan_in(partials):
        arrived = trade_rows(partials.reshape(slices, capacity, MODEL_WIDTH))
        summed = jnp.sum(
            arrived.reshape(EXPERTS, split, capacity, MODEL_WIDTH).astype(jnp.float32), axis=1
        ).reshape(slot_total, MODEL_WIDTH)
        return jnp.take(summed, clipped, axis=0) * keep_f[:, None]

    expert_rows = fan_out(expert_feed)
    first_matrix = inner_weight[0].astype(jnp.bfloat16)
    second_matrix = outer_weight[0].astype(jnp.bfloat16)
    pre_act = (
        jnp.dot(expert_rows, first_matrix, preferred_element_type=jnp.float32)
        + expert_bias[0, :ff_dev]
    )
    hidden = jax.nn.gelu(pre_act).astype(jnp.bfloat16)
    out_bias = lax.dynamic_update_slice(
        jnp.zeros((MODEL_WIDTH,), jnp.float32), expert_bias[0, ff_dev:], (member * piece,)
    )
    result = (jnp.dot(hidden, second_matrix, preferred_element_type=jnp.float32) + out_bias).astype(
        jnp.bfloat16
    )
    combined = fan_in(result)

    def tail_local(section_value, gate_value, combined_value, params):
        return finish_block(section_value, gate_value, combined_value, keep_f, live_f, params)

    layer_value, tail_back = jax.vjp(tail_local, section_one, gating, combined, small_params)
    grad_section, grad_gate, grad_combined, grad_small_tail = tail_back(
        cotangent.astype(jnp.float32)
    )
    grad_result = fan_out(grad_combined)
    grad_outer = lax.dot_general(
        hidden, grad_result, contract_rows, preferred_element_type=jnp.float32
    )
    grad_hidden = lax.dot_general(
        grad_result, second_matrix, contract_cols, preferred_element_type=jnp.float32
    )
    gelu_back = jax.vjp(jax.nn.gelu, pre_act)[1]
    grad_pre = gelu_back(grad_hidden)[0].astype(jnp.bfloat16)
    grad_inner = lax.dot_general(
        expert_rows, grad_pre, contract_rows, preferred_element_type=jnp.float32
    )
    column_total = jnp.sum(grad_result.astype(jnp.float32), axis=0)
    grad_bias = jnp.concatenate(
        [
            jnp.sum(grad_pre.astype(jnp.float32), axis=0),
            lax.dynamic_slice_in_dim(column_total, member * piece, piece, 0),
        ]
    )
    grad_rows = lax.dot_general(
        grad_pre, first_matrix, contract_cols, preferred_element_type=jnp.float32
    ).astype(jnp.bfloat16)
    grad_feed = fan_in(grad_rows)
    grad_inputs, grad_weights, grad_small_front = front_backward_split(
        tokens, gathered, small_params, kept, grad_section, grad_gate, grad_feed
    )
    grad_small = grad_small_front + grad_small_tail
    grad_dense, grad_small = sum_grads(grad_weights, grad_small)
    dense_out = adamw_step(
        dense_weight, grad_dense, dense_moment, dense_square, dense_rate, weight_decay
    )
    small_out = adamw_step(small_params, grad_small, small_moment, small_square, small_rate, 0.0)
    inner_out = adamw_step(
        inner_weight, grad_inner[None], inner_moment, inner_square, expert_rate, weight_decay
    )
    outer_out = adamw_step(
        outer_weight, grad_outer[None], outer_moment, outer_square, expert_rate, weight_decay
    )
    bias_out = adamw_step(expert_bias, grad_bias[None], bias_moment, bias_square, expert_rate, 0.0)
    return (
        layer_value.astype(jnp.bfloat16),
        grad_inputs.astype(jnp.bfloat16),
        dense_out[0],
        dense_out[1],
        dense_out[2],
        small_out[0],
        small_out[1],
        small_out[2],
        inner_out[0],
        inner_out[1],
        inner_out[2],
        inner_out[0].astype(jnp.bfloat16),
        outer_out[0],
        outer_out[1],
        outer_out[2],
        outer_out[0].astype(jnp.bfloat16),
        bias_out[0],
        bias_out[1],
        bias_out[2],
    )


def per_device(
    tokens,
    cotangent,
    routes,
    images,
    dense_weight,
    dense_moment,
    dense_square,
    small_params,
    small_moment,
    small_square,
    inner_weight,
    inner_moment,
    inner_square,
    outer_weight,
    outer_moment,
    outer_square,
    expert_bias,
    bias_moment,
    bias_square,
):
    slices = lax.axis_size(("wide", "narrow"))
    if slices != EXPERTS:
        return per_device_split(
            tokens,
            cotangent,
            routes,
            images,
            dense_weight,
            dense_moment,
            dense_square,
            small_params,
            small_moment,
            small_square,
            inner_weight,
            inner_moment,
            inner_square,
            outer_weight,
            outer_moment,
            outer_square,
            expert_bias,
            bias_moment,
            bias_square,
        )
    expert = lax.axis_index(("wide", "narrow"))
    ff_dev = inner_weight.shape[2]
    tok_rows = tokens.shape[0]
    capacity = (5 * tok_rows + 4 * EXPERTS - 1) // (4 * EXPERTS)
    slot_total = EXPERTS * capacity

    def trade(rows):
        traded = trade_rows(rows.reshape(slices, capacity, MODEL_WIDTH))
        return traded.reshape(slot_total, MODEL_WIDTH)

    scale_at = 7 * MODEL_WIDTH
    share = dense_weight.astype(jnp.bfloat16)
    across, *deep = axis_bits("narrow")
    held = join_quad(share, deep)
    held = join(held, across, -2)
    held, route_ids, cot = lax.optimization_barrier((held, routes, cotangent))
    dest, placed_cot = call_assign(images, route_ids, cot, capacity)
    cot_rows = trade(placed_cot)
    core, *rest = axis_bits("wide")
    for step in rest:
        held = join(held, step)
    held, params = lax.optimization_barrier((held, small_params))
    gathered = join(held, core, len(rest)).reshape(-1, share.shape[-1])
    table = bias_table(params)
    net_pieces = pieces(params)
    net = jnp.concatenate([net_pieces[10].T, net_pieces[8][None, :], net_pieces[9]])
    vectors = params[:scale_at].reshape(7, MODEL_WIDTH)
    scale_heads = jnp.exp(params[scale_at : scale_at + ATTENTION_HEADS])
    scale = jnp.repeat(scale_heads, WIN).reshape(-1, 1, GROUP * WIN)
    bias = spread_bias(table)
    placed, section, attended, mixed, raw, heads, probs = call_front(
        dest, tokens, gathered, vectors, scale, bias, capacity
    )
    placed, cot_rows = lax.optimization_barrier((placed, cot_rows))
    expert_rows = trade(placed)
    first_matrix = inner_weight[0].astype(jnp.bfloat16)
    second_matrix = outer_weight[0].astype(jnp.bfloat16)
    route_row = lax.dynamic_slice_in_dim(gathered, 4 * MODEL_WIDTH + expert, 1, 1)
    vecs = jnp.concatenate(
        [expert_bias[:, ff_dev:], vectors[2:4], route_row.astype(jnp.float32).reshape(1, -1)]
    )
    branch, grad_rows, hidden, grad_pre, grad_result, sums_expert, sum_pre = call_expert(
        expert_rows, cot_rows, first_matrix, second_matrix, expert_bias[:, :ff_dev], vecs
    )
    arrived = trade(grad_rows)
    grad_outer = dot_rows(hidden, grad_result)
    grad_inner = dot_rows(expert_rows, grad_pre)
    grad_bias = jnp.concatenate([sum_pre, sums_expert[0:1]], axis=1)[0]
    inner_out = adamw_step(
        inner_weight, grad_inner[None], inner_moment, inner_square, expert_rate, weight_decay
    )
    outer_out = adamw_step(
        outer_weight, grad_outer[None], outer_moment, outer_square, expert_rate, weight_decay
    )
    inner_out += (inner_out[0].astype(jnp.bfloat16),)
    outer_out += (outer_out[0].astype(jnp.bfloat16),)
    branch, arrived, inner_out, outer_out = lax.optimization_barrier(
        (branch, arrived, inner_out, outer_out)
    )
    branch_rows = trade(branch)
    total, low_attended, low_projected, sums = call_back(
        images,
        dest,
        arrived,
        cotangent,
        gathered,
        vectors,
        scale,
        attended,
        raw,
        heads,
        probs,
        sums_expert,
        table,
        net,
    )
    send, keep = call_dense(tokens, mixed, low_attended, low_projected, sums_expert)
    grad_inputs = call_inputs(total, low_projected, gathered)
    held = sum_chip(send, keep)
    narrow = lax.axis_size("narrow")
    sums = sums + swap_flat(sums, narrow)
    held, sums, branch_rows = lax.optimization_barrier((held, sums, branch_rows))
    grad_dense = sum_shares(held)
    sums = sum_quads(sum_quads(sums, 2, 4), 1, 2 * narrow)
    layer_out = call_layer(images, dest, branch_rows, section)
    share_rows = dense_weight.shape[0]
    half = 2 * MODEL_WIDTH
    grad_dense = jnp.concatenate(
        [
            grad_dense[:share_rows, :half],
            grad_dense[share_rows:, :half],
            grad_dense[:share_rows, half : half + EXPERTS],
        ],
        axis=1,
    )
    grad_scale = sums[SCALE_ROWS : SCALE_ROWS + ATTENTION_HEADS // GROUP, : GROUP * WIN]
    grad_small = jnp.concatenate(
        [
            sums[:7, :MODEL_WIDTH].reshape(-1),
            jnp.sum(grad_scale.reshape(ATTENTION_HEADS, WIN), axis=1) * scale_heads,
            sums[SHIFT_ROW : FIRST_ROWS + 2].reshape(-1),
            sums[SECOND_ROWS : SECOND_ROWS + ATTENTION_HEADS].T.reshape(-1),
        ]
    )
    dense_out = adamw_step(
        dense_weight, grad_dense, dense_moment, dense_square, dense_rate, weight_decay
    )
    small_out = adamw_step(small_params, grad_small, small_moment, small_square, small_rate, 0.0)
    bias_out = adamw_step(expert_bias, grad_bias[None], bias_moment, bias_square, expert_rate, 0.0)
    return (
        layer_out,
        grad_inputs,
        dense_out[0],
        dense_out[1],
        dense_out[2],
        small_out[0],
        small_out[1],
        small_out[2],
        inner_out[0],
        inner_out[1],
        inner_out[2],
        inner_out[3],
        outer_out[0],
        outer_out[1],
        outer_out[2],
        outer_out[3],
        bias_out[0],
        bias_out[1],
        bias_out[2],
    )


def solution(mesh):
    return jax.shard_map(
        per_device,
        mesh=mesh,
        in_specs=(
            P(("wide", "narrow"), None),
            P(("wide", "narrow"), None),
            P(("wide", "narrow"), None),
            P(("wide", "narrow")),
            P(("wide", "narrow"), None),
            P(("wide", "narrow"), None),
            P(("wide", "narrow"), None),
            P(),
            P(),
            P(),
            P(("wide", "narrow"), None, None),
            P(("wide", "narrow"), None, None),
            P(("wide", "narrow"), None, None),
            P(("wide", "narrow"), None, None),
            P(("wide", "narrow"), None, None),
            P(("wide", "narrow"), None, None),
            P(("wide", "narrow"), None),
            P(("wide", "narrow"), None),
            P(("wide", "narrow"), None),
        ),
        out_specs=(
            P(("wide", "narrow"), None),
            P(("wide", "narrow"), None),
            P(("wide", "narrow"), None),
            P(("wide", "narrow"), None),
            P(("wide", "narrow"), None),
            P(),
            P(),
            P(),
            P(("wide", "narrow"), None, None),
            P(("wide", "narrow"), None, None),
            P(("wide", "narrow"), None, None),
            P(("wide", "narrow"), None, None),
            P(("wide", "narrow"), None, None),
            P(("wide", "narrow"), None, None),
            P(("wide", "narrow"), None, None),
            P(("wide", "narrow"), None, None),
            P(("wide", "narrow"), None),
            P(("wide", "narrow"), None),
            P(("wide", "narrow"), None),
        ),
        check_vma=False,
    )
```

```python
import functools
import math

import jax
import jax.numpy as jnp
import numpy as np
from jax import lax
from jax.experimental import pallas as pl
from jax.experimental.pallas import tpu as pltpu
from jax.sharding import PartitionSpec as P

MODEL_WIDTH = 384
ATTENTION_HEADS = 12
HEAD_DIM = 32
BIAS_NET_HIDDEN = 512
EXPERTS = 32
SIDE = 8
IMG_TOK = 1024
STEP = 10
WIN = 64
GROUP = 4
GROUP_LANES = 128
VMEM_BYTES = 48 * 2**20
VMEM_MOST = 62 * 2**20
EXPERT_PARTS = 2
TABLE = 256
TABLE_MID = 119
STRIDE = 16
SUM_LANES = BIAS_NET_HIDDEN
SECOND_ROWS = 8
SHIFT_ROW = 20
FIRST_ROWS = 21
SCALE_ROWS = 24
SUM_ROWS = 32


highest = lax.Precision.HIGHEST
beta_one = 0.9
beta_two = 0.999
epsilon = 1e-08
dense_rate = 0.05
expert_rate = 0.05
small_rate = 0.3
weight_decay = 0.05
contract_rows = (((0,), (0,)), ((), ()))
contract_cols = (((1,), (1,)), ((), ()))


def pieces(small_params):
    length_list = (
        MODEL_WIDTH,
        MODEL_WIDTH,
        MODEL_WIDTH,
        MODEL_WIDTH,
        MODEL_WIDTH,
        MODEL_WIDTH,
        MODEL_WIDTH,
        ATTENTION_HEADS,
        BIAS_NET_HIDDEN,
        2 * BIAS_NET_HIDDEN,
        BIAS_NET_HIDDEN * ATTENTION_HEADS,
    )
    piece_collection = []
    offset = 0
    for length in length_list:
        piece_collection.append(small_params[offset : offset + length])
        offset = offset + length
    piece_collection[9] = piece_collection[9].reshape(2, BIAS_NET_HIDDEN)
    piece_collection[10] = piece_collection[10].reshape(BIAS_NET_HIDDEN, ATTENTION_HEADS)
    return piece_collection


def norm_rows(values, gain, shift):
    average = jnp.mean(values, axis=-1, keepdims=True)
    centred = values - average
    variance = jnp.mean(centred * centred, axis=-1, keepdims=True)
    return centred * lax.rsqrt(variance + 1e-05) * gain + shift


def position_bias(small_params):
    piece_collection = pieces(small_params)
    span = 2 * SIDE - 1
    offsets = jnp.arange(span, dtype=jnp.float32) - (SIDE - 1)
    coords = jnp.stack([jnp.repeat(offsets, span), jnp.tile(offsets, span)], axis=1) * (
        8.0 / (SIDE - 1)
    )
    coords = jnp.sign(coords) * jnp.log2(jnp.abs(coords) + 1.0) / 3.0
    hidden = jax.nn.gelu(
        jnp.dot(coords, piece_collection[9], precision=highest) + piece_collection[8]
    )
    table = 16.0 * jax.nn.sigmoid(jnp.dot(hidden, piece_collection[10], precision=highest))
    places = jnp.arange(WIN, dtype=jnp.int32)
    row_pos = places // SIDE
    col_pos = places % SIDE
    index = (row_pos[:, None] - row_pos[None, :] + SIDE - 1) * span + (
        col_pos[:, None] - col_pos[None, :] + SIDE - 1
    )
    lookup = (index.reshape(-1, 1) == jnp.arange(span * span, dtype=jnp.int32)[None, :]).astype(
        table.dtype
    )
    spread = jnp.dot(lookup, table, precision=highest)
    return spread.T.reshape(ATTENTION_HEADS, WIN, WIN)


def matmul_back(left_low, right_low, grad_low):
    grad_left = lax.dot_general(
        grad_low, right_low, contract_cols, preferred_element_type=jnp.float32
    )
    grad_right = lax.dot_general(
        left_low, grad_low, contract_rows, preferred_element_type=jnp.float32
    )
    return (grad_left, grad_right)


def add_joined_bias(raw, params):
    piece_collection = pieces(params)
    return raw + jnp.concatenate(
        [piece_collection[4], jnp.zeros_like(piece_collection[4]), piece_collection[5]]
    )


def add_out_bias(raw, params):
    return raw + pieces(params)[6]


def normalize_heads(projected):
    window_count = projected.shape[0] // WIN
    shaped = projected.reshape(window_count, WIN, 3, ATTENTION_HEADS, HEAD_DIM)
    queries = shaped[:, :, 0]
    key_vecs = shaped[:, :, 1]
    queries = queries * lax.rsqrt(jnp.sum(queries * queries, axis=-1, keepdims=True) + 1e-06)
    key_vecs = key_vecs * lax.rsqrt(jnp.sum(key_vecs * key_vecs, axis=-1, keepdims=True) + 1e-06)
    return (queries, key_vecs, shaped[:, :, 2])


def softmax_part(cosine, params):
    scale = jnp.exp(pieces(params)[7])[:, None, None]
    return jax.nn.softmax(cosine * scale + position_bias(params), axis=-1)


def front_forward_split(tokens_low, weights_low, params, route_ids):
    rows_here = tokens_low.shape[0]
    qkv_low = weights_low[:, : 3 * MODEL_WIDTH]
    out_low = weights_low[:, 3 * MODEL_WIDTH : 4 * MODEL_WIDTH]
    route_low = weights_low[:, 4 * MODEL_WIDTH :]
    raw_qkv = jnp.dot(tokens_low, qkv_low, preferred_element_type=jnp.float32)
    projected = add_joined_bias(raw_qkv, params)
    q_f, k_f, v_f = normalize_heads(projected)
    q_low = q_f.astype(jnp.bfloat16)
    k_low = k_f.astype(jnp.bfloat16)
    v_low = v_f.astype(jnp.bfloat16)
    cosine = jnp.einsum("wihd,wjhd->whij", q_low, k_low, preferred_element_type=jnp.float32)
    probs = softmax_part(cosine, params)
    probs_low = probs.astype(jnp.bfloat16)
    mixed_low = (
        jnp.einsum("whij,wjhd->wihd", probs_low, v_low, preferred_element_type=jnp.float32)
        .astype(jnp.bfloat16)
        .reshape(rows_here, MODEL_WIDTH)
    )
    attended = add_out_bias(jnp.dot(mixed_low, out_low, preferred_element_type=jnp.float32), params)
    piece_collection = pieces(params)
    section_one = tokens_low.astype(jnp.float32) + norm_rows(
        attended, piece_collection[0], piece_collection[1]
    )
    section_low = section_one.astype(jnp.bfloat16)
    logits = jnp.dot(section_low, route_low, preferred_element_type=jnp.float32)
    chosen_mask = (
        route_ids[:, None] == jnp.arange(logits.shape[1], dtype=jnp.int32)[None, :]
    ).astype(jnp.float32)
    gating = jax.nn.sigmoid(jnp.sum(logits * chosen_mask, axis=1))
    kept = (
        projected,
        q_low,
        k_low,
        v_low,
        cosine,
        probs_low,
        mixed_low,
        attended,
        section_low,
        logits,
        chosen_mask,
    )
    return (section_one, gating, section_low, kept)


def front_backward_split(tokens_low, weights_low, params, kept, grad_section, grad_gate, grad_feed):
    (
        projected,
        q_low,
        k_low,
        v_low,
        cosine,
        probs_low,
        mixed_low,
        attended,
        section_low,
        logits,
        chosen_mask,
    ) = kept
    rows_here = tokens_low.shape[0]
    window_count = rows_here // WIN
    qkv_low = weights_low[:, : 3 * MODEL_WIDTH]
    out_low = weights_low[:, 3 * MODEL_WIDTH : 4 * MODEL_WIDTH]
    route_low = weights_low[:, 4 * MODEL_WIDTH :]

    def gate_part(logit_values):
        return jax.nn.sigmoid(jnp.sum(logit_values * chosen_mask, axis=1))

    gate_back = jax.vjp(gate_part, logits)[1]
    grad_logits = gate_back(grad_gate)[0].astype(jnp.bfloat16)
    grad_from_route, grad_route = matmul_back(section_low, route_low, grad_logits)
    grad_total = grad_section + grad_feed + grad_from_route

    def section_part(attended_value, params_value):
        piece_collection = pieces(params_value)
        return norm_rows(attended_value, piece_collection[0], piece_collection[1])

    section_back = jax.vjp(section_part, attended, params)[1]
    grad_attended, grad_params_a = section_back(grad_total)
    grad_att_low = grad_attended.astype(jnp.bfloat16)
    grad_params_b = jax.vjp(add_out_bias, jnp.zeros_like(attended), params)[1](
        grad_att_low.astype(jnp.float32)
    )[1]
    grad_mixed, grad_out = matmul_back(mixed_low, out_low, grad_att_low)
    grad_mixed_low = grad_mixed.astype(jnp.bfloat16).reshape(
        window_count, WIN, ATTENTION_HEADS, HEAD_DIM
    )
    grad_probs = jnp.einsum(
        "wihd,wjhd->whij", grad_mixed_low, v_low, preferred_element_type=jnp.float32
    )
    grad_v = jnp.einsum(
        "whij,wihd->wjhd", probs_low, grad_mixed_low, preferred_element_type=jnp.float32
    )
    soft_back = jax.vjp(softmax_part, cosine, params)[1]
    grad_cosine, grad_params_c = soft_back(grad_probs)
    grad_cos_low = grad_cosine.astype(jnp.bfloat16)
    grad_q = jnp.einsum("whij,wjhd->wihd", grad_cos_low, k_low, preferred_element_type=jnp.float32)
    grad_k = jnp.einsum("whij,wihd->wjhd", grad_cos_low, q_low, preferred_element_type=jnp.float32)
    norm_back = jax.vjp(normalize_heads, projected)[1]
    grad_projected = norm_back((grad_q, grad_k, grad_v))[0]
    grad_proj_low = grad_projected.astype(jnp.bfloat16)
    grad_params_d = jax.vjp(add_joined_bias, jnp.zeros_like(projected), params)[1](
        grad_proj_low.astype(jnp.float32)
    )[1]
    grad_tokens, grad_qkv = matmul_back(tokens_low, qkv_low, grad_proj_low)
    grad_inputs = grad_total + grad_tokens
    grad_weights = jnp.concatenate([grad_qkv, grad_out, grad_route], axis=1)
    grad_params = grad_params_a + grad_params_b + grad_params_c + grad_params_d
    return (grad_inputs, grad_weights, grad_params)


def finish_block(section_one, gating, combined, kept_rows, live_rows, small_params):
    piece_collection = pieces(small_params)
    branch = (
        norm_rows(combined, piece_collection[2], piece_collection[3])
        * (gating * kept_rows)[:, None]
    )
    return (section_one + branch) * live_rows[:, None]


def assign(route_ids, count, experts, capacity):
    places = jnp.arange(route_ids.shape[0], dtype=jnp.int32)
    live_rows = places // IMG_TOK < count
    chosen = (
        (route_ids[:, None] == jnp.arange(experts, dtype=jnp.int32)[None, :]) & live_rows[:, None]
    ).astype(jnp.int32)
    before = jnp.cumsum(chosen, axis=0) - chosen
    slot = jnp.sum(before * chosen, axis=1)
    kept_rows = live_rows & (slot < capacity)
    dest_slot = jnp.where(kept_rows, route_ids * capacity + slot, experts * capacity)
    return (live_rows, kept_rows, dest_slot)


def adamw_step(weight, gradient, first, second, rate, decay):
    first_new = beta_one * first + (1.0 - beta_one) * gradient
    second_new = beta_two * second + (1.0 - beta_two) * gradient * gradient
    first_hat = first_new / (1.0 - beta_one**STEP)
    second_hat = second_new / (1.0 - beta_two**STEP)
    weight_new = weight - rate * (first_hat / (jnp.sqrt(second_hat) + epsilon) + decay * weight)
    return (weight_new, first_new, second_new)


def trade_rows(payload):
    arrived_rows = lax.all_to_all(
        payload, ("wide", "narrow"), split_axis=0, concat_axis=0, tiled=True
    )
    return arrived_rows


def axis_bits(axis):
    size = lax.axis_size(axis)
    return [(axis, 1 << k) for k in range(size.bit_length() - 1)]


def swap(value, step):
    axis, offset = step
    return lax.ppermute(value, axis, [(i, i ^ offset) for i in range(lax.axis_size(axis))])


def upper(step):
    axis, offset = step
    return (lax.axis_index(axis) & offset) > 0


def gather_rows(share):
    steps = axis_bits("narrow") + axis_bits("wide")
    first, rest = steps[0], steps[1:]
    other = swap(share, first)
    block = jnp.where(
        upper(first), jnp.concatenate([other, share]), jnp.concatenate([share, other])
    )
    held = block
    done = []
    core = ("wide", 1)
    for step in [s for s in rest if s != core] + [core]:
        place = sum(1 for d in done if rest.index(d) > rest.index(step))
        other = swap(held, step)
        held = jnp.where(
            upper(step), jnp.stack([other, held], place), jnp.stack([held, other], place)
        )
        done.append(step)
    return held.reshape(-1, share.shape[1])


def sum_grads(partial, small):
    steps = axis_bits("narrow") + axis_bits("wide")
    first, rest = steps[0], steps[1:]
    core = ("wide", 1)
    order = [core] + [s for s in rest[::-1] if s != core]
    count = lax.axis_size(("wide", "narrow"))
    share = partial.shape[0] // count
    held = partial.reshape((2,) * len(rest) + (2 * share, partial.shape[1]))
    left = rest[::-1]
    for step in order:
        place = left.index(step)
        side = upper(step).astype(jnp.int32)
        send = lax.dynamic_index_in_dim(held, 1 - side, place, keepdims=False)
        keep = lax.dynamic_index_in_dim(held, side, place, keepdims=False)
        other = swap(send.astype(jnp.bfloat16), step)
        small = small + swap(small, step)
        held = keep + other.astype(jnp.float32)
        left = [s for s in left if s != step]
    side = upper(first)
    send = jnp.where(side, held[:share], held[share:])
    keep = jnp.where(side, held[share:], held[:share])
    other = swap(send.astype(jnp.bfloat16), first)
    small = small + swap(small, first)
    return keep + other.astype(jnp.float32), small


def join(held, step, axis=None):
    other = swap(held, step)
    if axis is None or axis >= 0:
        both = functools.partial(jnp.stack, axis=axis or 0)
    else:
        both = functools.partial(jnp.concatenate, axis=axis)
    return jnp.where(upper(step), both([other, held]), both([held, other]))


def join_quad(held, steps):
    axis, low = steps[0]
    high = steps[1][1]
    near, far, last = (swap(held, (axis, offset)) for offset in (low, high, low + high))
    ahead = upper(steps[1])
    blocks = [
        jnp.where(ahead, second, first)
        for first, second in ((held, far), (near, last), (far, held), (last, near))
    ]
    return jnp.where(
        upper(steps[0]),
        jnp.stack([blocks[1], blocks[0], blocks[3], blocks[2]]),
        jnp.stack(blocks),
    )


def swap_flat(value, offset):
    axes = ("wide", "narrow")
    return lax.ppermute(value, axes, [(i, i ^ offset) for i in range(lax.axis_size(axes))])


def sum_quads(small, low, high):
    near = small + swap_flat(small, low)
    return near + (swap_flat(small, high) + swap_flat(small, low + high))


def sum_chip(send, keep):
    return (keep + swap(send, ("wide", 1)).astype(jnp.float32)).astype(jnp.bfloat16)


def sum_shares(held):
    wide, narrow = lax.axis_size("wide"), lax.axis_size("narrow")
    groups = [
        [w * narrow + n for w in range(core, wide, 2) for n in range(narrow)] for core in range(2)
    ]
    arrived = lax.all_to_all(held, ("wide", "narrow"), 0, 0, axis_index_groups=groups, tiled=True)
    return jnp.sum(arrived.astype(jnp.float32), axis=0)


def lane_masks(dtype):
    lane = lax.broadcasted_iota(jnp.int32, (1, GROUP_LANES), 1) // HEAD_DIM
    return [(lane == h).astype(jnp.float32).astype(dtype) for h in range(GROUP)]


def dot(left, right):
    return jnp.dot(left, right, preferred_element_type=jnp.float32)


def dot_cols(left, right):
    return lax.dot_general(left, right, contract_cols, preferred_element_type=jnp.float32)


def dot_rows(left, right):
    return lax.dot_general(left, right, contract_rows, preferred_element_type=jnp.float32)


def stack_heads(rows, masks):
    return jnp.concatenate([rows * m for m in masks], axis=0)


def pick_heads(blocks, masks):
    n = blocks.shape[0] // GROUP
    return sum(blocks[n * h : n * h + n] * masks[h] for h in range(GROUP))


def head_sums(values):
    row = lax.broadcasted_iota(jnp.int32, (2 * GROUP_LANES, GROUP_LANES), 0) % GROUP_LANES
    col = lax.broadcasted_iota(jnp.int32, (2 * GROUP_LANES, GROUP_LANES), 1)
    ones = (row // HEAD_DIM == col // HEAD_DIM).astype(jnp.float32).astype(jnp.bfloat16)
    high = values.astype(jnp.bfloat16)
    rest = (values - high.astype(jnp.float32)).astype(jnp.bfloat16)
    sums = []
    for start in range(0, values.shape[1], GROUP_LANES):
        cut = slice(start, start + GROUP_LANES)
        sums.append(dot(jnp.concatenate([high[:, cut], rest[:, cut]], axis=1), ones))
    return jnp.concatenate(sums, axis=1)


def send_rows(dest_row, rows, out_ref):
    total = out_ref.shape[0]
    block = math.gcd(total, 256)
    for start in range(0, total, block):
        slot = lax.broadcasted_iota(jnp.int32, (block, rows.shape[0]), 0) + start
        chosen = jnp.where(slot == dest_row, 1.0, 0.0).astype(jnp.bfloat16)
        out_ref[pl.ds(start, block), :] = dot(chosen, rows).astype(jnp.bfloat16)


def gelu_pair(pre):
    inner = math.sqrt(2.0 / math.pi)
    square = pre * pre
    bend = jnp.tanh(pre * (inner + (inner * 0.044715) * square))
    half = 0.5 + 0.5 * bend
    slope = half + pre * (half * (1.0 - bend)) * (inner + (3.0 * inner * 0.044715) * square)
    return pre * half, slope


def take_rows(dest_row, rows):
    count, total = dest_row.shape[1], rows.shape[0]
    places = jnp.broadcast_to(dest_row.astype(jnp.float32), (GROUP_LANES, count)).T
    lane = lax.broadcasted_iota(jnp.int32, (count, GROUP_LANES), 1).astype(jnp.float32)
    chosen = jnp.concatenate(
        [
            jnp.where(places == lane + float(start), 1.0, 0.0).astype(jnp.bfloat16)
            for start in range(0, total, GROUP_LANES)
        ],
        axis=1,
    )
    return dot(chosen, rows)


def assign_kernel(capacity, count_ref, route_ref, cot_ref, dest_ref, out_ref):
    tokens = route_ref.shape[1]
    total = out_ref.shape[0]
    span = GROUP_LANES
    live_end = count_ref[0] * IMG_TOK
    first = lax.broadcasted_iota(jnp.int32, (span, span), 0)
    second = lax.broadcasted_iota(jnp.int32, (span, span), 1)
    earlier = jnp.where(first < second, 1.0, 0.0).astype(jnp.bfloat16)
    whole = jnp.ones((span, span), jnp.bfloat16)
    carry = jnp.zeros((EXPERTS, span), jnp.float32)
    for start in range(0, tokens, span):
        route = route_ref[:, start : start + span]
        place = lax.broadcasted_iota(jnp.int32, (1, span), 1) + start
        expert = lax.broadcasted_iota(jnp.int32, (EXPERTS, span), 0)
        chosen = jnp.where((expert == route) & (place < live_end), 1.0, 0.0)
        low = chosen.astype(jnp.bfloat16)
        before = dot(low, earlier) + carry
        carry = carry + dot(low, whole)
        slot = jnp.sum(before * chosen, axis=0, keepdims=True).astype(jnp.int32)
        keep = (place < live_end) & (slot < capacity)
        dest_ref[:, start : start + span] = jnp.where(keep, route * capacity + slot, total)
    send_rows(dest_ref[...], cot_ref[...], out_ref)


def call_assign(images, routes, cotangent, capacity):
    tokens = routes.shape[0]
    total = EXPERTS * capacity
    return pl.pallas_call(
        functools.partial(assign_kernel, capacity),
        out_shape=(
            jax.ShapeDtypeStruct((1, tokens), jnp.int32),
            jax.ShapeDtypeStruct((total, MODEL_WIDTH), jnp.bfloat16),
        ),
        in_specs=[
            pl.BlockSpec(memory_space=pltpu.SMEM),
            pl.BlockSpec(memory_space=pltpu.VMEM),
            pl.BlockSpec(memory_space=pltpu.VMEM),
        ],
        out_specs=(
            pl.BlockSpec(memory_space=pltpu.VMEM),
            pl.BlockSpec(memory_space=pltpu.VMEM),
        ),
        cost_estimate=pl.CostEstimate(
            flops=2 * total * tokens * MODEL_WIDTH, bytes_accessed=4 * 10**6, transcendentals=0
        ),
        compiler_params=pltpu.CompilerParams(vmem_limit_bytes=VMEM_BYTES),
        name="assign",
    )(images, routes.reshape(1, tokens), cotangent)


def front_kernel(
    dest_ref,
    tokens_ref,
    weight_ref,
    rows_ref,
    scale_ref,
    bias_ref,
    placed_ref,
    section_ref,
    attended_ref,
    mixed_ref,
    raw_ref,
    heads_ref,
    probs_ref,
    low_ref,
):
    step = pl.program_id(0)
    block = tokens_ref.shape[0]
    width = MODEL_WIDTH
    tokens = tokens_ref[...]
    masks_low = lane_masks(jnp.bfloat16)
    masks = lane_masks(jnp.float32)
    projected = dot(tokens, weight_ref[:, : 3 * width])
    queries = projected[:, :width] + rows_ref[4:5, :]
    keys = projected[:, width : 2 * width]
    values = projected[:, 2 * width :] + rows_ref[5:6, :]
    raw_ref[:, :width] = queries
    raw_ref[:, width:] = keys
    heads_ref[:, :width] = (queries * lax.rsqrt(head_sums(queries * queries) + 1e-06)).astype(
        jnp.bfloat16
    )
    heads_ref[:, width : 2 * width] = (
        keys * lax.rsqrt(head_sums(keys * keys) + 1e-06)
    ).astype(jnp.bfloat16)
    heads_ref[:, 2 * width :] = values.astype(jnp.bfloat16)
    units = [
        (window, group)
        for window in range(block // WIN)
        for group in range(width // GROUP_LANES)
    ]

    def part(window, group, side):
        start = side * width + group * GROUP_LANES
        return heads_ref[window * WIN : window * WIN + WIN, start : start + GROUP_LANES]

    cosines = [dot_cols(part(w, g, 1), stack_heads(part(w, g, 0), masks_low)) for w, g in units]
    all_probs = []
    for (window, group), cosine in zip(units, cosines):
        scores = cosine * scale_ref[group] + bias_ref[group]
        powers = jnp.exp(scores - jnp.max(scores, axis=0, keepdims=True))
        probs = powers * (1.0 / jnp.sum(powers, axis=0, keepdims=True))
        probs_ref[window, group] = probs
        all_probs.append(probs.astype(jnp.bfloat16))
    mixes = [pick_heads(dot_rows(p, part(w, g, 2)), masks) for (w, g), p in zip(units, all_probs)]
    for (window, group), mixed in zip(units, mixes):
        mixed_ref[
            window * WIN : window * WIN + WIN,
            group * GROUP_LANES : group * GROUP_LANES + GROUP_LANES,
        ] = mixed.astype(jnp.bfloat16)
    attended = dot(mixed_ref[...], weight_ref[:, 3 * width : 4 * width]) + rows_ref[6:7, :]
    attended_ref[...] = attended
    section = tokens.astype(jnp.float32) + norm_rows(attended, rows_ref[0:1, :], rows_ref[1:2, :])
    section_ref[...] = section
    low_ref[pl.ds(pl.multiple_of(step * block, block), block), :] = section.astype(jnp.bfloat16)

    @pl.when(step == pl.num_programs(0) - 1)
    def _():
        send_rows(dest_ref[...], low_ref[...], placed_ref)


def token_block(tok_rows):
    return math.gcd(tok_rows, 256)


def whole(shape):
    return pl.BlockSpec(shape, lambda i: (0,) * len(shape))


def by_rows(block, width):
    return pl.BlockSpec((block, width), lambda i: (i, 0))


def call_front(dest, tokens, gathered, rows, scale, bias, capacity):
    count, width = tokens.shape
    total = EXPERTS * capacity
    block = token_block(count)
    groups = width // GROUP_LANES
    probs_shape = (count // WIN, groups, WIN, GROUP * WIN)
    return pl.pallas_call(
        front_kernel,
        grid=(count // block,),
        out_shape=(
            jax.ShapeDtypeStruct((total, width), jnp.bfloat16),
            jax.ShapeDtypeStruct((count, width), jnp.float32),
            jax.ShapeDtypeStruct((count, width), jnp.float32),
            jax.ShapeDtypeStruct((count, width), jnp.bfloat16),
            jax.ShapeDtypeStruct((count, 2 * width), jnp.float32),
            jax.ShapeDtypeStruct((count, 3 * width), jnp.bfloat16),
            jax.ShapeDtypeStruct(probs_shape, jnp.float32),
        ),
        in_specs=[
            whole(dest.shape),
            by_rows(block, width),
            whole(gathered.shape),
            whole(rows.shape),
            whole(scale.shape),
            whole(bias.shape),
        ],
        out_specs=(
            whole((total, width)),
            by_rows(block, width),
            by_rows(block, width),
            by_rows(block, width),
            by_rows(block, 2 * width),
            by_rows(block, 3 * width),
            pl.BlockSpec((block // WIN,) + probs_shape[1:], lambda i: (i, 0, 0, 0)),
        ),
        scratch_shapes=[pltpu.VMEM((count, width), jnp.bfloat16)],
        cost_estimate=pl.CostEstimate(
            flops=2 * count * width * width * 8, bytes_accessed=20 * 10**6, transcendentals=0
        ),
        compiler_params=pltpu.CompilerParams(vmem_limit_bytes=VMEM_BYTES),
        name="front",
    )(dest, tokens, gathered, rows, scale, bias)


def back_kernel(
    count_ref,
    dest_ref,
    arrived_ref,
    cot_ref,
    weight_ref,
    rows_ref,
    scale_ref,
    attended_ref,
    raw_ref,
    heads_ref,
    probs_ref,
    expert_ref,
    table_ref,
    coords_ref,
    net_ref,
    total_ref,
    low_attended,
    low_projected,
    sums_ref,
    grad_bias_ref,
    grad_scale_ref,
    grad_heads,
):
    step = pl.program_id(0)
    block = cot_ref.shape[0]
    width = MODEL_WIDTH
    start_row = pl.multiple_of(step * block, block)
    masks_low = lane_masks(jnp.bfloat16)
    masks = lane_masks(jnp.float32)

    @pl.when(step == 0)
    def _():
        sums_ref[...] = jnp.zeros_like(sums_ref)
        grad_bias_ref[...] = jnp.zeros_like(grad_bias_ref)
        grad_scale_ref[...] = jnp.zeros_like(grad_scale_ref)

    place = lax.broadcasted_iota(jnp.int32, (block, 1), 0) + start_row
    live = jnp.where(place < count_ref[0] * IMG_TOK, 1.0, 0.0)
    feed = take_rows(dest_ref[...], arrived_ref[...])
    total = cot_ref[...].astype(jnp.float32) * live + feed
    attended = attended_ref[...]
    centred = attended - jnp.mean(attended, axis=-1, keepdims=True)
    spread = lax.rsqrt(jnp.mean(centred * centred, axis=-1, keepdims=True) + 1e-05)
    unit = centred * spread
    grad_unit = total * rows_ref[0:1, :]
    grad_attended = spread * (
        grad_unit
        - jnp.mean(grad_unit, axis=-1, keepdims=True)
        - unit * jnp.mean(grad_unit * unit, axis=-1, keepdims=True)
    )
    grad_low = grad_attended.astype(jnp.bfloat16)
    total_ref[...] = total
    low_attended[...] = grad_low
    sums_ref[0:1, :width] += jnp.sum(total * unit, axis=0, keepdims=True)
    sums_ref[1:2, :width] += jnp.sum(total, axis=0, keepdims=True)
    sums_ref[6:7, :width] += jnp.sum(grad_low.astype(jnp.float32), axis=0, keepdims=True)
    grad_mixed = dot_cols(grad_low, weight_ref[:, 3 * width : 4 * width]).astype(jnp.bfloat16)
    units = [
        (window, group)
        for window in range(block // WIN)
        for group in range(width // GROUP_LANES)
    ]

    def cut(window, group, side):
        start = side * width + group * GROUP_LANES
        return slice(window * WIN, window * WIN + WIN), slice(start, start + GROUP_LANES)

    queries = [stack_heads(heads_ref[cut(w, g, 0)], masks_low) for w, g in units]
    grad_outs = [stack_heads(grad_mixed[cut(w, g, 0)], masks_low) for w, g in units]
    all_grad_probs = [
        dot_cols(heads_ref[cut(w, g, 2)], grad_out) for (w, g), grad_out in zip(units, grad_outs)
    ]
    cosines = [dot_cols(heads_ref[cut(w, g, 1)], query) for (w, g), query in zip(units, queries)]
    all_probs, grad_cosines = [], []
    for (window, group), grad_probs, cosine in zip(units, all_grad_probs, cosines):
        probs = probs_ref[window, group]
        all_probs.append(probs.astype(jnp.bfloat16))
        weighed = probs * grad_probs
        grad_scores = weighed - probs * jnp.sum(weighed, axis=0, keepdims=True)
        grad_bias_ref[group] += grad_scores
        grad_scale_ref[group] += jnp.sum(grad_scores * cosine, axis=0, keepdims=True)
        grad_cosines.append((grad_scores * scale_ref[group]).astype(jnp.bfloat16))
    for (w, g), probs, grad_out in zip(units, all_probs, grad_outs):
        grad_heads[cut(w, g, 2)] = dot(probs, grad_out)
    for (w, g), grad_cosine, query in zip(units, grad_cosines, queries):
        grad_heads[cut(w, g, 1)] = dot(grad_cosine, query)
    for (w, g), grad_cosine in zip(units, grad_cosines):
        grad_heads[cut(w, g, 0)] = pick_heads(
            dot_rows(grad_cosine, heads_ref[cut(w, g, 1)]), masks
        )
    for side in range(2):
        cut = slice(side * width, side * width + width)
        raw = raw_ref[:, cut]
        inverse = lax.rsqrt(head_sums(raw * raw) + 1e-06)
        unit = raw * inverse
        grad = grad_heads[:, cut]
        low_projected[:, cut] = (inverse * (grad - unit * head_sums(grad * unit))).astype(
            jnp.bfloat16
        )
    low_projected[:, 2 * width :] = grad_heads[:, 2 * width :].astype(jnp.bfloat16)
    grad_projected = low_projected[...]
    sums_ref[4:5, :width] += jnp.sum(
        grad_projected[:, :width].astype(jnp.float32), axis=0, keepdims=True
    )
    sums_ref[5:6, :width] += jnp.sum(
        grad_projected[:, 2 * width :].astype(jnp.float32), axis=0, keepdims=True
    )
    @pl.when(step == pl.num_programs(0) - 1)
    def _():
        sums_ref[2:4, :width] = expert_ref[1:3, :]
        for group in range(grad_scale_ref.shape[0]):
            at = SCALE_ROWS + group
            sums_ref[at : at + 1, : GROUP * WIN] = grad_scale_ref[group]
        net_back(
            sum_offsets(grad_bias_ref), table_ref[...], coords_ref[...], net_ref, sums_ref
        )


def sum_offsets(grad_bias_ref):
    row = lax.broadcasted_iota(jnp.int32, (GROUP * WIN, TABLE), 0)
    lane = lax.broadcasted_iota(jnp.int32, (GROUP * WIN, TABLE), 1)
    query = row % WIN
    aim = TABLE_MID - STRIDE * (query // SIDE) - query % SIDE
    spreads = [
        jnp.where((lane == aim) & (row // WIN == h), 1.0, 0.0).astype(jnp.bfloat16)
        for h in range(GROUP)
    ]
    sums = []
    for group in range(grad_bias_ref.shape[0]):
        grad = grad_bias_ref[group]
        high = grad.astype(jnp.bfloat16)
        rest = grad - high.astype(jnp.float32)
        middle = rest.astype(jnp.bfloat16)
        last = (rest - middle.astype(jnp.float32)).astype(jnp.bfloat16)
        parts = jnp.concatenate([high, middle, last], axis=0)
        for h in range(GROUP):
            spread = dot(parts, spreads[h])
            spread = spread[:WIN] + spread[WIN : 2 * WIN] + spread[2 * WIN :]
            rows = spread[:SIDE]
            for r in range(1, SIDE):
                rows = rows + pltpu.roll(spread[SIDE * r : SIDE * r + SIDE], STRIDE * r, 1)
            rows = pltpu.roll(rows, 0, 1, stride=1, stride_axis=0)
            sums.append(jnp.sum(rows, axis=0, keepdims=True))
    return jnp.concatenate(sums, axis=0)


def net_back(grad, table, coords, net_ref, sums_ref):
    heads = table.shape[0]
    second, shift, first = net_ref[:heads], net_ref[heads : heads + 1], net_ref[heads + 1 : heads + 3]
    pre = coords[:, 0:1] * first[0:1] + coords[:, 1:2] * first[1:2] + shift
    hidden, slope = gelu_pair(pre)
    grad_logits = grad * table * (1.0 - table * (1.0 / 16.0))
    sums_ref[SECOND_ROWS : SECOND_ROWS + heads, :] = jnp.dot(
        grad_logits, hidden, precision=highest, preferred_element_type=jnp.float32
    )
    grad_pre = slope * lax.dot_general(
        grad_logits, second, contract_rows, precision=highest, preferred_element_type=jnp.float32
    )
    sums_ref[SHIFT_ROW : SHIFT_ROW + 1, :] = jnp.sum(grad_pre, axis=0, keepdims=True)
    for k in range(2):
        sums_ref[FIRST_ROWS + k : FIRST_ROWS + k + 1, :] = jnp.sum(
            grad_pre * coords[:, k : k + 1], axis=0, keepdims=True
        )


def call_back(
    images, dest, arrived, cotangent, gathered, rows, scale, attended, raw, heads, probs,
    sums_expert, table, net,
):
    count, width = cotangent.shape
    block = token_block(count)
    groups = width // GROUP_LANES
    coords = jnp.asarray(offset_coords())
    return pl.pallas_call(
        back_kernel,
        grid=(count // block,),
        out_shape=(
            jax.ShapeDtypeStruct((count, width), jnp.float32),
            jax.ShapeDtypeStruct((count, width), jnp.bfloat16),
            jax.ShapeDtypeStruct((count, 3 * width), jnp.bfloat16),
            jax.ShapeDtypeStruct((SUM_ROWS, SUM_LANES), jnp.float32),
        ),
        in_specs=[
            pl.BlockSpec(memory_space=pltpu.SMEM),
            pl.BlockSpec((1, block), lambda i: (0, i)),
            whole(arrived.shape),
            by_rows(block, width),
            whole(gathered.shape),
            whole(rows.shape),
            whole(scale.shape),
            by_rows(block, width),
            by_rows(block, 2 * width),
            by_rows(block, 3 * width),
            pl.BlockSpec((block // WIN,) + probs.shape[1:], lambda i: (i, 0, 0, 0)),
            whole(sums_expert.shape),
            whole(table.shape),
            whole(coords.shape),
            whole(net.shape),
        ],
        out_specs=(
            by_rows(block, width),
            by_rows(block, width),
            by_rows(block, 3 * width),
            whole((SUM_ROWS, SUM_LANES)),
        ),
        scratch_shapes=[
            pltpu.VMEM((groups, WIN, GROUP * WIN), jnp.float32),
            pltpu.VMEM((groups, 1, GROUP * WIN), jnp.float32),
            pltpu.VMEM((block, 3 * width), jnp.float32),
        ],
        cost_estimate=pl.CostEstimate(
            flops=2 * count * width * width * 10, bytes_accessed=20 * 10**6, transcendentals=0
        ),
        compiler_params=pltpu.CompilerParams(vmem_limit_bytes=VMEM_MOST),
        name="back",
    )(
        images, dest, arrived, cotangent, gathered, rows, scale, attended, raw, heads, probs,
        sums_expert, table, coords, net,
    )


def dense_kernel(
    narrow,
    place_ref,
    tokens_ref,
    mixed_ref,
    attended_ref,
    projected_ref,
    expert_ref,
    send_ref,
    keep_ref,
):
    width = tokens_ref.shape[1]
    grad_dense = jnp.concatenate(
        [
            dot_rows(tokens_ref[...], projected_ref[...]),
            dot_rows(mixed_ref[...], attended_ref[...]),
        ],
        axis=1,
    )
    chips = keep_ref.shape[0]
    on_first = place_ref[0] == 0
    row = lax.broadcasted_iota(jnp.int32, (GROUP_LANES, width), 0)
    grad_route = jnp.where(row == place_ref[1], expert_ref[3:4, :], 0.0).T
    share = width // (2 * chips)
    for chip in range(chips):
        cuts = []
        for core in range(2):
            row = (chip // narrow * 2 * narrow + core * narrow + chip % narrow) * share
            rows, route = grad_dense[row : row + share], grad_route[row : row + share]
            halves = jnp.concatenate([rows[:, : 2 * width], rows[:, 2 * width :]], axis=0)
            route = jnp.concatenate([route, jnp.zeros_like(route)], axis=0)
            cuts.append(jnp.concatenate([halves, route], axis=1))
        keep_ref[chip] = jnp.where(on_first, cuts[0], cuts[1])
        send_ref[chip] = jnp.where(on_first, cuts[1], cuts[0]).astype(jnp.bfloat16)


def call_dense(tokens, mixed, attended, projected, sums_expert):
    count, width = tokens.shape
    narrow = lax.axis_size("narrow")
    chips = narrow * lax.axis_size("wide") // 2
    shape = (chips, width // chips, 2 * width + GROUP_LANES)
    place = jnp.stack([lax.axis_index("wide") % 2, lax.axis_index(("wide", "narrow"))])
    return pl.pallas_call(
        functools.partial(dense_kernel, narrow),
        out_shape=(
            jax.ShapeDtypeStruct(shape, jnp.bfloat16),
            jax.ShapeDtypeStruct(shape, jnp.float32),
        ),
        in_specs=[pl.BlockSpec(memory_space=pltpu.SMEM)]
        + [pl.BlockSpec(memory_space=pltpu.VMEM)] * 5,
        out_specs=(pl.BlockSpec(memory_space=pltpu.VMEM),) * 2,
        cost_estimate=pl.CostEstimate(
            flops=8 * count * width * width, bytes_accessed=7 * 10**6, transcendentals=0
        ),
        compiler_params=pltpu.CompilerParams(vmem_limit_bytes=VMEM_BYTES),
        name="dense",
    )(place.astype(jnp.int32), tokens, mixed, attended, projected, sums_expert)


def inputs_kernel(total_ref, projected_ref, weight_ref, out_ref):
    wide = projected_ref.shape[1]
    out_ref[...] = (
        total_ref[...] + dot_cols(projected_ref[...], weight_ref[:, :wide])
    ).astype(jnp.bfloat16)


def call_inputs(total, projected, gathered):
    count, width = total.shape
    block = token_block(count)
    return pl.pallas_call(
        inputs_kernel,
        grid=(count // block,),
        out_shape=jax.ShapeDtypeStruct((count, width), jnp.bfloat16),
        in_specs=[
            by_rows(block, width),
            by_rows(block, 3 * width),
            whole(gathered.shape),
        ],
        out_specs=by_rows(block, width),
        cost_estimate=pl.CostEstimate(
            flops=0, bytes_accessed=0, transcendentals=0
        ),
        compiler_params=pltpu.CompilerParams(vmem_limit_bytes=VMEM_BYTES),
        name="inputs",
    )(total, projected, gathered)


def layer_kernel(count_ref, dest_ref, branch_ref, section_ref, out_ref):
    block = out_ref.shape[0]
    place = lax.broadcasted_iota(jnp.int32, (block, 1), 0) + pl.program_id(0) * block
    live = jnp.where(place < count_ref[0] * IMG_TOK, 1.0, 0.0)
    branch = take_rows(dest_ref[...], branch_ref[...])
    out_ref[...] = ((section_ref[...] + branch) * live).astype(jnp.bfloat16)


def call_layer(images, dest, branch, section):
    count, width = section.shape
    block = token_block(count)
    return pl.pallas_call(
        layer_kernel,
        grid=(count // block,),
        out_shape=jax.ShapeDtypeStruct((count, width), jnp.bfloat16),
        in_specs=[
            pl.BlockSpec(memory_space=pltpu.SMEM),
            pl.BlockSpec((1, block), lambda i: (0, i)),
            whole(branch.shape),
            by_rows(block, width),
        ],
        out_specs=by_rows(block, width),
        cost_estimate=pl.CostEstimate(
            flops=0, bytes_accessed=0, transcendentals=0
        ),
        compiler_params=pltpu.CompilerParams(vmem_limit_bytes=VMEM_BYTES),
        name="layer",
    )(images, dest, branch, section)


def expert_kernel(
    rows_ref,
    cot_ref,
    first_ref,
    second_ref,
    bias_one_ref,
    vecs_ref,
    branch_ref,
    back_ref,
    hidden_ref,
    grad_pre_ref,
    grad_result_ref,
    sums_ref,
    sum_pre_ref,
):
    @pl.when(pl.program_id(0) == 0)
    def _():
        sums_ref[...] = jnp.zeros_like(sums_ref)
        sum_pre_ref[...] = jnp.zeros_like(sum_pre_ref)

    bias_two, gain, shift, route = (vecs_ref[i : i + 1, :] for i in range(4))
    count = rows_ref.shape[0]
    size = count // EXPERT_PARTS
    cuts = [slice(start, start + size) for start in range(0, count, size)]
    pres = [dot(rows_ref[cut, :], first_ref[...]) + bias_one_ref[...] for cut in cuts]
    pairs = [gelu_pair(pre) for pre in pres]
    hiddens = [hidden.astype(jnp.bfloat16) for hidden, _ in pairs]
    raws = [dot(hidden, second_ref[...]) + bias_two for hidden in hiddens]
    grads = []
    for cut, hidden, raw in zip(cuts, hiddens, raws):
        hidden_ref[cut, :] = hidden
        rows = rows_ref[cut, :].astype(jnp.float32)
        result = raw.astype(jnp.bfloat16).astype(jnp.float32)
        gating = jax.nn.sigmoid(jnp.sum(rows * route, axis=-1, keepdims=True))
        centred = result - jnp.mean(result, axis=-1, keepdims=True)
        spread = lax.rsqrt(jnp.mean(centred * centred, axis=-1, keepdims=True) + 1e-05)
        unit = centred * spread
        normed = unit * gain + shift
        branch_ref[cut, :] = (normed * gating).astype(jnp.bfloat16)
        cot = cot_ref[cut, :].astype(jnp.float32)
        grad_gate = jnp.sum(cot * normed, axis=-1, keepdims=True)
        gated = cot * gating
        grad_unit = gated * gain
        grad_result = (
            spread
            * (
                grad_unit
                - jnp.mean(grad_unit, axis=-1, keepdims=True)
                - unit * jnp.mean(grad_unit * unit, axis=-1, keepdims=True)
            )
        ).astype(jnp.bfloat16)
        grad_result_ref[cut, :] = grad_result
        grad_logit = (
            (grad_gate * gating * (1.0 - gating)).astype(jnp.bfloat16).astype(jnp.float32)
        )
        sums_ref[0:1, :] += jnp.sum(grad_result.astype(jnp.float32), axis=0, keepdims=True)
        sums_ref[1:2, :] += jnp.sum(gated * unit, axis=0, keepdims=True)
        sums_ref[2:3, :] += jnp.sum(gated, axis=0, keepdims=True)
        sums_ref[3:4, :] += jnp.sum(rows * grad_logit, axis=0, keepdims=True)
        grads.append((grad_result, grad_logit))
    grad_hiddens = [dot_cols(grad, second_ref[...]) for grad, _ in grads]
    grad_pres = [
        (grad * slope).astype(jnp.bfloat16) for grad, (_, slope) in zip(grad_hiddens, pairs)
    ]
    for cut, grad_pre, (_, grad_logit) in zip(cuts, grad_pres, grads):
        grad_pre_ref[cut, :] = grad_pre
        sum_pre_ref[...] += jnp.sum(grad_pre.astype(jnp.float32), axis=0, keepdims=True)
        back_ref[cut, :] = (dot_cols(grad_pre, first_ref[...]) + grad_logit * route).astype(
            jnp.bfloat16
        )


def call_expert(rows, cot, first, second, bias_one, vecs):
    count, width = rows.shape
    ff = first.shape[1]
    block = math.gcd(count, 640)
    return pl.pallas_call(
        expert_kernel,
        grid=(count // block,),
        out_shape=(
            pltpu.HBM((count, width), jnp.bfloat16),
            pltpu.HBM((count, width), jnp.bfloat16),
            pltpu.HBM((count, ff), jnp.bfloat16),
            pltpu.HBM((count, ff), jnp.bfloat16),
            pltpu.HBM((count, width), jnp.bfloat16),
            jax.ShapeDtypeStruct((8, width), jnp.float32),
            jax.ShapeDtypeStruct((1, ff), jnp.float32),
        ),
        in_specs=[
            by_rows(block, width),
            by_rows(block, width),
            whole(first.shape),
            whole(second.shape),
            whole(bias_one.shape),
            whole(vecs.shape),
        ],
        out_specs=(
            by_rows(block, width),
            by_rows(block, width),
            by_rows(block, ff),
            by_rows(block, ff),
            by_rows(block, width),
            whole((8, width)),
            whole((1, ff)),
        ),
        cost_estimate=pl.CostEstimate(
            flops=8 * count * width * ff, bytes_accessed=16 * 10**6, transcendentals=count * ff
        ),
        compiler_params=pltpu.CompilerParams(vmem_limit_bytes=VMEM_BYTES),
        name="expert",
    )(
        pltpu.with_memory_space_constraint(rows, pltpu.HBM),
        pltpu.with_memory_space_constraint(cot, pltpu.HBM),
        first,
        pltpu.with_memory_space_constraint(second, pltpu.HBM),
        bias_one,
        vecs,
    )


def offset_coords():
    place = TABLE_MID - np.arange(TABLE)
    row = (place + STRIDE // 2 - 1) // STRIDE
    coords = np.stack([row, place - STRIDE * row], axis=1) * (8.0 / (SIDE - 1))
    return (np.sign(coords) * np.log2(np.abs(coords) + 1.0) / 3.0).astype(np.float32)


def bias_table(params):
    piece_collection = pieces(params)
    hidden = jax.nn.gelu(
        jnp.dot(offset_coords(), piece_collection[9], precision=highest) + piece_collection[8]
    )
    return 16.0 * jax.nn.sigmoid(jnp.dot(hidden, piece_collection[10], precision=highest)).T


def spread_bias(table):
    places = jnp.arange(WIN, dtype=jnp.int32)
    coded = STRIDE * (places // SIDE) + places % SIDE
    index = TABLE_MID + coded[:, None] - coded[None, :]
    lookup = (index.reshape(1, -1) == jnp.arange(TABLE, dtype=jnp.int32)[:, None]).astype(
        table.dtype
    )
    bias = jnp.dot(table, lookup, precision=highest).reshape(-1, GROUP, WIN, WIN)
    return bias.transpose(0, 2, 1, 3).reshape(-1, WIN, GROUP * WIN)


def per_device_split(
    tokens,
    cotangent,
    routes,
    images,
    dense_weight,
    dense_moment,
    dense_square,
    small_params,
    small_moment,
    small_square,
    inner_weight,
    inner_moment,
    inner_square,
    outer_weight,
    outer_moment,
    outer_square,
    expert_bias,
    bias_moment,
    bias_square,
):
    slices = lax.axis_size(("wide", "narrow"))
    split = slices // EXPERTS
    member = lax.axis_index(("wide", "narrow")) % split
    piece = MODEL_WIDTH // split
    ff_dev = inner_weight.shape[2]
    tok_rows = tokens.shape[0]
    capacity = (5 * tok_rows + 4 * EXPERTS - 1) // (4 * EXPERTS)
    slot_total = EXPERTS * capacity
    route_ids = routes[:, 0]
    live_rows, kept_rows, dest_slot = assign(route_ids, images[0], EXPERTS, capacity)
    live_f = live_rows.astype(jnp.float32)
    keep_f = kept_rows.astype(jnp.float32)
    clipped = jnp.minimum(dest_slot, slot_total - 1)
    gathered = gather_rows(dense_weight.astype(jnp.bfloat16))
    section_one, gating, expert_feed, kept = front_forward_split(
        tokens, gathered, small_params, route_ids
    )

    def fan_out(rows_value):
        placed_rows = (
            jnp.zeros((slot_total, MODEL_WIDTH), jnp.bfloat16)
            .at[dest_slot]
            .set(rows_value.astype(jnp.bfloat16), mode="drop")
        )
        copies = jnp.broadcast_to(
            placed_rows.reshape(EXPERTS, 1, capacity, MODEL_WIDTH),
            (EXPERTS, split, capacity, MODEL_WIDTH),
        )
        return trade_rows(copies.reshape(slices, capacity, MODEL_WIDTH)).reshape(
            slices * capacity, MODEL_WIDTH
        )

    def fan_in(partials):
        arrived = trade_rows(partials.reshape(slices, capacity, MODEL_WIDTH))
        summed = jnp.sum(
            arrived.reshape(EXPERTS, split, capacity, MODEL_WIDTH).astype(jnp.float32), axis=1
        ).reshape(slot_total, MODEL_WIDTH)
        return jnp.take(summed, clipped, axis=0) * keep_f[:, None]

    expert_rows = fan_out(expert_feed)
    first_matrix = inner_weight[0].astype(jnp.bfloat16)
    second_matrix = outer_weight[0].astype(jnp.bfloat16)
    pre_act = (
        jnp.dot(expert_rows, first_matrix, preferred_element_type=jnp.float32)
        + expert_bias[0, :ff_dev]
    )
    hidden = jax.nn.gelu(pre_act).astype(jnp.bfloat16)
    out_bias = lax.dynamic_update_slice(
        jnp.zeros((MODEL_WIDTH,), jnp.float32), expert_bias[0, ff_dev:], (member * piece,)
    )
    result = (jnp.dot(hidden, second_matrix, preferred_element_type=jnp.float32) + out_bias).astype(
        jnp.bfloat16
    )
    combined = fan_in(result)

    def tail_local(section_value, gate_value, combined_value, params):
        return finish_block(section_value, gate_value, combined_value, keep_f, live_f, params)

    layer_value, tail_back = jax.vjp(tail_local, section_one, gating, combined, small_params)
    grad_section, grad_gate, grad_combined, grad_small_tail = tail_back(
        cotangent.astype(jnp.float32)
    )
    grad_result = fan_out(grad_combined)
    grad_outer = lax.dot_general(
        hidden, grad_result, contract_rows, preferred_element_type=jnp.float32
    )
    grad_hidden = lax.dot_general(
        grad_result, second_matrix, contract_cols, preferred_element_type=jnp.float32
    )
    gelu_back = jax.vjp(jax.nn.gelu, pre_act)[1]
    grad_pre = gelu_back(grad_hidden)[0].astype(jnp.bfloat16)
    grad_inner = lax.dot_general(
        expert_rows, grad_pre, contract_rows, preferred_element_type=jnp.float32
    )
    column_total = jnp.sum(grad_result.astype(jnp.float32), axis=0)
    grad_bias = jnp.concatenate(
        [
            jnp.sum(grad_pre.astype(jnp.float32), axis=0),
            lax.dynamic_slice_in_dim(column_total, member * piece, piece, 0),
        ]
    )
    grad_rows = lax.dot_general(
        grad_pre, first_matrix, contract_cols, preferred_element_type=jnp.float32
    ).astype(jnp.bfloat16)
    grad_feed = fan_in(grad_rows)
    grad_inputs, grad_weights, grad_small_front = front_backward_split(
        tokens, gathered, small_params, kept, grad_section, grad_gate, grad_feed
    )
    grad_small = grad_small_front + grad_small_tail
    grad_dense, grad_small = sum_grads(grad_weights, grad_small)
    dense_out = adamw_step(
        dense_weight, grad_dense, dense_moment, dense_square, dense_rate, weight_decay
    )
    small_out = adamw_step(small_params, grad_small, small_moment, small_square, small_rate, 0.0)
    inner_out = adamw_step(
        inner_weight, grad_inner[None], inner_moment, inner_square, expert_rate, weight_decay
    )
    outer_out = adamw_step(
        outer_weight, grad_outer[None], outer_moment, outer_square, expert_rate, weight_decay
    )
    bias_out = adamw_step(expert_bias, grad_bias[None], bias_moment, bias_square, expert_rate, 0.0)
    return (
        layer_value.astype(jnp.bfloat16),
        grad_inputs.astype(jnp.bfloat16),
        dense_out[0],
        dense_out[1],
        dense_out[2],
        small_out[0],
        small_out[1],
        small_out[2],
        inner_out[0],
        inner_out[1],
        inner_out[2],
        inner_out[0].astype(jnp.bfloat16),
        outer_out[0],
        outer_out[1],
        outer_out[2],
        outer_out[0].astype(jnp.bfloat16),
        bias_out[0],
        bias_out[1],
        bias_out[2],
    )


def per_device(
    tokens,
    cotangent,
    routes,
    images,
    dense_weight,
    dense_moment,
    dense_square,
    small_params,
    small_moment,
    small_square,
    inner_weight,
    inner_moment,
    inner_square,
    outer_weight,
    outer_moment,
    outer_square,
    expert_bias,
    bias_moment,
    bias_square,
):
    slices = lax.axis_size(("wide", "narrow"))
    if slices != EXPERTS:
        return per_device_split(
            tokens,
            cotangent,
            routes,
            images,
            dense_weight,
            dense_moment,
            dense_square,
            small_params,
            small_moment,
            small_square,
            inner_weight,
            inner_moment,
            inner_square,
            outer_weight,
            outer_moment,
            outer_square,
            expert_bias,
            bias_moment,
            bias_square,
        )
    expert = lax.axis_index(("wide", "narrow"))
    ff_dev = inner_weight.shape[2]
    tok_rows = tokens.shape[0]
    capacity = (5 * tok_rows + 4 * EXPERTS - 1) // (4 * EXPERTS)
    slot_total = EXPERTS * capacity

    def trade(rows):
        traded = trade_rows(rows.reshape(slices, capacity, MODEL_WIDTH))
        return traded.reshape(slot_total, MODEL_WIDTH)

    scale_at = 7 * MODEL_WIDTH
    share = dense_weight.astype(jnp.bfloat16)
    across, *deep = axis_bits("narrow")
    held = join_quad(share, deep)
    held = join(held, across, -2)
    held, route_ids, cot = lax.optimization_barrier((held, routes, cotangent))
    dest, placed_cot = call_assign(images, route_ids, cot, capacity)
    cot_rows = trade(placed_cot)
    core, *rest = axis_bits("wide")
    for step in rest:
        held = join(held, step)
    held, params = lax.optimization_barrier((held, small_params))
    gathered = join(held, core, len(rest)).reshape(-1, share.shape[-1])
    table = bias_table(params)
    net_pieces = pieces(params)
    net = jnp.concatenate([net_pieces[10].T, net_pieces[8][None, :], net_pieces[9]])
    vectors = params[:scale_at].reshape(7, MODEL_WIDTH)
    scale_heads = jnp.exp(params[scale_at : scale_at + ATTENTION_HEADS])
    scale = jnp.repeat(scale_heads, WIN).reshape(-1, 1, GROUP * WIN)
    bias = spread_bias(table)
    placed, section, attended, mixed, raw, heads, probs = call_front(
        dest, tokens, gathered, vectors, scale, bias, capacity
    )
    placed, cot_rows = lax.optimization_barrier((placed, cot_rows))
    expert_rows = trade(placed)
    first_matrix = inner_weight[0].astype(jnp.bfloat16)
    second_matrix = outer_weight[0].astype(jnp.bfloat16)
    route_row = lax.dynamic_slice_in_dim(gathered, 4 * MODEL_WIDTH + expert, 1, 1)
    vecs = jnp.concatenate(
        [expert_bias[:, ff_dev:], vectors[2:4], route_row.astype(jnp.float32).reshape(1, -1)]
    )
    branch, grad_rows, hidden, grad_pre, grad_result, sums_expert, sum_pre = call_expert(
        expert_rows, cot_rows, first_matrix, second_matrix, expert_bias[:, :ff_dev], vecs
    )
    arrived = trade(grad_rows)
    grad_outer = dot_rows(hidden, grad_result)
    grad_inner = dot_rows(expert_rows, grad_pre)
    grad_bias = jnp.concatenate([sum_pre, sums_expert[0:1]], axis=1)[0]
    inner_out = adamw_step(
        inner_weight, grad_inner[None], inner_moment, inner_square, expert_rate, weight_decay
    )
    outer_out = adamw_step(
        outer_weight, grad_outer[None], outer_moment, outer_square, expert_rate, weight_decay
    )
    inner_out += (inner_out[0].astype(jnp.bfloat16),)
    outer_out += (outer_out[0].astype(jnp.bfloat16),)
    branch, arrived, inner_out, outer_out = lax.optimization_barrier(
        (branch, arrived, inner_out, outer_out)
    )
    branch_rows = trade(branch)
    total, low_attended, low_projected, sums = call_back(
        images,
        dest,
        arrived,
        cotangent,
        gathered,
        vectors,
        scale,
        attended,
        raw,
        heads,
        probs,
        sums_expert,
        table,
        net,
    )
    send, keep = call_dense(tokens, mixed, low_attended, low_projected, sums_expert)
    grad_inputs = call_inputs(total, low_projected, gathered)
    held = sum_chip(send, keep)
    narrow = lax.axis_size("narrow")
    sums = sums + swap_flat(sums, narrow)
    held, sums, branch_rows = lax.optimization_barrier((held, sums, branch_rows))
    grad_dense = sum_shares(held)
    sums = sum_quads(sum_quads(sums, 2, 4), 1, 2 * narrow)
    layer_out = call_layer(images, dest, branch_rows, section)
    share_rows = dense_weight.shape[0]
    half = 2 * MODEL_WIDTH
    grad_dense = jnp.concatenate(
        [
            grad_dense[:share_rows, :half],
            grad_dense[share_rows:, :half],
            grad_dense[:share_rows, half : half + EXPERTS],
        ],
        axis=1,
    )
    grad_scale = sums[SCALE_ROWS : SCALE_ROWS + ATTENTION_HEADS // GROUP, : GROUP * WIN]
    grad_small = jnp.concatenate(
        [
            sums[:7, :MODEL_WIDTH].reshape(-1),
            jnp.sum(grad_scale.reshape(ATTENTION_HEADS, WIN), axis=1) * scale_heads,
            sums[SHIFT_ROW : FIRST_ROWS + 2].reshape(-1),
            sums[SECOND_ROWS : SECOND_ROWS + ATTENTION_HEADS].T.reshape(-1),
        ]
    )
    dense_out = adamw_step(
        dense_weight, grad_dense, dense_moment, dense_square, dense_rate, weight_decay
    )
    small_out = adamw_step(small_params, grad_small, small_moment, small_square, small_rate, 0.0)
    bias_out = adamw_step(expert_bias, grad_bias[None], bias_moment, bias_square, expert_rate, 0.0)
    return (
        layer_out,
        grad_inputs,
        dense_out[0],
        dense_out[1],
        dense_out[2],
        small_out[0],
        small_out[1],
        small_out[2],
        inner_out[0],
        inner_out[1],
        inner_out[2],
        inner_out[3],
        outer_out[0],
        outer_out[1],
        outer_out[2],
        outer_out[3],
        bias_out[0],
        bias_out[1],
        bias_out[2],
    )


def solution(mesh):
    return jax.shard_map(
        per_device,
        mesh=mesh,
        in_specs=(
            P(("wide", "narrow"), None),
            P(("wide", "narrow"), None),
            P(("wide", "narrow"), None),
            P(("wide", "narrow")),
            P(("wide", "narrow"), None),
            P(("wide", "narrow"), None),
            P(("wide", "narrow"), None),
            P(),
            P(),
            P(),
            P(("wide", "narrow"), None, None),
            P(("wide", "narrow"), None, None),
            P(("wide", "narrow"), None, None),
            P(("wide", "narrow"), None, None),
            P(("wide", "narrow"), None, None),
            P(("wide", "narrow"), None, None),
            P(("wide", "narrow"), None),
            P(("wide", "narrow"), None),
            P(("wide", "narrow"), None),
        ),
        out_specs=(
            P(("wide", "narrow"), None),
            P(("wide", "narrow"), None),
            P(("wide", "narrow"), None),
            P(("wide", "narrow"), None),
            P(("wide", "narrow"), None),
            P(),
            P(),
            P(),
            P(("wide", "narrow"), None, None),
            P(("wide", "narrow"), None, None),
            P(("wide", "narrow"), None, None),
            P(("wide", "narrow"), None, None),
            P(("wide", "narrow"), None, None),
            P(("wide", "narrow"), None, None),
            P(("wide", "narrow"), None, None),
            P(("wide", "narrow"), None, None),
            P(("wide", "narrow"), None),
            P(("wide", "narrow"), None),
            P(("wide", "narrow"), None),
        ),
        check_vma=False,
    )
```
